32 devices in a mesh: dp: 8 (over z, x), mp: 4 (over y, core).
Axes of the slice: x: 2, y: 2, z: 4, core: 2. Of those that a mesh axis runs over, the one named last changes fastest.
Arguments:
- patches: bfloat16 [128, 196, 768], P(('dp', 'mp')), may hold values from -6 to 6
- keep_mask: int32 [128, 196], P(('dp', 'mp')), may hold values from 0 to 1, as said below
- labels: int32 [128], P(('dp', 'mp')), may hold values from 0 to 999
- stem_weight: float32 [768, 768], replicated, may hold values from -0.21875 to 0.21875
- position_table: float32 [197, 768], replicated, may hold values from -3 to 3
- attend_in: float32 [768, 3, 768], P('dp', None, 'mp'), may hold values from -0.21875 to 0.21875
- attend_out: float32 [768, 768], P('mp', 'dp'), may hold values from -0.875 to 0.875
- expand: float32 [768, 3072], P('dp', 'mp'), may hold values from -0.21875 to 0.21875
- contract: float32 [3072, 768], P('mp', 'dp'), may hold values from -0.109375 to 0.109375
- head_weight: float32 [768, 1000], replicated, may hold values from -0.21875 to 0.21875
- vectors: float32 [12520], replicated, as said below
- stem_rows: float32 [768], replicated, may hold values from 6.009615e-07 to 2.403846e-06
- stem_cols: float32 [768], replicated, may hold values from 6.009615e-07 to 2.403846e-06
- table_rows: float32 [197], replicated, may hold values from 4.6227813e-09 to 1.8491125e-08
- table_cols: float32 [768], replicated, may hold values from 4.6227813e-09 to 1.8491125e-08
- attend_in_rows: float32 [768], replicated, may hold values from 1.2019231e-07 to 3.0048077e-06
- attend_in_cols: float32 [3, 768], replicated, may hold values from 1.5024038e-07 to 6.009615e-07
- attend_out_rows: float32 [768], replicated, may hold values from 1.5024038e-07 to 6.009615e-07
- attend_out_cols: float32 [768], replicated, may hold values from 1.2019231e-07 to 3.0048077e-06
- expand_rows: float32 [768], replicated, may hold values from 1.2019231e-07 to 3.0048077e-06
- expand_cols: float32 [3072], replicated, may hold values from 1.5024038e-07 to 6.009615e-07
- contract_rows: float32 [3072], replicated, may hold values from 1.5024038e-07 to 6.009615e-07
- contract_cols: float32 [768], replicated, may hold values from 1.2019231e-07 to 3.0048077e-06
- head_rows: float32 [768], replicated, may hold values from 7.8125e-06 to 3.125e-05
- head_cols: float32 [1000], replicated, may hold values from 7.8125e-06 to 3.125e-05
- vector_second: float32 [12520], replicated, may hold values from 6.009615e-07 to 2.403846e-06
Outputs:
- loss_sum: float32 [], replicated
- stem_new: float32 [768, 768], replicated
- stem_rows_new: float32 [768], replicated
- stem_cols_new: float32 [768], replicated
- table_new: float32 [197, 768], replicated
- table_rows_new: float32 [197], replicated
- table_cols_new: float32 [768], replicated
- attend_in_new: float32 [768, 3, 768], P('dp', None, 'mp')
- attend_in_copy: bfloat16 [768, 3, 768], P('dp', None, 'mp')
- attend_in_rows_new: float32 [768], replicated
- attend_in_cols_new: float32 [3, 768], replicated
- attend_out_new: float32 [768, 768], P('mp', 'dp')
- attend_out_copy: bfloat16 [768, 768], P('mp', 'dp')
- attend_out_rows_new: float32 [768], replicated
- attend_out_cols_new: float32 [768], replicated
- expand_new: float32 [768, 3072], P('dp', 'mp')
- expand_copy: bfloat16 [768, 3072], P('dp', 'mp')
- expand_rows_new: float32 [768], replicated
- expand_cols_new: float32 [3072], replicated
- contract_new: float32 [3072, 768], P('mp', 'dp')
- contract_copy: bfloat16 [3072, 768], P('mp', 'dp')
- contract_rows_new: float32 [3072], replicated
- contract_cols_new: float32 [768], replicated
- head_new: float32 [768, 1000], replicated
- head_rows_new: float32 [768], replicated
- head_cols_new: float32 [1000], replicated
- vectors_new: float32 [12520], replicated
- vector_grad: float32 [12520], replicated
- vector_second_new: float32 [12520], replicated
The draws below stay inside these ranges and needn't reach their ends.
Inputs may be any that keep to these rules, and one draw needn't show every extreme that they name: `keep_mask`: each image keeps 64 to 196 of its patches; some image keeps exactly 64 and some keeps all. `vectors`: gains one, two and last lie near 1, all other entries near 0.
All inputs are finite; a program needn't handle non-finite values.
Results may differ from the reference program's by a relative error of at most 0.011.
Values may be sent and summed in bfloat16 or wider, within the bound.
No kernel may reach another device: no remote copies, remote signals or barrier semaphores. Data moves between devices by JAX's collectives and lax.ppermute only.
A program may use at most 256 MiB of HBM per device.

```python
import math
import jax
import jax.numpy as jnp
from jax import lax

D = 768
HEADS = 12
HEAD_DIM = 64
FF = 3072
CLASSES = 1000
PATCHES = 196
PATCH_DIM = 768
KEEP_LEAST = 64
SLOTS = 197
IMAGES = 128
VECTOR_LEN = 12520


def draw_keep_mask(key, part):
    key = jax.random.fold_in(key, 7)
    count_key, order_key, chosen_key = jax.random.split(key, 3)
    counts = jax.random.randint(count_key, (IMAGES,), KEEP_LEAST, PATCHES + 1)
    chosen = jax.random.permutation(chosen_key, IMAGES)
    counts = counts.at[chosen[0]].set(PATCHES).at[chosen[1]].set(KEEP_LEAST)
    orders = jax.vmap(lambda subkey: jax.random.permutation(subkey, PATCHES))(jax.random.split(order_key, IMAGES))
    return (orders < counts[:, None]).astype(jnp.int32)


def draw_vectors(key, part):
    key = jax.random.fold_in(key, 11)
    noise = jax.random.normal(key, (VECTOR_LEN,), jnp.float32) * 0.2
    index = jnp.arange(VECTOR_LEN)
    first = (index >= D) & (index < 2 * D)
    second = (index >= 6 * D) & (index < 7 * D)
    last = (index >= 9 * D + FF) & (index < 10 * D + FF)
    return noise + jnp.where(first | second | last, 1.0, 0.0).astype(jnp.float32)


def rising_state(key, length, spread):
    base = 0.0025 / ((KEEP_LEAST + PATCHES) // 2 * IMAGES)
    place_frac = jnp.arange(length, dtype=jnp.float32) / max(length - 1, 1)
    jitter = jnp.exp(jax.random.uniform(key, (length,), jnp.float32, -0.22, 0.22))
    return base * jnp.exp(place_frac * jnp.log(spread)) * jitter


def draw_attend_in_rows(key, part):
    key = jax.random.fold_in(key, 21)
    return rising_state(key, D, 4.0)


def draw_attend_out_cols(key, part):
    key = jax.random.fold_in(key, 22)
    return rising_state(key, D, 4.0)


def draw_expand_rows(key, part):
    key = jax.random.fold_in(key, 23)
    return rising_state(key, D, 4.0)


def draw_contract_cols(key, part):
    key = jax.random.fold_in(key, 24)
    return rising_state(key, D, 4.0)


def plant(array, rng, low, high):
    longest = array.shape.index(max(array.shape))
    spots = []
    for shift in (0, 1):
        where = [jax.random.randint(jax.random.fold_in(rng, axis), (), 0, length) for axis, length in enumerate(array.shape)]
        where[longest] = (where[longest] + shift) % array.shape[longest]
        spots.append(tuple(where))
    return array.at[spots[0]].set(low).at[spots[1]].set(high)


def block_scale(own_key, shape, shards, least, top_value):
    level, own = 1.0, jax.random.fold_in(own_key, 6)
    for position, parts in shards:
        heights = jnp.exp(jax.random.uniform(jax.random.fold_in(own, position), (parts,), jnp.float32, least / len(shards), top_value / len(shards)))
        level = level * jnp.repeat(heights, shape[position] // parts).reshape([-1 if axis == position else 1 for axis in range(len(shape))])
    return level


def scatter_about(key, dims, scale, bound, cuts=(), kind=jnp.bfloat16):
    values = scale * jax.random.normal(key, dims, jnp.float32)
    if cuts:
        values = values * block_scale(key, dims, cuts, -0.22, 0.18)
    return jnp.clip(values, -bound, bound).astype(kind)


def setup_inputs(seed: int = 0) -> dict:
    seeds = jax.random.split(jax.random.key(seed), 27)
    return {
        "patches": scatter_about(seeds[0], (IMAGES, PATCHES, PATCH_DIM), 1.0, 6.0, ((0, 32),)),
        "keep_mask": draw_keep_mask(jax.random.fold_in(seeds[26], 71), 0),
        "labels": plant(jax.random.randint(seeds[2], (IMAGES,), 0, CLASSES), jax.random.fold_in(seeds[2], 1), 0, CLASSES - 1).astype(jnp.int32),
        "stem_weight": scatter_about(seeds[3], (PATCH_DIM, D), PATCH_DIM ** -0.5, 0.21875, (), jnp.float32),
        "position_table": scatter_about(seeds[4], (SLOTS, D), 0.5, 3.0, (), jnp.float32),
        "attend_in": scatter_about(seeds[5], (D, 3, D), D ** -0.5, 0.21875, ((0, 8), (2, 4)), jnp.float32),
        "attend_out": scatter_about(seeds[6], (D, D), (D // 16) ** -0.5, 0.875, ((0, 4), (1, 8)), jnp.float32),
        "expand": scatter_about(seeds[7], (D, FF), D ** -0.5, 0.21875, ((0, 8), (1, 4)), jnp.float32),
        "contract": scatter_about(seeds[8], (FF, D), FF ** -0.5, 0.109375, ((0, 4), (1, 8)), jnp.float32),
        "head_weight": scatter_about(seeds[9], (D, CLASSES), D ** -0.5, 0.21875, (), jnp.float32),
        "vectors": draw_vectors(jax.random.fold_in(seeds[26], 71), 0),
        "stem_rows": jnp.clip(jnp.exp(jax.random.uniform(seeds[11], (PATCH_DIM,), jnp.float32, math.log(6.009615276525437e-07), math.log(2.403846110610175e-06))), 6.009615276525437e-07, 2.403846110610175e-06),
        "stem_cols": jnp.clip(jnp.exp(jax.random.uniform(seeds[12], (D,), jnp.float32, math.log(6.009615276525437e-07), math.log(2.403846110610175e-06))), 6.009615276525437e-07, 2.403846110610175e-06),
        "table_rows": jnp.clip(jnp.exp(jax.random.uniform(seeds[13], (SLOTS,), jnp.float32, math.log(4.622781268892595e-09), math.log(1.849112507557038e-08))), 4.622781268892595e-09, 1.849112507557038e-08),
        "table_cols": jnp.clip(jnp.exp(jax.random.uniform(seeds[14], (D,), jnp.float32, math.log(4.622781268892595e-09), math.log(1.849112507557038e-08))), 4.622781268892595e-09, 1.849112507557038e-08),
        "attend_in_rows": draw_attend_in_rows(jax.random.fold_in(seeds[26], 71), 0),
        "attend_in_cols": jnp.clip(jnp.exp(jax.random.uniform(seeds[16], (3, D), jnp.float32, math.log(1.5024038191313593e-07), math.log(6.009615276525437e-07))), 1.5024038191313593e-07, 6.009615276525437e-07),
        "attend_out_rows": jnp.clip(jnp.exp(jax.random.uniform(seeds[17], (D,), jnp.float32, math.log(1.5024038191313593e-07), math.log(6.009615276525437e-07))), 1.5024038191313593e-07, 6.009615276525437e-07),
        "attend_out_cols": draw_attend_out_cols(jax.random.fold_in(seeds[26], 71), 0),
        "expand_rows": draw_expand_rows(jax.random.fold_in(seeds[26], 71), 0),
        "expand_cols": jnp.clip(jnp.exp(jax.random.uniform(seeds[20], (FF,), jnp.float32, math.log(1.5024038191313593e-07), math.log(6.009615276525437e-07))), 1.5024038191313593e-07, 6.009615276525437e-07),
        "contract_rows": jnp.clip(jnp.exp(jax.random.uniform(seeds[21], (FF,), jnp.float32, math.log(1.5024038191313593e-07), math.log(6.009615276525437e-07))), 1.5024038191313593e-07, 6.009615276525437e-07),
        "contract_cols": draw_contract_cols(jax.random.fold_in(seeds[26], 71), 0),
        "head_rows": jnp.clip(jnp.exp(jax.random.uniform(seeds[23], (D,), jnp.float32, math.log(7.812500371073838e-06), math.log(3.125000148429535e-05))), 7.812500371073838e-06, 3.125000148429535e-05),
        "head_cols": jnp.clip(jnp.exp(jax.random.uniform(seeds[24], (CLASSES,), jnp.float32, math.log(7.812500371073838e-06), math.log(3.125000148429535e-05))), 7.812500371073838e-06, 3.125000148429535e-05),
        "vector_second": jnp.clip(jnp.exp(jax.random.uniform(seeds[25], (VECTOR_LEN,), jnp.float32, math.log(6.009615276525437e-07), math.log(2.403846110610175e-06))), 6.009615276525437e-07, 2.403846110610175e-06),
    }


eps_norm = 1e-06
eps_one = 1e-30
eps_two = 0.001
decay_rate = 0.5
clip_level = 0.3
step_rate = 1.0
smoothing = 0.1
highest = lax.Precision.HIGHEST

@jax.custom_vjp
def low(v):
    return lax.optimization_barrier(v.astype(jnp.bfloat16)).astype(jnp.float32)

@jax.custom_vjp
def low_back(v):
    return v

def low_keep(v):
    return (low(v), None)

def low_pass(kept, grad):
    return (grad,)

def back_keep(v):
    return (v, None)

def back_low(kept, grad):
    return (low(grad),)
low.defvjp(low_keep, low_pass)
low_back.defvjp(back_keep, back_low)

def layer_norm(values, gain, shift):
    centred = values - lax.optimization_barrier(jnp.mean(values, -1, keepdims=True))
    variance = lax.optimization_barrier(jnp.mean(centred * centred, -1, keepdims=True))
    return centred * lax.rsqrt(variance + eps_norm) * gain + shift

def product(form, left, right):
    return jnp.einsum(form, left, right, precision=highest)

def pieces_of(vectors):
    widths = [D] * 8 + [FF] + [D] * 3 + [CLASSES]
    pieces = []
    offset = 0
    for extent in widths:
        pieces.append(vectors[offset:offset + extent])
        offset = offset + extent
    return pieces

def image_loss(params, pixels, kept_rows, classes):
    stem_weight, position_table, attend_in, attend_out, expand, contract, head_weight, vectors = params
    stem_bias, gain_one, shift_one, query_bias, value_bias, attend_bias, gain_two, shift_two, expand_bias, contract_bias, gain_last, shift_last, head_bias = pieces_of(vectors)
    batch_count = pixels.shape[0]
    embedded = low_back(product('bpi,id->bpd', pixels, low(stem_weight))) + stem_bias
    start_rows = jnp.zeros((batch_count, 1, D), jnp.float32)
    stream = jnp.concatenate([start_rows, embedded], 1) + position_table
    present = jnp.concatenate([jnp.ones((batch_count, 1), jnp.float32), kept_rows.astype(jnp.float32)], 1)
    normed = low(layer_norm(stream, gain_one, shift_one))
    projected = low_back(product('bsd,dte->bste', normed, low(attend_in)))
    query_rows = low(projected[:, :, 0] + query_bias).reshape(batch_count, SLOTS, HEADS, HEAD_DIM)
    key_rows = low(projected[:, :, 1]).reshape(batch_count, SLOTS, HEADS, HEAD_DIM)
    value_rows = low(projected[:, :, 2] + value_bias).reshape(batch_count, SLOTS, HEADS, HEAD_DIM)
    raw_scores = low_back(product('bqhe,bkhe->bhqk', query_rows, key_rows) * HEAD_DIM ** (-0.5))
    scores = jnp.where(present[:, None, None, :] > 0.5, raw_scores, -1e+30)
    attention = low(jax.nn.softmax(scores, -1))
    attended = low_back(low(product('bhqk,bkhe->bqhe', attention, value_rows))).reshape(batch_count, SLOTS, D)
    stream = stream + low_back(product('bsd,de->bse', attended, low(attend_out))) + attend_bias
    normed = low(layer_norm(stream, gain_two, shift_two))
    hidden = low_back(product('bsd,df->bsf', normed, low(expand))) + expand_bias
    active = low(jax.nn.gelu(hidden))
    stream = stream + low_back(product('bsf,fd->bsd', active, low(contract))) + contract_bias
    kept_count = lax.optimization_barrier(jnp.sum(present, 1))
    pooled = lax.optimization_barrier(jnp.sum(present[:, :, None] * stream, 1)) / kept_count[:, None]
    final_row = low(layer_norm(pooled, gain_last, shift_last))
    logits = low_back(product('bd,dc->bc', final_row, low(head_weight))) + head_bias
    log_probs = jax.nn.log_softmax(logits, -1)
    target = smoothing / CLASSES + (1.0 - smoothing) * jax.nn.one_hot(classes, CLASSES, dtype=jnp.float32)
    return -jnp.sum(target * log_probs)

def factored_step(weight, grad, rows, cols):
    squared = grad * grad + eps_one
    rows_new = decay_rate * rows + (1.0 - decay_rate) * lax.optimization_barrier(jnp.mean(squared, 1))
    cols_new = decay_rate * cols + (1.0 - decay_rate) * lax.optimization_barrier(jnp.mean(squared, 0))
    denominator = rows_new[:, None] * cols_new[None, :] / jnp.mean(rows_new)
    update = grad * lax.rsqrt(denominator)
    update = update / jnp.maximum(1.0, jnp.sqrt(jnp.mean(update * update)) / clip_level)
    magnitude = jnp.maximum(eps_two, jnp.sqrt(jnp.mean(weight * weight)))
    return (weight - step_rate * magnitude * update, rows_new, cols_new)

def vector_step(vectors, grad, second):
    second_new = decay_rate * second + (1.0 - decay_rate) * (grad * grad + eps_one)
    update = grad * lax.rsqrt(second_new)
    update = update / jnp.maximum(1.0, jnp.sqrt(jnp.mean(update * update)) / clip_level)
    magnitude = jnp.maximum(eps_two, jnp.sqrt(jnp.mean(vectors * vectors)))
    return (vectors - step_rate * magnitude * update, second_new)

def reference(patches, keep_mask, labels, stem_weight, position_table, attend_in, attend_out, expand, contract, head_weight, vectors, stem_rows, stem_cols, table_rows, table_cols, attend_in_rows, attend_in_cols, attend_out_rows, attend_out_cols, expand_rows, expand_cols, contract_rows, contract_cols, head_rows, head_cols, vector_second):
    params = (stem_weight, position_table, attend_in, attend_out, expand, contract, head_weight, vectors)
    group_size = 8

    def one_group(carry, index):
        grads, loss_total = carry
        offset = index * group_size
        pixels = lax.dynamic_slice_in_dim(patches, offset, group_size, 0).astype(jnp.float32)
        kept_rows = lax.dynamic_slice_in_dim(keep_mask, offset, group_size, 0)
        classes = lax.dynamic_slice_in_dim(labels, offset, group_size, 0)
        group_loss, pullback = jax.vjp(lambda weights: image_loss(weights, pixels, kept_rows, classes), params)
        group_grads, = pullback(jnp.asarray(1.0 / IMAGES, jnp.float32))
        grads = jax.tree.map(jnp.add, grads, group_grads)
        return ((grads, loss_total + group_loss), None)
    zero_grads = jax.tree.map(jnp.zeros_like, params)
    steps_all = jnp.arange(IMAGES // group_size, dtype=jnp.int32)
    (grads, loss_sum), unused = lax.scan(one_group, (zero_grads, jnp.zeros((), jnp.float32)), steps_all)
    grad_stem, grad_table, grad_in, grad_out, grad_expand, grad_contract, grad_head, grad_vector = grads
    stem_new, stem_rows_new, stem_cols_new = factored_step(stem_weight, grad_stem, stem_rows, stem_cols)
    table_new, table_rows_new, table_cols_new = factored_step(position_table, grad_table, table_rows, table_cols)
    in_new, in_rows_new, in_cols_new = factored_step(attend_in.reshape(D, 3 * D), grad_in.reshape(D, 3 * D), attend_in_rows, attend_in_cols.reshape(3 * D))
    in_new = in_new.reshape(D, 3, D)
    in_cols_new = in_cols_new.reshape(3, D)
    out_new, out_rows_new, out_cols_new = factored_step(attend_out, grad_out, attend_out_rows, attend_out_cols)
    expand_new, expand_rows_new, expand_cols_new = factored_step(expand, grad_expand, expand_rows, expand_cols)
    contract_new, contract_rows_new, contract_cols_new = factored_step(contract, grad_contract, contract_rows, contract_cols)
    head_new, head_rows_new, head_cols_new = factored_step(head_weight, grad_head, head_rows, head_cols)
    vectors_new, second_new = vector_step(vectors, grad_vector, vector_second)
    return (loss_sum, stem_new, stem_rows_new, stem_cols_new, table_new, table_rows_new, table_cols_new, in_new, in_new.astype(jnp.bfloat16), in_rows_new, in_cols_new, out_new, out_new.astype(jnp.bfloat16), out_rows_new, out_cols_new, expand_new, expand_new.astype(jnp.bfloat16), expand_rows_new, expand_cols_new, contract_new, contract_new.astype(jnp.bfloat16), contract_rows_new, contract_cols_new, head_new, head_rows_new, head_cols_new, vectors_new, grad_vector, second_new)
```

```python
import functools

import jax
import jax.numpy as jnp
from jax import lax
from jax.experimental import pallas as pl
from jax.experimental.pallas import tpu as pltpu
from jax.sharding import PartitionSpec as P

D = 768
HEAD_DIM = 64
FF = 3072
CLASSES = 1000

eps_norm = 1e-06
eps_one = 1e-30
eps_two = 0.001
decay_rate = 0.5
clip_level = 0.3
step_rate = 1.0
smoothing = 0.1

ALL = ("dp", "mp")
f32 = jnp.float32
bf16 = jnp.bfloat16


class Chain:
    def __init__(self, stages):
        self.stages = stages
        self.result = None
        self.flight = next(stages)

    def advance(self, arrived):
        try:
            self.flight = self.stages.send(arrived)
        except StopIteration as end:
            self.flight, self.result = (), end.value


def sync(chains, *values):
    chains = [chain if isinstance(chain, tuple) else (chain,) for chain in chains]
    flights = [(chain[0].flight,) + chain[1:] for chain in chains]
    flights, values = lax.optimization_barrier((flights, values))
    for chain, flight in zip(chains, flights):
        chain[0].advance(flight if len(flight) > 1 else flight[0])
    return values[0] if len(values) == 1 else values


class Plain:
    blocks = None

    def __init__(self, rows, cols):
        self.rows, self.cols = rows, cols
        self.place = jnp.stack(
            [jnp.zeros((), jnp.int32)] * 4 + [lax.axis_index("dp"), lax.axis_index("mp")]
        ).astype(jnp.int32)

    def gather(self, piece):
        full = lax.all_gather(piece, ALL, axis=0)
        full = full.reshape((self.rows, self.cols) + piece.shape).swapaxes(0, 1)
        for _ in range(4):
            yield ()
        return (full.reshape(self.cols, self.rows * piece.shape[0], piece.shape[1]),)

    def whole(self, full):
        return full

    def mixed(self, body, full):
        return body(((full, False),), ())

    def reduce(self, far):
        _, near = yield ()
        grads = jnp.stack([near[1], far[1], near[0], far[0]])
        grads = grads.reshape(self.cols, self.rows, -1, grads.shape[2])
        grads = grads.swapaxes(0, 1).reshape((-1,) + grads.shape[2:])
        total = lax.psum_scatter(grads, ALL, scatter_dimension=0).astype(f32)
        for _ in range(3):
            total = yield total
        return total

    def add(self, values):
        values = lax.psum(values, ALL)
        for _ in range(5):
            values = yield values
        return values

    def add_large(self, values):
        values = lax.psum(values, ALL)
        for _ in range(8):
            values = yield values
        return values


def joined(mine, theirs, index):
    return jnp.where(
        index == 0, jnp.concatenate([mine, theirs]), jnp.concatenate([theirs, mine])
    )


def assemble(place_ref, mine_ref, theirs_ref, full_ref, sems):
    z, x, y, core = (place_ref[i] for i in range(4))
    deep, size = mine_ref.shape[1], mine_ref.shape[2]
    copies = []
    for side, source in enumerate((mine_ref, theirs_ref)):
        owner = core if side == 0 else 1 - core
        for quarter in range(4):
            second, first = quarter % 2, quarter // 2
            its_x = x ^ jnp.where(owner == 1, first, second)
            its_y = y ^ jnp.where(owner == 1, second, first)
            for level in range(deep):
                block = lax.rem(z + level, deep) * 2 + its_x
                copies.append(
                    pltpu.make_async_copy(
                        source.at[quarter, level],
                        full_ref.at[its_y * 2 + owner, block],
                        sems.at[len(copies)],
                    )
                )
    for copy in copies:
        copy.start()
    for copy in copies:
        copy.wait()


class Grid:
    deep, devices, blocks = 4, 32, 8

    def __init__(self):
        dp, mp = lax.axis_index("dp"), lax.axis_index("mp")
        self.z, self.x, self.y, self.core = dp // 2, dp % 2, mp // 2, mp % 2
        self.place = jnp.stack([self.z, self.x, self.y, self.core, dp, mp]).astype(jnp.int32)
        self.at_first = jnp.where(self.core == 0, self.y, self.x)
        self.at_second = jnp.where(self.core == 0, self.x, self.y)
        self.other = self.pairs(lambda z, x, y, c: (z, x, y, 1 - c))
        self.first = self.pairs(lambda z, x, y, c: (z, x ^ c, y ^ (1 - c), c))
        self.second = self.pairs(lambda z, x, y, c: (z, x ^ (1 - c), y ^ c, c))
        self.along_x = self.pairs(lambda z, x, y, c: (z, 1 - x, y, c))
        self.along_y = self.pairs(lambda z, x, y, c: (z, x, 1 - y, c))
        self.up = [self.pairs(lambda z, x, y, c, s=s: ((z + s) % 4, x, y, c)) for s in range(4)]
        self.flip_z = [self.pairs(lambda z, x, y, c, s=s: (z ^ s, x, y, c)) for s in range(4)]

    def pairs(self, move):
        table = []
        for index in range(self.devices):
            z, x, y, c = move(index // 8, index // 4 % 2, index // 2 % 2, index % 2)
            table.append((index, ((z * 2 + x) * 2 + y) * 2 + c))
        return table

    @staticmethod
    def send(values, table):
        return lax.ppermute(values, ALL, table)

    def gather(self, piece):
        got = yield [self.send(piece, self.up[-s]) for s in (1, 2, 3)]
        column = jnp.stack([piece] + got)[None]
        got = yield self.send(column, self.second)
        pair = jnp.concatenate([column, got])
        got = yield self.send(pair, self.first)
        quad = jnp.concatenate([pair, got])
        theirs = yield self.send(quad, self.other)
        return quad, theirs

    def mixed(self, body, quad, theirs):
        full = (4, self.blocks) + quad.shape[2:]
        return body(
            ((quad, "any"), (theirs, "any")), ((full, quad.dtype), ((self.devices,), None))
        )

    def whole(self, quad, theirs):
        r, c = quad.shape[2:]
        full = pl.pallas_call(
            assemble,
            in_specs=[
                pl.BlockSpec(memory_space=pltpu.SMEM),
                pl.BlockSpec(memory_space=pl.ANY),
                pl.BlockSpec(memory_space=pl.ANY),
            ],
            out_specs=pl.BlockSpec(memory_space=pltpu.VMEM),
            out_shape=jax.ShapeDtypeStruct((4, self.blocks, r, c), quad.dtype),
            scratch_shapes=[pltpu.SemaphoreType.DMA((self.devices,))],
            compiler_params=pltpu.CompilerParams(vmem_limit_bytes=16 * 1024 * 1024),
        )(self.place, quad, theirs)
        return full.reshape(4, self.blocks * r, c)

    def reduce(self, far):
        theirs, near = yield self.send(far, self.other)
        shape = (4, self.deep, near.shape[1] // self.blocks, near.shape[2])
        near, theirs = near.reshape(shape), theirs.reshape(shape)

        def chip(index):
            return (
                lax.dynamic_index_in_dim(near, index, 0, keepdims=False).astype(f32)
                + lax.dynamic_index_in_dim(theirs, index, 0, keepdims=False).astype(f32)
            )

        got = yield self.send(jnp.stack([chip(0), chip(1 + self.core)]).astype(bf16), self.first)
        away = (chip(2 - self.core) + got[0].astype(f32)).astype(bf16)
        came = yield self.send(away, self.second)
        column = chip(3) + got[1].astype(f32) + came.astype(f32)
        low = column.astype(bf16)
        total = column[0]
        for part in (yield [self.send(low[s], self.up[s]) for s in (1, 2, 3)]):
            total = total + part.astype(f32)
        return total

    def add(self, values):
        for table in (self.other, self.along_y, self.along_x, self.flip_z[1], self.flip_z[2]):
            values = values + (yield self.send(values, table))
        return values

    def add_large(self, values):
        shape = values.shape
        values = values.reshape((self.devices, -1) + shape[1:])
        steps = (
            (self.core, self.other),
            (self.at_first, self.first),
            (self.at_second, self.second),
        )
        for index, table in steps:
            half = values.shape[0] // 2
            theirs = lax.dynamic_slice_in_dim(values, (1 - index) * half, half, 0)
            got = yield self.send(theirs.astype(bf16), table)
            mine = lax.dynamic_slice_in_dim(values, index * half, half, 0)
            values = mine.astype(f32) + got.astype(f32)
        low = values.astype(bf16)
        parts = [
            lax.dynamic_index_in_dim(low, (self.z + s) % 4, 0, keepdims=False) for s in (1, 2, 3)
        ]
        total = lax.dynamic_index_in_dim(values, self.z, 0, keepdims=False)
        for part in (yield [self.send(part, self.up[s]) for s, part in enumerate(parts, 1)]):
            total = total + part.astype(f32)
        total = total.astype(bf16)
        got = yield [self.send(total, self.up[-s]) for s in (1, 2, 3)]
        pile = jnp.stack([total] + got)
        pile = lax.dynamic_slice_in_dim(jnp.concatenate([pile, pile]), 4 - self.z, 4, 0)
        for index, table in reversed(steps):
            pile = joined(pile, (yield self.send(pile, table)), index)
        return pile.reshape(shape)


def layer_norm(values, gain, shift):
    centred = values - jnp.mean(values, -1, keepdims=True)
    variance = jnp.mean(centred * centred, -1, keepdims=True)
    return centred * lax.rsqrt(variance + eps_norm) * gain + shift


def pieces_of(vectors):
    widths = [D] * 8 + [FF] + [D] * 3 + [CLASSES]
    pieces = []
    offset = 0
    for extent in widths:
        pieces.append(vectors[offset : offset + extent])
        offset = offset + extent
    return pieces


def product(form, left, right):
    return jnp.einsum(form, left, right, preferred_element_type=f32)


def factored_step(weight, square, grad, rows, cols):
    squared = grad * grad + eps_one
    rows_new = decay_rate * rows + (1.0 - decay_rate) * jnp.mean(squared, 1)
    cols_new = decay_rate * cols + (1.0 - decay_rate) * jnp.mean(squared, 0)
    denominator = rows_new[:, None] * cols_new[None, :] / jnp.mean(rows_new)
    update = grad * lax.rsqrt(denominator)
    update = update / jnp.maximum(1.0, jnp.sqrt(jnp.mean(update * update)) / clip_level)
    magnitude = jnp.maximum(eps_two, jnp.sqrt(square / weight.size))
    return (weight - step_rate * magnitude * update, rows_new, cols_new)


def vector_step(vectors, square, grad, second):
    second_new = decay_rate * second + (1.0 - decay_rate) * (grad * grad + eps_one)
    update = grad * lax.rsqrt(second_new)
    update = update / jnp.maximum(1.0, jnp.sqrt(jnp.mean(update * update)) / clip_level)
    magnitude = jnp.maximum(eps_two, jnp.sqrt(square / vectors.size))
    return (vectors - step_rate * magnitude * update, second_new)


def normal_parts(values):
    centred = values - jnp.mean(values, -1, keepdims=True)
    inverse = lax.rsqrt(jnp.mean(centred * centred, -1, keepdims=True) + eps_norm)
    return centred * inverse, inverse


def pull_normal(values, gain, grads):
    hat, inverse = normal_parts(values)
    scaled = grads * gain
    mean_one = jnp.mean(scaled, -1, keepdims=True)
    mean_two = jnp.mean(scaled * hat, -1, keepdims=True)
    below = (scaled - mean_one - hat * mean_two) * inverse
    return below, jnp.sum(grads * hat, 0, keepdims=True), jnp.sum(grads, 0, keepdims=True)


def dot(left, right, left_dim=1, right_dim=0):
    return lax.dot_general(
        left, right, (((left_dim,), (right_dim,)), ((), ())), preferred_element_type=f32
    )


def probabilities(query, key, visible):
    scores = dot(query, key, 1, 1) * HEAD_DIM ** (-0.5)
    scores = jnp.where(visible, scores, -1e30)
    raised = jnp.exp(scores - jnp.max(scores, -1, keepdims=True))
    return raised * (1.0 / jnp.sum(raised, -1, keepdims=True))


def head_masks(share):
    lane = lax.broadcasted_iota(jnp.int32, (1, share), 1) // HEAD_DIM
    return [lane == head for head in range(share // HEAD_DIM)]


def stacked(rows, masks):
    return jnp.concatenate([jnp.where(mask, rows, jnp.zeros((), rows.dtype)) for mask in masks])


def unstacked(every, masks):
    size = every.shape[0] // len(masks)
    result = every[:size]
    for head, mask in enumerate(masks[1:], 1):
        result = jnp.where(mask, every[head * size : (head + 1) * size], result)
    return result


def turn(place_ref, values, result_ref, blocks):
    turned = values.T
    if blocks is None:
        result_ref[...] = turned
        return
    size, deep = turned.shape[0] // blocks, blocks // 2
    for block in range(blocks):
        level = lax.rem(block // 2 - place_ref[0] + deep, deep)
        spot = (1 - (block % 2 ^ place_ref[1])) * deep + level
        rows = pl.ds(pl.multiple_of(spot * size, size), size)
        result_ref[rows, :] = turned[block * size : (block + 1) * size, :]


def attend_kernel(
    place_ref,
    rows_ref,
    weight_ref,
    query_bias_ref,
    value_bias_ref,
    present_ref,
    stream_ref,
    bias_ref,
    gain_ref,
    shift_ref,
    column_ref,
    qkv_ref,
    attended_ref,
    stream_out_ref,
    rows_out_ref,
    turned_one_ref,
    turned_two_ref,
    sum_ref,
    *,
    blocks,
):
    step = pl.program_id(0)
    count, padded = present_ref.shape
    share = attended_ref.shape[2]
    weight = weight_ref[0]

    @pl.when(step == 0)
    def _():
        turn(place_ref, rows_ref[...], turned_one_ref, blocks)

    projected = dot(rows_ref[...], weight[:, : 3 * share])
    query = (projected[:, :share] + query_bias_ref[0]).astype(bf16)
    key = projected[:, share : 2 * share].astype(bf16)
    value = (projected[:, 2 * share :] + value_bias_ref[0]).astype(bf16)
    qkv_ref[0, 0] = query
    qkv_ref[0, 1] = key
    qkv_ref[0, 2] = value
    masks = head_masks(share)
    for image in range(count):
        span = slice(image * padded, (image + 1) * padded)
        visible = present_ref[image : image + 1, :] > 0.5
        low = probabilities(stacked(query[span], masks), key[span], visible).astype(bf16)
        every = dot(low, value[span])
        attended_ref[0, span, :] = unstacked(every, masks).astype(bf16)
    part = dot(attended_ref[0], weight[:, 3 * share :], 1, 1)

    @pl.when(step == 0)
    def _():
        stream_out_ref[...] = stream_ref[...] + bias_ref[...] + part

    @pl.when(step > 0)
    def _():
        stream_out_ref[...] += part

    @pl.when(step == pl.num_programs(0) - 1)
    def _():
        hat, _ = normal_parts(stream_out_ref[...])
        rows_two = (hat * gain_ref[...] + shift_ref[...]).astype(bf16)
        rows_out_ref[...] = rows_two
        turn(place_ref, rows_two, turned_two_ref, blocks)
        for image in range(count):
            span = slice(image * padded, (image + 1) * padded)
            line = jnp.sum(stream_out_ref[span, :] * column_ref[span, :], 0, keepdims=True)
            sum_ref[image : image + 1, :] = line
            sum_ref[image + count : image + count + 1, :] = line


def hidden_kernel(
    place_ref, rows_ref, weight_ref, bias_ref, chooser_ref, column_ref, sum_ref, slope_ref
):
    hidden = dot(rows_ref[...], weight_ref[0]) + bias_ref[0]
    first, second = 0.7978845608028654, 0.044715
    square = hidden * hidden
    bent = jnp.tanh(first * hidden * (1.0 + second * square))
    half = 0.5 * (1.0 + bent)
    active = (hidden * half).astype(bf16)
    sum_ref[0] = dot(chooser_ref[...], active)
    slope = half + 0.5 * hidden * (1.0 - bent * bent) * first * (1.0 + 3.0 * second * square)
    slope_ref[0] = (slope * column_ref[...]).astype(bf16)


def expand_back_kernel(
    place_ref,
    turned_ref,
    weight_ref,
    slope_ref,
    d_active_ref,
    *refs,
):
    grad_ref, bias_ref, d_rows_ref, d_hidden_low = refs[-4:]
    step = pl.program_id(0)
    count = d_active_ref.shape[1] // 2
    padded = slope_ref.shape[1] // count
    bias = jnp.zeros((1, d_hidden_low.shape[1]), f32)
    for image in range(count):
        span = slice(image * padded, (image + 1) * padded)
        d_hidden = slope_ref[0, span, :].astype(f32) * d_active_ref[0, image : image + 1, :]
        bias = bias + jnp.sum(d_hidden, 0, keepdims=True)
        d_hidden_low[span, :] = d_hidden.astype(bf16)
    bias_ref[0] = bias
    grad_ref[0] = dot(turned_ref[...], d_hidden_low[...]).astype(bf16)
    part = dot(d_hidden_low[...], weight_ref[0], 1, 1)

    @pl.when(step == 0)
    def _():
        d_rows_ref[...] = part + refs[0][...] if len(refs) > 4 else part

    @pl.when(step > 0)
    def _():
        d_rows_ref[...] += part


def between_kernel(
    place_ref,
    d_rows_ref,
    d_row_ref,
    column_ref,
    stream_ref,
    gain_ref,
    d_stream_ref,
    d_low_ref,
    turned_ref,
    vector_ref,
    *,
    blocks,
):
    count = d_row_ref.shape[0] // 2
    padded = stream_ref.shape[0] // count
    below, gain, shift = pull_normal(stream_ref[...], gain_ref[...], d_rows_ref[...])
    vector_ref[1:2, :] = gain
    vector_ref[2:3, :] = shift
    bias = jnp.zeros((1, below.shape[1]), f32)
    for image in range(count):
        span = slice(image * padded, (image + 1) * padded)
        d_stream = below[span] + d_row_ref[image : image + 1, :] * column_ref[span, :]
        bias = bias + jnp.sum(d_stream, 0, keepdims=True)
        d_stream_ref[span, :] = d_stream
        d_low_ref[span, :] = d_stream.astype(bf16)
    vector_ref[0:1, :] = bias
    turn(place_ref, d_low_ref[...], turned_ref, blocks)


def attend_back_kernel(
    place_ref,
    turned_ref,
    weight_ref,
    qkv_ref,
    attended_ref,
    column_ref,
    d_low_ref,
    d_turned_ref,
    *refs,
):
    grad_ref, bias_ref, d_rows_ref, d_projected = refs[-4:]
    step = pl.program_id(0)
    share = attended_ref.shape[2]
    count = bias_ref.shape[1] // 2
    padded = attended_ref.shape[1] // count
    scale = HEAD_DIM ** (-0.5)
    weight = weight_ref[0]
    d_attended = dot(d_low_ref[...], weight[:, 3 * share :]).astype(bf16)
    masks = head_masks(share)
    for image in range(count):
        span = slice(image * padded, (image + 1) * padded)
        hidden = column_ref[span, :] < 0.5
        query, key, value = (qkv_ref[0, part, span, :] for part in range(3))
        query = query * jnp.asarray(scale, bf16)
        queries = stacked(query, masks)
        d_images = stacked(d_attended[span], masks)
        scores = jnp.where(hidden, -1e30, dot(key, queries, 1, 1))
        raised = jnp.exp(scores - jnp.max(scores, 0, keepdims=True))
        probs = raised * (1.0 / jnp.sum(raised, 0, keepdims=True))
        d_probs = dot(value, d_images, 1, 1)
        inner = jnp.sum(probs * d_probs, 0, keepdims=True)
        d_scores = (probs * (d_probs - inner)).astype(bf16)
        d_value = dot(probs.astype(bf16), d_images)
        d_key = dot(d_scores, queries)
        d_query = unstacked(dot(d_scores, key, 0, 0), masks) * scale
        bias_ref[0, image : image + 1, :] = jnp.sum(d_query, 0, keepdims=True)
        bias_ref[0, count + image : count + image + 1, :] = jnp.sum(d_value, 0, keepdims=True)
        d_projected[span, :share] = d_query.astype(bf16)
        d_projected[span, share : 2 * share] = d_key.astype(bf16)
        d_projected[span, 2 * share :] = d_value.astype(bf16)
    grad_ref[0, :, : 3 * share] = dot(turned_ref[...], d_projected[...]).astype(bf16)
    grad_ref[0, :, 3 * share :] = dot(d_turned_ref[...], attended_ref[0]).astype(bf16)
    part = dot(d_projected[...], weight[:, : 3 * share], 1, 1)

    @pl.when(step == 0)
    def _():
        d_rows_ref[...] = part + refs[0][...] if len(refs) > 4 else part

    @pl.when(step > 0)
    def _():
        d_rows_ref[...] += part


def stem_back_kernel(
    place_ref, d_rows_ref, d_stream_ref, stream_ref, gain_ref, pixels_ref, both_ref, vector_ref
):
    rows, width = pixels_ref.shape
    padded = both_ref.shape[0] - width
    below, gain, shift = pull_normal(stream_ref[...], gain_ref[...], d_rows_ref[...])
    vector_ref[0:1, :] = gain
    vector_ref[1:2, :] = shift
    below = below + d_stream_ref[...]
    slots = vector_ref.shape[0] - 8
    table = below[:slots]
    for image in range(1, rows // slots):
        table = table + below[image * slots : (image + 1) * slots]
    vector_ref[8:, :] = table
    both_ref[:width, :] = dot(pixels_ref[...].T, below.astype(bf16)).astype(bf16)
    both_ref[width : width + slots, :] = table.astype(bf16)
    both_ref[width + slots :, :] = jnp.zeros((padded - slots, both_ref.shape[1]), bf16)


def classify(pooled, labels, head, gain, shift, bias, inverse_count):
    hat, inverse = normal_parts(pooled)
    low = (hat * gain + shift).astype(bf16)
    logits = dot(low, head) + bias
    logits = logits - jnp.max(logits, -1, keepdims=True)
    raised = jnp.exp(logits)
    total = jnp.sum(raised, -1, keepdims=True)
    lane = lax.broadcasted_iota(jnp.int32, logits.shape, 1)
    target = jnp.where(lane == labels.astype(jnp.int32), 1.0 - smoothing, 0.0) + smoothing / CLASSES
    score = jnp.sum(target * (logits - jnp.log(total)), -1, keepdims=True)
    d_logits = (raised * (1.0 / total) - target) * inverse_count
    d_final = dot(d_logits.astype(bf16), head, 1, 1)
    scaled = d_final * gain
    mean_one = jnp.mean(scaled, -1, keepdims=True)
    mean_two = jnp.mean(scaled * hat, -1, keepdims=True)
    return score, low, d_logits, d_final, hat, (scaled - mean_one - hat * mean_two) * inverse


def split(values):
    high = values.astype(bf16)
    return high, (values - high.astype(f32)).astype(bf16)


def own_head_kernel(
    place_ref,
    active_ref,
    sum_ref,
    facts_ref,
    contract_bias_ref,
    gain_ref,
    shift_ref,
    head_ref,
    head_bias_ref,
    *refs,
    inverse_count,
):
    if len(refs) == 4:
        full_ref, piece_ref, d_row_ref, d_active_ref = refs
    else:
        mine_ref, theirs_ref, piece_ref, d_row_ref, d_active_ref, full_ref, sems = refs
        assemble(place_ref, mine_ref, theirs_ref, full_ref, sems)
    groups, twice, width = active_ref.shape
    rows = sum_ref.shape[1]
    mixed = jnp.zeros((twice, rows), f32)
    for group in range(groups):
        weight = full_ref[group].reshape(rows, width)
        for part in split(active_ref[group]):
            mixed = mixed + dot(part, weight, 1, 1)
    kept, labels = facts_ref[:, 0:1], facts_ref[:, 1:2]
    pooled = (sum_ref[...] + mixed) / kept + contract_bias_ref[...]
    d_pooled = classify(
        pooled,
        labels,
        head_ref[...],
        gain_ref[...],
        shift_ref[...],
        head_bias_ref[...],
        inverse_count,
    )[-1]
    d_row = d_pooled / kept
    d_row_ref[...] = d_row
    d_row_low = d_row.astype(bf16)
    first = lax.broadcasted_iota(jnp.int32, (twice, 1), 0) < twice // 2
    for group in range(groups):
        d_active_ref[group] = dot(d_row_low, full_ref[group].reshape(rows, width))
    for part, (line, fact) in enumerate(zip(split(pooled), split(facts_ref[...]))):
        piece_ref[part * twice : (part + 1) * twice, :rows] = line
        piece_ref[part * twice : (part + 1) * twice, rows:] = fact
    for half in range(groups // 2):
        line = jnp.where(first, active_ref[2 * half], active_ref[2 * half + 1])
        span = slice((2 + half) * twice, (3 + half) * twice)
        piece_ref[span, :rows] = line.astype(bf16)
        piece_ref[span, rows:] = jnp.zeros((twice, piece_ref.shape[1] - rows), bf16)


def all_head_kernel(
    place_ref,
    pieces_ref,
    gain_ref,
    shift_ref,
    head_ref,
    head_bias_ref,
    grad_ref,
    contract_ref,
    vector_ref,
    bias_ref,
    *,
    inverse_count,
):
    pieces = pieces_ref[0].astype(f32)
    count, rows = pieces.shape[0], gain_ref.shape[1]
    twice = pieces.shape[1] // 4

    def part(index):
        return pieces[:, index * twice : (index + 1) * twice].reshape(count * twice, -1)

    lines = part(0) + part(1)
    pooled, kept, labels = lines[:, :rows], lines[:, rows : rows + 1], lines[:, rows + 1 : rows + 2]
    score, low, d_logits, d_final, hat, d_pooled = classify(
        pooled,
        labels,
        head_ref[...],
        gain_ref[...],
        shift_ref[...],
        head_bias_ref[...],
        inverse_count,
    )
    half = lax.broadcasted_iota(jnp.int32, (count * twice, 1), 0) % twice // (twice // 2)
    once = half == 0
    d_logits = jnp.where(once, d_logits, 0.0)
    own = place_ref[5]
    active = jnp.where(own // 2 == 0, part(2)[:, :rows], part(3)[:, :rows]).astype(bf16)
    d_row = jnp.where(half == own % 2, d_pooled / kept, 0.0).astype(bf16)
    share = contract_ref.shape[0]
    line = lax.broadcasted_iota(jnp.int32, (rows, share), 0)
    lane = lax.broadcasted_iota(jnp.int32, (rows, share), 1)
    chooser = (line == lane + place_ref[4] * share).astype(f32).astype(bf16)
    d_row = dot(d_row, chooser).astype(bf16)

    def total(values):
        return jnp.sum(jnp.where(once, values, 0.0), 0, keepdims=True)

    results = (
        (grad_ref, slice(None), dot(low, d_logits.astype(bf16), 0, 0)),
        (contract_ref, slice(None), dot(d_row, active, 0, 0)),
        (vector_ref, slice(0, 1), total(d_pooled)),
        (vector_ref, slice(1, 2), total(d_final * hat)),
        (vector_ref, slice(2, 3), total(d_final)),
        (bias_ref, slice(0, 1), jnp.sum(d_logits, 0, keepdims=True)),
        (bias_ref, slice(1, 2), -total(score) + jnp.zeros((1, bias_ref.shape[1]), f32)),
    )
    for ref, span, value in results:

        @pl.when(pl.program_id(0) == 0)
        def _(ref=ref, span=span, value=value):
            ref[span, :] = value

        @pl.when(pl.program_id(0) > 0)
        def _(ref=ref, span=span, value=value):
            ref[span, :] += value


def layout(data, groups):
    return 0, data, data + 5 * groups, -(-(data + 5 * groups + 6) // 8) * 8


def across(column):
    n = column.shape[0]
    wide = jnp.broadcast_to(column, (n, 128))
    if n < 128:
        wide = jnp.concatenate([wide, jnp.zeros((128 - n, 128), f32)])
    return wide.T[0:1]


def down(row, n):
    return jnp.broadcast_to(row, (128, 128)).T[:n, 0:1]


def put(count, index, line):
    spot = lax.broadcasted_iota(jnp.int32, (count, 1), 0)
    return jnp.where(spot == index, line, 0.0)


def pick(lines, index):
    spot = lax.broadcasted_iota(jnp.int32, (lines.shape[0], 1), 0)
    return jnp.sum(jnp.where(spot == index, lines, 0.0), 0, keepdims=True)


def sums_kernel(
    place_ref,
    attend_ref,
    expand_ref,
    contract_ref,
    squares_ref,
    vector_one_ref,
    vector_two_ref,
    expand_far_ref,
    expand_near_ref,
    heads_far_ref,
    heads_near_ref,
    sums_ref,
    *,
    data,
    groups,
    share,
    patch_count,
):
    block, group = place_ref[4], place_ref[5]
    own = place_ref[2] * 2 + place_ref[3]
    _, at_group, at_single, _ = layout(data, groups)
    sums_ref[...] = jnp.zeros(sums_ref.shape, f32)
    lane = lax.broadcasted_iota(jnp.int32, (1, attend_ref.shape[1]), 1)
    for index, ref in enumerate((attend_ref, expand_ref, contract_ref)):
        grad = ref[...]
        squared = grad * grad + eps_one
        span = slice(at_group + index * groups, at_group + (index + 1) * groups)
        sums_ref[span, :] = put(groups, group, jnp.sum(squared, 0, keepdims=True))
        if index == 0:
            lines = (
                jnp.sum(jnp.where(lane < 3 * share, squared, 0.0), 1, keepdims=True),
                jnp.sum(jnp.where(lane < 3 * share, 0.0, squared), 1, keepdims=True),
            )
        else:
            lines = (jnp.sum(squared, 1, keepdims=True),)
        for part, line in enumerate(lines):
            spot = (index + (index > 0) + part) * 128
            sums_ref[:data, spot : spot + 128] = put(data, block, across(line))
    sums_ref[:data, 512:640] = put(data, block, squares_ref[...])
    at_group += 3 * groups
    lines = jnp.zeros((groups, expand_far_ref.shape[2]), f32)
    for ref, order in ((expand_far_ref, (3, 1)), (expand_near_ref, (2, 0))):
        for step, distance in enumerate(order):
            lines = lines + put(groups, own ^ distance, ref[step])
    sums_ref[at_group : at_group + groups, :] = lines
    at_group += groups
    count = heads_far_ref.shape[1] // 2
    for at, span in ((0, slice(count)), (256, slice(count, 2 * count))):
        lines = jnp.zeros((groups, share), f32)
        for ref, order in ((heads_far_ref, (3, 1)), (heads_near_ref, (2, 0))):
            for step, distance in enumerate(order):
                line = jnp.sum(ref[step][span], 0, keepdims=True)
                lines = lines + put(groups, own ^ distance, line)
        sums_ref[at_group : at_group + groups, at : at + share] = lines
    stem_bias = jnp.sum(vector_one_ref[8 : 8 + patch_count, :], 0, keepdims=True)
    singles = (stem_bias, vector_one_ref[0:2, :], vector_two_ref[0:3, :])
    for line in singles:
        sums_ref[at_single : at_single + line.shape[0], :] = line
        at_single += line.shape[0]


def renew_kernel(
    place_ref,
    sums_ref,
    rows_ref,
    cols_ref,
    attend_ref,
    expand_ref,
    contract_ref,
    rows_new_ref,
    cols_new_ref,
    update_ref,
    scalar_ref,
    square_ref,
    *,
    data,
    groups,
    share,
):
    block, group = place_ref[4], place_ref[5]
    size = attend_ref.shape[0]
    width = attend_ref.shape[1]
    _, at_group, _, _ = layout(data, groups)
    length, hidden = data * size, groups * width
    lane = lax.broadcasted_iota(jnp.int32, (1, width), 1)
    first = lane < 3 * share
    spare = lax.broadcasted_iota(jnp.int32, (1, 128), 1) < size
    counts = (3 * length, length, hidden, hidden)
    means = []
    for index, count in enumerate(counts):
        span = slice(index * 128, (index + 1) * 128)
        new = decay_rate * rows_ref[:, span] + (1.0 - decay_rate) * (sums_ref[:data, span] / count)
        rows_new_ref[:, span] = new
        means.append(jnp.sum(jnp.where(spare, new, 0.0), keepdims=True) / length)
    for index, count in enumerate((length, length, length)):
        span = slice(index * groups, (index + 1) * groups)
        lines = sums_ref[at_group + index * groups : at_group + (index + 1) * groups, :]
        new = decay_rate * cols_ref[span, :] + (1.0 - decay_rate) * (lines / count)
        cols_new_ref[span, :] = new
        if index == 0:
            means[1] = jnp.sum(jnp.where(first, 0.0, new), keepdims=True) / length
        if index == 2:
            means[3] = jnp.sum(new, keepdims=True) / hidden
    scalars = jnp.zeros((1, 128), f32)
    place_lane = lax.broadcasted_iota(jnp.int32, (1, 128), 1)
    for index, ref in enumerate((attend_ref, expand_ref, contract_ref)):
        across_row = pick(cols_new_ref[index * groups : (index + 1) * groups, :], group)

        def row(which):
            span = slice(which * 128, (which + 1) * 128)
            return down(pick(rows_new_ref[:, span], block), size)

        if index == 0:
            denominator = jnp.where(
                first, row(0) * across_row / means[0], row(1) * across_row / means[1]
            )
        else:
            denominator = row(index + 1) * across_row / means[index + 1]
        update = ref[...] * lax.rsqrt(denominator)
        update_ref[index] = update
        squared = update * update
        if index == 0:
            totals = (jnp.where(first, squared, 0.0), jnp.where(first, 0.0, squared))
        else:
            totals = (squared,)
        for part, total in enumerate(totals):
            spot = index + (index > 0) + part
            scalars = jnp.where(place_lane == spot, jnp.sum(total, keepdims=True), scalars)
    scalar_ref[...] = jnp.broadcast_to(scalars, scalar_ref.shape)
    squares = jnp.sum(sums_ref[:data, 512:640], 0, keepdims=True)
    square_ref[...] = jnp.broadcast_to(squares, square_ref.shape)


def step_kernel(
    place_ref,
    update_ref,
    scalar_ref,
    square_ref,
    attend_ref,
    expand_ref,
    contract_ref,
    in_ref,
    in_low_ref,
    out_ref,
    out_low_ref,
    expand_new_ref,
    expand_low_ref,
    contract_new_ref,
    contract_low_ref,
    *,
    sizes,
):
    share = in_ref.shape[2]
    scales = []
    for index, size in enumerate(sizes):
        total = scalar_ref[0:1, index : index + 1]
        square = square_ref[0:1, index : index + 1]
        clip = jnp.maximum(1.0, jnp.sqrt(total / size) / clip_level)
        scales.append(step_rate * jnp.maximum(eps_two, jnp.sqrt(square / size)) / clip)
    lane = lax.broadcasted_iota(jnp.int32, (1, attend_ref.shape[1]), 1)
    scale = jnp.where(lane < 3 * share, scales[0], scales[1])
    attend = attend_ref[...] - scale * update_ref[0]
    for part in range(3):
        lines = attend[:, part * share : (part + 1) * share]
        in_ref[part] = lines
        in_low_ref[part] = lines.astype(bf16)
    out = attend[:, 3 * share :].T
    out_ref[...] = out
    out_low_ref[...] = out.astype(bf16)
    expand = expand_ref[...] - scales[2] * update_ref[1]
    expand_new_ref[...] = expand
    expand_low_ref[...] = expand.astype(bf16)
    contract = (contract_ref[...] - scales[3] * update_ref[2]).T
    contract_new_ref[...] = contract
    contract_low_ref[...] = contract.astype(bf16)


def call(body, groups, place, operands, results, scratch=(), flops=0, turns=None):
    def group(step, place_ref):
        if turns is None:
            return step
        return (place_ref[2] * 2 + place_ref[3]) ^ (turns[0] + turns[1] * step)

    def spec(shape, by_group, index):
        if by_group == "any":
            return pl.BlockSpec(memory_space=pl.ANY)
        if by_group:
            return pl.BlockSpec((1,) + shape[1:], lambda g, p: (index(g, p),) + (0,) * (len(shape) - 1))
        return pl.BlockSpec(shape, lambda g, p: (0,) * len(shape))

    return pl.pallas_call(
        body,
        grid_spec=pltpu.PrefetchScalarGridSpec(
            num_scalar_prefetch=1,
            grid=(groups,),
            in_specs=[spec(value.shape, by_group, group) for value, by_group in operands],
            out_specs=[spec(shape, by_group, lambda g, p: g) for shape, _, by_group in results],
            scratch_shapes=[
                pltpu.SemaphoreType.DMA(shape) if kind is None else pltpu.VMEM(shape, kind)
                for shape, kind in scratch
            ],
        ),
        out_shape=[jax.ShapeDtypeStruct(shape, kind) for shape, kind, _ in results],
        compiler_params=pltpu.CompilerParams(vmem_limit_bytes=48 * 1024 * 1024),
        cost_estimate=pl.CostEstimate(flops=flops, bytes_accessed=16_000_000, transcendentals=0),
    )(place, *[value for value, _ in operands])


def local(
    patches,
    keep_mask,
    labels,
    stem_weight,
    position_table,
    attend_in,
    attend_out,
    expand,
    contract,
    head_weight,
    vectors,
    stem_rows,
    stem_cols,
    table_rows,
    table_cols,
    attend_in_rows,
    attend_in_cols,
    attend_out_rows,
    attend_out_cols,
    expand_rows,
    expand_cols,
    contract_rows,
    contract_cols,
    head_rows,
    head_cols,
    vector_second,
):
    data_size, model_size = lax.axis_size("dp"), lax.axis_size("mp")
    links = Grid() if (data_size, model_size) == (8, 4) else Plain(data_size, model_size)
    here = links.place
    count, patch_count, _ = patches.shape
    groups = model_size
    pair = groups // 2
    image_count = count * data_size * model_size
    inverse_count = 1.0 / image_count
    row_share, _, head_share = attend_in.shape
    hidden_share = expand.shape[1]
    in_share = 3 * head_share
    slots = patch_count + 1
    padded = -(-slots // 16) * 16
    rows = count * padded
    (
        stem_bias,
        gain_one,
        shift_one,
        query_bias,
        value_bias,
        attend_bias,
        gain_two,
        shift_two,
        expand_bias,
        contract_bias,
        gain_last,
        shift_last,
        head_bias,
    ) = pieces_of(vectors)

    attend_own = jnp.concatenate([attend_in.reshape(row_share, in_share), attend_out.T], 1)
    attend_chain = Chain(links.gather(attend_own.astype(bf16)))
    contract_own = contract.T
    squares = jnp.stack([jnp.sum(w * w) for w in (attend_in, attend_out, expand, contract)])
    squares = jnp.pad(squares[None], ((0, 0), (0, 124)))
    stem_low = stem_weight.astype(bf16)
    pixels = jnp.pad(patches, ((0, 0), (0, padded - patch_count), (0, 0))).reshape(rows, -1)
    table = jnp.concatenate(
        [position_table[1:] + stem_bias, position_table[:1], jnp.zeros((padded - slots, D), f32)]
    )
    present = jnp.concatenate(
        [
            keep_mask.astype(f32),
            jnp.ones((count, 1), f32),
            jnp.zeros((count, padded - slots), f32),
        ],
        1,
    )
    expand_piece, contract_piece = expand.astype(bf16), contract_own.astype(bf16)
    (
        attend_own,
        contract_own,
        squares,
        stem_low,
        pixels,
        table,
        present,
        expand_piece,
        contract_piece,
    ) = sync(
        [attend_chain],
        attend_own,
        contract_own,
        squares,
        stem_low,
        pixels,
        table,
        present,
        expand_piece,
        contract_piece,
    )
    expand_chain = Chain(links.gather(expand_piece))
    stream_zero = dot(pixels, stem_low).reshape(count, padded, D) + table
    stream_zero = stream_zero.reshape(rows, D)
    rows_one = layer_norm(stream_zero, gain_one, shift_one).astype(bf16)
    stream_zero, rows_one, contract_piece, head_weight, position_table, stem_weight = sync(
        [attend_chain, expand_chain],
        stream_zero,
        rows_one,
        contract_piece,
        head_weight,
        position_table,
        stem_weight,
    )
    contract_chain = Chain(links.gather(contract_piece))
    head_low = head_weight.astype(bf16)
    whole_squares = [jnp.sum(w * w) for w in (stem_weight, position_table, head_weight, vectors)]
    kept = jnp.sum(present, 1)[:, None]
    facts = jnp.concatenate([kept, labels[:, None].astype(f32), jnp.zeros((count, 126), f32)], 1)
    facts = jnp.concatenate([facts, facts])
    chooser = (jnp.eye(count)[:, :, None] * present[None]).reshape(count, rows).astype(bf16)
    chooser = jnp.concatenate([chooser, chooser])
    column = present.reshape(rows, 1)

    def by_block(values):
        return jnp.pad(values.reshape(data_size, row_share), ((0, 0), (0, 128 - row_share)))

    old_rows = jnp.concatenate(
        [by_block(v) for v in (attend_in_rows, attend_out_cols, expand_rows, contract_cols)], 1
    )
    in_cols = attend_in_cols.reshape(3, groups, head_share).swapaxes(0, 1)
    old_cols = jnp.concatenate(
        [
            jnp.concatenate(
                [in_cols.reshape(groups, -1), attend_out_rows.reshape(groups, -1)], 1
            ),
            expand_cols.reshape(groups, -1),
            contract_rows.reshape(groups, -1),
        ]
    )
    head_low, whole_squares, facts, chooser, column, old_rows, old_cols = sync(
        [attend_chain, contract_chain],
        head_low,
        whole_squares,
        facts,
        chooser,
        column,
        old_rows,
        old_cols,
    )
    sync([attend_chain, expand_chain])
    attend_all = links.whole(*attend_chain.result)

    qkv, attended, stream_one, rows_two, turned_one, turned_two, stream_sum = call(
        functools.partial(attend_kernel, blocks=links.blocks),
        groups,
        here,
        (
            (rows_one, False),
            (attend_all, True),
            (query_bias.reshape(groups, 1, head_share), True),
            (value_bias.reshape(groups, 1, head_share), True),
            (present, False),
            (stream_zero, False),
            (attend_bias[None], False),
            (gain_two[None], False),
            (shift_two[None], False),
            (column, False),
        ),
        (
            ((groups, 3, rows, head_share), bf16, True),
            ((groups, rows, head_share), bf16, True),
            ((rows, D), f32, False),
            ((rows, D), bf16, False),
            ((D, rows), bf16, False),
            ((D, rows), bf16, False),
            ((2 * count, D), f32, False),
        ),
        flops=2 * rows * D * 4 * D,
    )
    rows_two, stream_sum = sync([expand_chain, contract_chain], rows_two, stream_sum)
    rows_two = sync([expand_chain], rows_two)
    expand_all = links.whole(*expand_chain.result)
    active_sum, slope = call(
        hidden_kernel,
        groups,
        here,
        (
            (rows_two, False),
            (expand_all, True),
            (expand_bias.reshape(groups, 1, hidden_share), True),
            (chooser, False),
            (column, False),
        ),
        (
            ((groups, 2 * count, hidden_share), f32, True),
            ((groups, rows, hidden_share), bf16, True),
        ),
        flops=2 * rows * D * FF,
    )
    active_sum, slope = sync([contract_chain], active_sum, slope)
    active_sum, slope = sync([contract_chain], active_sum, slope)
    vectors_last = (contract_bias[None], gain_last[None], shift_last[None])

    def own_head(operands, scratch):
        return call(
            functools.partial(own_head_kernel, inverse_count=inverse_count),
            1,
            here,
            ((active_sum, False), (stream_sum, False), (facts, False))
            + tuple((value, False) for value in vectors_last + (head_low, head_bias[None]))
            + operands,
            (
                ((8 * count, D + 128), bf16, False),
                ((2 * count, D), f32, False),
                ((groups, 2 * count, hidden_share), f32, False),
            ),
            scratch,
        )

    piece, d_row, d_active_row = links.mixed(own_head, *contract_chain.result)

    pieces_chain = Chain(links.gather(piece))
    turns = ((3, -2), (2, -2))

    def expand_back(turn_order, d_active, *before):
        return call(
            expand_back_kernel,
            pair,
            here,
            (
                (turned_two, False),
                (expand_all, True),
                (slope, True),
                (d_active, True),
            )
            + tuple((value, False) for value in before),
            (
                ((pair, D, hidden_share), bf16, True),
                ((pair, 1, hidden_share), f32, True),
                ((rows, D), f32, False),
            ),
            (((rows, hidden_share), bf16),),
            flops=2 * rows * D * FF,
            turns=turn_order,
        )

    far_grad, expand_far, d_rows_two = expand_back(turns[0], d_active_row)
    far_grad, d_rows_two = sync([pieces_chain], far_grad, d_rows_two)
    expand_sum = Chain(links.reduce(far_grad))
    near_grad, expand_near, d_rows_two = expand_back(turns[1], d_active_row, d_rows_two)
    d_rows_two = sync([pieces_chain, (expand_sum, near_grad)], d_rows_two)
    d_stream, d_attend_low, d_turned, vector_two = call(
        functools.partial(between_kernel, blocks=links.blocks),
        1,
        here,
        (
            (d_rows_two, False),
            (d_row, False),
            (column, False),
            (stream_one, False),
            (gain_two[None], False),
        ),
        (
            ((rows, D), f32, False),
            ((rows, D), bf16, False),
            ((D, rows), bf16, False),
            ((8, D), f32, False),
        ),
    )

    def attend_back(turn_order, *before):
        return call(
            attend_back_kernel,
            pair,
            here,
            (
                (turned_one, False),
                (attend_all, True),
                (qkv, True),
                (attended, True),
                (column, False),
                (d_attend_low, False),
                (d_turned, False),
            )
            + tuple((value, False) for value in before),
            (
                ((pair, D, D), bf16, True),
                ((pair, 2 * count, head_share), f32, True),
                ((rows, D), f32, False),
            ),
            (((rows, 3 * head_share), bf16),),
            flops=2 * rows * D * 4 * D,
            turns=turn_order,
        )

    far_grad, heads_far, d_rows_one = attend_back(turns[0])
    far_grad, d_rows_one = sync([pieces_chain, expand_sum], far_grad, d_rows_one)
    attend_sum = Chain(links.reduce(far_grad))
    near_grad, heads_near, d_rows_one = attend_back(turns[1], d_rows_one)
    d_rows_one = sync([pieces_chain, expand_sum, (attend_sum, near_grad)], d_rows_one)
    spread = data_size * model_size
    unit = 16 * spread if spread <= 32 else spread
    both_rows = -(-(D + padded) // unit) * unit
    both, vector_one = call(
        stem_back_kernel,
        1,
        here,
        (
            (d_rows_one, False),
            (d_stream, False),
            (stream_zero, False),
            (gain_one[None], False),
            (pixels, False),
        ),
        (((both_rows, D), bf16, False), ((8 + padded, D), f32, False)),
        flops=2 * rows * D * D,
    )
    pieces = links.whole(*pieces_chain.result).reshape((-1,) + piece.shape)
    steps = max(1, pieces.shape[0] // 32)
    grad_head, grad_contract, vector_last, vector_head = call(
        functools.partial(all_head_kernel, inverse_count=inverse_count),
        steps,
        here,
        (
            (pieces.reshape((steps, -1) + piece.shape), True),
            (gain_last[None], False),
            (shift_last[None], False),
            (head_low, False),
            (head_bias[None], False),
        ),
        (
            ((D, CLASSES), f32, False),
            ((row_share, hidden_share), f32, False),
            ((8, D), f32, False),
            ((8, CLASSES), f32, False),
        ),
    )
    loss_sum = vector_head[1, 0]
    both, grad_contract, grad_head = sync(
        [attend_sum, expand_sum], both, grad_contract, grad_head
    )
    grad_expand = expand_sum.result
    both_sum = Chain(links.add_large(both))
    grad_expand = sync([attend_sum, both_sum], grad_expand)
    head_new, head_rows_new, head_cols_new = factored_step(
        head_weight, whole_squares[2], grad_head, head_rows, head_cols
    )
    head_new, grad_expand = sync([attend_sum, both_sum], head_new, grad_expand)
    grad_attend = attend_sum.result

    names = dict(data=data_size, groups=groups, share=head_share)
    _, at_group, at_single, lines = layout(data_size, groups)
    (sums,) = call(
        functools.partial(sums_kernel, patch_count=patch_count, **names),
        1,
        here,
        tuple(
            (value, False)
            for value in (
                grad_attend,
                grad_expand,
                grad_contract,
                squares,
                vector_one,
                vector_two,
                expand_far,
                expand_near,
                heads_far,
                heads_near,
            )
        ),
        (((lines, D), f32, False),),
    )
    sums_chain = Chain(links.add(sums))
    for _ in range(5):
        sync([sums_chain, both_sum])
    sums = sums_chain.result
    rows_new, cols_new, update, scalars, square_totals = call(
        functools.partial(renew_kernel, **names),
        1,
        here,
        tuple(
            (value, False)
            for value in (sums, old_rows, old_cols, grad_attend, grad_expand, grad_contract)
        ),
        (
            (old_rows.shape, f32, False),
            (old_cols.shape, f32, False),
            ((3, row_share, D), f32, False),
            ((8, 128), f32, False),
            ((8, 128), f32, False),
        ),
    )
    scalars_chain = Chain(links.add(scalars))
    sync([scalars_chain, both_sum])
    both = both_sum.result.astype(f32)
    grad_table = jnp.concatenate([both[D + patch_count : D + slots], both[D : D + patch_count]])
    stem_new, stem_rows_new, stem_cols_new = factored_step(
        stem_weight, whole_squares[0], both[:D], stem_rows, stem_cols
    )
    sync([scalars_chain])
    stem_new = sync([scalars_chain], stem_new)
    table_new, table_rows_new, table_cols_new = factored_step(
        position_table, whole_squares[1], grad_table, table_rows, table_cols
    )
    table_new = sync([scalars_chain], table_new)

    def of_groups(index, start=0, stop=D):
        spot = at_group + index * groups
        return sums[spot : spot + groups, start:stop].reshape(-1)

    single = sums[at_single : at_single + 6]
    grad_vector = jnp.concatenate(
        [
            single[0],
            single[1],
            single[2],
            of_groups(4, 0, head_share),
            of_groups(4, 256, 256 + head_share),
            single[3],
            single[4],
            single[5],
            of_groups(3),
            vector_last[0],
            vector_last[1],
            vector_last[2],
            vector_head[0],
        ]
    )
    vectors_new, second_new = vector_step(vectors, whole_squares[3], grad_vector, vector_second)
    vectors_new = sync([scalars_chain], vectors_new)
    block = call(
        functools.partial(step_kernel, sizes=(3 * D * D, D * D, D * FF, FF * D)),
        1,
        here,
        tuple(
            (value, False)
            for value in (
                update,
                scalars_chain.result,
                square_totals,
                attend_own,
                expand,
                contract_own,
            )
        ),
        tuple(
            (shape, kind, False)
            for shape in (
                (3, row_share, head_share),
                (head_share, row_share),
                (row_share, hidden_share),
                (hidden_share, row_share),
            )
            for kind in (f32, bf16)
        ),
    )
    in_new, in_copy, out_new, out_copy, expand_new, expand_copy, contract_new, contract_copy = block

    def of_blocks(index):
        return rows_new[:, index * 128 : index * 128 + row_share].reshape(-1)

    in_cols_new = cols_new[:groups, :in_share].reshape(groups, 3, head_share).swapaxes(0, 1)
    return (
        loss_sum,
        stem_new,
        stem_rows_new,
        stem_cols_new,
        table_new,
        table_rows_new,
        table_cols_new,
        in_new.swapaxes(0, 1),
        in_copy.swapaxes(0, 1),
        of_blocks(0),
        in_cols_new.reshape(3, D),
        out_new,
        out_copy,
        cols_new[:groups, in_share:].reshape(-1),
        of_blocks(1),
        expand_new,
        expand_copy,
        of_blocks(2),
        cols_new[groups : 2 * groups].reshape(-1),
        contract_new,
        contract_copy,
        cols_new[2 * groups :].reshape(-1),
        of_blocks(3),
        head_new,
        head_rows_new,
        head_cols_new,
        vectors_new,
        grad_vector,
        second_new,
    )


def solution(mesh):
    placed = (
        P(ALL, None, None),
        P(ALL, None),
        P(ALL),
        P(),
        P(),
        P("dp", None, "mp"),
        P("mp", "dp"),
        P("dp", "mp"),
        P("mp", "dp"),
    ) + (P(),) * 17
    block = (P("dp", None, "mp"), P("mp", "dp"), P("dp", "mp"), P("mp", "dp"))
    given = [P()] * 7
    for spec in block:
        given += [spec, spec, P(), P()]
    given += [P()] * 6
    return jax.shard_map(
        local, mesh=mesh, in_specs=placed, out_specs=tuple(given), check_vma=False
    )
```

```python
import functools

import jax
import jax.numpy as jnp
from jax import lax
from jax.experimental import pallas as pl
from jax.experimental.pallas import tpu as pltpu
from jax.sharding import PartitionSpec as P

D = 768
HEAD_DIM = 64
FF = 3072
CLASSES = 1000

eps_norm = 1e-06
eps_one = 1e-30
eps_two = 0.001
decay_rate = 0.5
clip_level = 0.3
step_rate = 1.0
smoothing = 0.1

ALL = ("dp", "mp")
f32 = jnp.float32
bf16 = jnp.bfloat16


def after(value, *others):
    return lax.optimization_barrier((value,) + others)[0]


class Chain:
    def __init__(self, stages):
        self.stages = stages
        self.result = None
        self.sent, self.flight = next(stages)

    def advance(self, arrived):
        try:
            self.sent, self.flight = self.stages.send(arrived)
        except StopIteration as end:
            self.sent, self.flight, self.result = (), (), end.value


def sync(chains, *values):
    chains = [chain if isinstance(chain, tuple) else (chain,) for chain in chains]
    flights = [(chain[0].flight,) + chain[1:] for chain in chains]
    flights, values = lax.optimization_barrier((flights, values))
    for chain, flight in zip(chains, flights):
        chain[0].advance(flight if len(flight) > 1 else flight[0])
    return values[0] if len(values) == 1 else values


class Plain:
    blocks = None

    def __init__(self, rows, cols):
        self.rows, self.cols = rows, cols
        self.place = jnp.stack(
            [jnp.zeros((), jnp.int32)] * 4
            + [lax.axis_index("dp"), lax.axis_index("mp"), jnp.zeros((), jnp.int32)]
            + [jnp.full((), 4, jnp.int32)]
        ).astype(jnp.int32)

    def gather(self, piece):
        full = lax.all_gather(piece, ALL, axis=0)
        full = full.reshape((self.rows, self.cols) + piece.shape).swapaxes(0, 1)
        for _ in range(4):
            yield (), ()
        return (full.reshape(self.cols, self.rows * piece.shape[0], piece.shape[1]),)

    def whole(self, full):
        return full

    def reduce(self, far):
        _, near = yield (), ()
        grads = jnp.stack([near[1], far[1], near[0], far[0]])
        grads = grads.reshape(self.cols, self.rows, -1, grads.shape[2])
        grads = grads.swapaxes(0, 1).reshape((-1,) + grads.shape[2:])
        total = lax.psum_scatter(grads, ALL, scatter_dimension=0).astype(f32)
        for _ in range(3):
            total = yield (), total
        return total

    def add(self, values):
        values = lax.psum(values, ALL)
        for _ in range(5):
            values = yield (), values
        return values

    def add_large(self, far, near):
        values = lax.psum((near, far), ALL)
        for _ in range(8):
            values = yield (), values
        return values


def group_copies(place_ref, piece_refs, full_ref, sems, distance):
    near_ref, far_ref = piece_refs[2:] if distance % 2 else piece_refs[:2]
    flip = distance // 2
    x = place_ref[1]
    source = far_ref if flip else near_ref
    along_y = [
        pltpu.make_async_copy(source.at[0], full_ref.at[:, x], sems.at[0]),
        pltpu.make_async_copy(source.at[1], full_ref.at[:, 1 - x], sems.at[1]),
    ]
    along_x = [
        pltpu.make_async_copy(near_ref.at[flip], full_ref.at[:, x], sems.at[0]),
        pltpu.make_async_copy(far_ref.at[flip], full_ref.at[:, 1 - x], sems.at[1]),
    ]
    return along_y, along_x


def each_copy(place_ref, distance, choices, act):
    owner = place_ref[3] ^ (distance % 2)
    for core in range(2):

        @pl.when(owner == core)
        def _(copies=choices[core]):
            for copy in copies:
                act(copy)


def start_copy(copy):
    copy.start()


def wait_copy(copy):
    copy.wait()


def column_kernel(place_ref, *refs):
    *piece_refs, column_ref = refs
    for step, ref in enumerate(piece_refs):
        column_ref[0, lax.rem(place_ref[0] + step, len(piece_refs))] = ref[...]


class Grid:
    deep, devices, blocks = 4, 32, 8

    def __init__(self):
        dp, mp = lax.axis_index("dp"), lax.axis_index("mp")
        self.z, self.x, self.y, self.core = dp // 2, dp % 2, mp // 2, mp % 2
        self.at_first = jnp.where(self.core == 0, self.y, self.x)
        self.at_second = jnp.where(self.core == 0, self.x, self.y)
        chunk = self.core * 4 + self.at_first * 2 + self.at_second
        other_chunk = (1 - self.core) * 4 + self.at_second * 2 + self.at_first
        self.place = jnp.stack([self.z, self.x, self.y, self.core, dp, mp, chunk, other_chunk])
        self.place = self.place.astype(jnp.int32)
        self.other = self.pairs(lambda z, x, y, c: (z, x, y, 1 - c))
        self.first = self.pairs(lambda z, x, y, c: (z, x ^ c, y ^ (1 - c), c))
        self.second = self.pairs(lambda z, x, y, c: (z, x ^ (1 - c), y ^ c, c))
        self.along_x = self.pairs(lambda z, x, y, c: (z, 1 - x, y, c))
        self.along_y = self.pairs(lambda z, x, y, c: (z, x, 1 - y, c))
        self.up = [self.pairs(lambda z, x, y, c, s=s: ((z + s) % 4, x, y, c)) for s in range(4)]
        self.flip_z = [self.pairs(lambda z, x, y, c, s=s: (z ^ s, x, y, c)) for s in range(4)]

    def pairs(self, move):
        table = []
        for index in range(self.devices):
            z, x, y, c = move(index // 8, index // 4 % 2, index // 2 % 2, index % 2)
            table.append((index, ((z * 2 + x) * 2 + y) * 2 + c))
        return table

    @staticmethod
    def send(values, table):
        return lax.ppermute(values, ALL, table)

    def gather(self, piece):
        got = yield piece, [self.send(piece, self.up[-s]) for s in (1, 2, 3)]
        column = pl.pallas_call(
            column_kernel,
            in_specs=[pl.BlockSpec(memory_space=pltpu.SMEM)]
            + [pl.BlockSpec(memory_space=pltpu.VMEM)] * self.deep,
            out_specs=pl.BlockSpec(memory_space=pltpu.VMEM),
            out_shape=jax.ShapeDtypeStruct((1, self.deep) + piece.shape, piece.dtype),
        )(self.place, piece, *got)
        got = yield column, self.send(column, self.second)
        pair = jnp.concatenate([column, got])
        rest, theirs = yield pair, (self.send(pair, self.first), self.send(pair, self.other))
        rest_theirs = yield rest, self.send(rest, self.other)
        return pair, rest, theirs, rest_theirs

    def whole(self, *pieces):
        blocks, (r, c) = self.blocks, pieces[0].shape[2:]

        def body(place_ref, *refs):
            full_ref, sems = refs[-2:]
            own = place_ref[2] * 2 + place_ref[3]
            groups = [
                (i, group_copies(place_ref, refs[:4], full_ref.at[own ^ i], sems.at[i], i))
                for i in range(4)
            ]
            for act in (start_copy, wait_copy):
                for distance, choices in groups:
                    each_copy(place_ref, distance, choices, act)

        full = pl.pallas_call(
            body,
            in_specs=[pl.BlockSpec(memory_space=pltpu.SMEM)]
            + [pl.BlockSpec(memory_space=pl.ANY)] * 4,
            out_specs=pl.BlockSpec(memory_space=pltpu.VMEM),
            out_shape=jax.ShapeDtypeStruct((4, self.deep, 2, r, c), pieces[0].dtype),
            scratch_shapes=[pltpu.SemaphoreType.DMA((4, 2))],
            compiler_params=pltpu.CompilerParams(vmem_limit_bytes=16 * 1024 * 1024),
        )(self.place, *pieces)
        return full.reshape(4, blocks * r, c)

    def reduce(self, far):
        theirs, near = yield far, self.send(far, self.other)
        shape = (4, self.deep, near.shape[1] // self.blocks, near.shape[2])
        near, theirs = near.reshape(shape), theirs.reshape(shape)

        def chip(index):
            return (
                lax.dynamic_index_in_dim(near, index, 0, keepdims=False).astype(f32)
                + lax.dynamic_index_in_dim(theirs, index, 0, keepdims=False).astype(f32)
            )

        sent = jnp.stack([chip(0), chip(1 + self.core)]).astype(bf16)
        got = yield sent, self.send(sent, self.first)
        away = (chip(2 - self.core) + got[0].astype(f32)).astype(bf16)
        came = yield away, self.send(away, self.second)
        column = chip(3) + got[1].astype(f32) + came.astype(f32)
        low = column.astype(bf16)
        total = column[0]
        for part in (yield low, [self.send(low[s], self.up[s]) for s in (1, 2, 3)]):
            total = total + part.astype(f32)
        return total

    def add(self, values):
        for table in (self.other, self.along_y, self.along_x, self.flip_z[1], self.flip_z[2]):
            values = values + (yield values, self.send(values, table))
        return values

    def add_large(self, far, near):
        values = near.astype(f32) + (yield far, self.send(far, self.other)).astype(f32)
        for table in (self.first, self.second):
            half = values.shape[0] // 2
            sent = values[half:].astype(bf16)
            got = yield sent, self.send(sent, table)
            values = values[:half] + got.astype(f32)
        pile = values.astype(bf16)
        for table in (self.flip_z[1], self.flip_z[2]):
            got = yield pile, self.send(pile, table)
            pile = (pile.astype(f32) + got.astype(f32)).astype(bf16)
        for table in (self.second, self.first):
            pile = jnp.concatenate([pile, (yield pile, self.send(pile, table))])
        return pile, (yield pile, self.send(pile, self.other))


def normal_parts(values):
    centred = values - jnp.mean(values, -1, keepdims=True)
    inverse = lax.rsqrt(jnp.mean(centred * centred, -1, keepdims=True) + eps_norm)
    return centred * inverse, inverse


def pull_normal(values, gain, grads):
    hat, inverse = normal_parts(values)
    scaled = grads * gain
    mean_one = jnp.mean(scaled, -1, keepdims=True)
    mean_two = jnp.mean(scaled * hat, -1, keepdims=True)
    below = (scaled - mean_one - hat * mean_two) * inverse
    return below, jnp.sum(grads * hat, 0, keepdims=True), jnp.sum(grads, 0, keepdims=True)


STEM_BIAS, GAIN_ONE, SHIFT_ONE, QUERY_BIAS, VALUE_BIAS, ATTEND_BIAS, GAIN_TWO, SHIFT_TWO = range(8)
EXPAND_BIAS, CONTRACT_BIAS, GAIN_LAST, SHIFT_LAST, HEAD_BIAS = 8, 12, 13, 14, 15


def line(vectors_ref, index):
    return vectors_ref[index : index + 1, :]


def share_of(vectors_ref, index, group, share):
    result = vectors_ref[index : index + 1, :share]
    for other in range(1, vectors_ref.shape[1] // share):
        part = vectors_ref[index : index + 1, other * share : (other + 1) * share]
        result = jnp.where(group == other, part, result)
    return result


def own_group(place_ref, order):
    step = pl.program_id(0)
    distance = order[0]
    for index, value in enumerate(order[1:], 1):
        distance = jnp.where(step == index, value, distance)
    return (place_ref[2] * 2 + place_ref[3]) ^ distance


def dot(left, right, left_dim=1, right_dim=0):
    return lax.dot_general(
        left, right, (((left_dim,), (right_dim,)), ((), ())), preferred_element_type=f32
    )


def put(count, index, line):
    spot = lax.broadcasted_iota(jnp.int32, (count, 1), 0)
    return jnp.where(spot == index, line, 0.0)


def pick(lines, index):
    spot = lax.broadcasted_iota(jnp.int32, (lines.shape[0], 1), 0)
    return jnp.sum(jnp.where(spot == index, lines, 0.0), 0, keepdims=True)


def upright(row):
    n = row.shape[1]
    more = -n % 128
    if more:
        row = jnp.concatenate([row, jnp.zeros((1, more), f32)], 1)
    return jnp.broadcast_to(row, (128, n + more)).T[:n, 0:1]


def lying(column):
    n = column.shape[0]
    wide = jnp.broadcast_to(column, (n, 128))
    more = -n % 128
    if more:
        wide = jnp.concatenate([wide, jnp.zeros((more, 128), f32)])
    return wide.T[0:1, :n]


def probabilities(query, key, visible):
    scores = dot(query, key, 1, 1) * HEAD_DIM ** (-0.5)
    scores = jnp.where(visible, scores, -1e30)
    raised = jnp.exp(scores - jnp.max(scores, -1, keepdims=True))
    return raised * (1.0 / jnp.sum(raised, -1, keepdims=True))


def head_masks(share):
    lane = lax.broadcasted_iota(jnp.int32, (1, share), 1) // HEAD_DIM
    return [lane == head for head in range(share // HEAD_DIM)]


def stacked(rows, masks):
    return jnp.concatenate([jnp.where(mask, rows, jnp.zeros((), rows.dtype)) for mask in masks])


def unstacked(every, masks):
    size = every.shape[0] // len(masks)
    result = every[:size]
    for head, mask in enumerate(masks[1:], 1):
        result = jnp.where(mask, every[head * size : (head + 1) * size], result)
    return result


def turn(place_ref, values, result_ref, blocks):
    turned = values.T
    if blocks is None:
        result_ref[...] = turned
        return
    size, deep = turned.shape[0] // blocks, blocks // 2
    for block in range(blocks):
        level = lax.rem(block // 2 - place_ref[0] + deep, deep)
        spot = (1 - (block % 2 ^ place_ref[1])) * deep + level
        rows = pl.ds(pl.multiple_of(spot * size, size), size)
        result_ref[rows, :] = turned[block * size : (block + 1) * size, :]


def pieces_kernel(
    place_ref,
    in_ref,
    out_ref,
    expand_ref,
    contract_ref,
    own_ref,
    attend_low_ref,
    expand_low_ref,
    contract_low_ref,
    square_ref,
):
    share = out_ref.shape[0]
    lane = lax.broadcasted_iota(jnp.int32, (1, 128), 1)
    for part in range(3):
        own_ref[:, part * share : (part + 1) * share] = in_ref[part]
    own_ref[:, 3 * share :] = out_ref[...].T
    attend_low_ref[...] = own_ref[...].astype(bf16)
    expand_low_ref[...] = expand_ref[...].astype(bf16)
    contract_low_ref[...] = contract_ref[...].astype(bf16)
    totals = jnp.zeros((1, 128), f32)
    for index, ref in enumerate((in_ref, out_ref, expand_ref, contract_ref)):
        values = ref[...]
        total = jnp.sum(values * values, keepdims=True).reshape(1, 1)
        totals = jnp.where(lane == index, total, totals)
    square_ref[...] = totals


def stem_kernel(
    place_ref,
    labels_ref,
    pixels_ref,
    stem_ref,
    table_ref,
    vectors_ref,
    mask_ref,
    stream_ref,
    rows_ref,
    present_ref,
    column_ref,
    facts_ref,
):
    count, patch_count = mask_ref.shape
    padded = present_ref.shape[1]
    low = stem_ref[...].astype(bf16)
    slot = lax.broadcasted_iota(jnp.int32, (padded, 1), 0)
    table = table_ref[...] + jnp.where(slot < patch_count, line(vectors_ref, STEM_BIAS), 0.0)
    for image in range(count):
        span = slice(image * padded, (image + 1) * padded)
        stream = dot(pixels_ref[span, :], low) + table
        stream_ref[span, :] = stream
        hat, _ = normal_parts(stream)
        normed = hat * line(vectors_ref, GAIN_ONE) + line(vectors_ref, SHIFT_ONE)
        rows_ref[span, :] = normed.astype(bf16)
    lane = lax.broadcasted_iota(jnp.int32, (count, padded), 1)
    present_ref[...] = jnp.where(lane == patch_count, 1.0, 0.0)
    present_ref[:, :patch_count] = mask_ref[...].astype(f32)
    lane = lax.broadcasted_iota(jnp.int32, (1, 128), 1)
    for image in range(count):
        present = present_ref[image : image + 1, :]
        column_ref[image * padded : (image + 1) * padded, :] = upright(present)
        kept = jnp.sum(present, 1, keepdims=True)
        label = labels_ref[image].astype(f32)
        fact = jnp.where(lane == 0, kept, jnp.where(lane == 1, label, 0.0))
        facts_ref[image : image + 1, :] = fact
        facts_ref[count + image : count + image + 1, :] = fact


def attend_kernel(
    place_ref,
    weight,
    rows_ref,
    vectors_ref,
    present_ref,
    stream_ref,
    column_ref,
    qkv_ref,
    attended_ref,
    stream_out_ref,
    rows_out_ref,
    turned_one_ref,
    turned_two_ref,
    sum_ref,
    *,
    blocks,
    order,
):
    step = pl.program_id(0)
    count, padded = present_ref.shape
    share = attended_ref.shape[2]

    @pl.when(step == 0)
    def _():
        turn(place_ref, rows_ref[...], turned_one_ref, blocks)

    group = own_group(place_ref, order)
    projected = dot(rows_ref[...], weight(0, 3 * share))
    query = projected[:, :share] + share_of(vectors_ref, QUERY_BIAS, group, share)
    query = query.astype(bf16)
    key = projected[:, share : 2 * share].astype(bf16)
    value = projected[:, 2 * share :] + share_of(vectors_ref, VALUE_BIAS, group, share)
    value = value.astype(bf16)
    qkv_ref[0, 0] = query
    qkv_ref[0, 1] = key
    qkv_ref[0, 2] = value
    masks = head_masks(share)
    for image in range(count):
        span = slice(image * padded, (image + 1) * padded)
        visible = present_ref[image : image + 1, :] > 0.5
        low = probabilities(stacked(query[span], masks), key[span], visible).astype(bf16)
        every = dot(low, value[span])
        attended_ref[0, span, :] = unstacked(every, masks).astype(bf16)
    part = dot(attended_ref[0], weight(3 * share, 4 * share), 1, 1)

    @pl.when(step == 0)
    def _():
        stream_out_ref[...] = stream_ref[...] + line(vectors_ref, ATTEND_BIAS) + part

    @pl.when(step > 0)
    def _():
        stream_out_ref[...] += part

    @pl.when(step == pl.num_programs(0) - 1)
    def _():
        hat, _ = normal_parts(stream_out_ref[...])
        rows_two = hat * line(vectors_ref, GAIN_TWO) + line(vectors_ref, SHIFT_TWO)
        rows_two = rows_two.astype(bf16)
        rows_out_ref[...] = rows_two
        turn(place_ref, rows_two, turned_two_ref, blocks)
        for image in range(count):
            span = slice(image * padded, (image + 1) * padded)
            total = jnp.sum(stream_out_ref[span, :] * column_ref[span, :], 0, keepdims=True)
            sum_ref[image : image + 1, :] = total
            sum_ref[image + count : image + count + 1, :] = total


def hidden_kernel(
    place_ref,
    weight,
    rows_ref,
    vectors_ref,
    present_ref,
    column_ref,
    sum_ref,
    slope_ref,
    *,
    order,
):
    bias = pick(vectors_ref[EXPAND_BIAS : EXPAND_BIAS + len(order), :], own_group(place_ref, order))
    hidden = dot(rows_ref[...], weight()) + bias
    first, second = 0.7978845608028654, 0.044715
    square = hidden * hidden
    half = 0.5 + 0.5 * jnp.tanh(hidden * (first + first * second * square))
    active = (hidden * half).astype(bf16)
    count, padded = present_ref.shape
    row = lax.broadcasted_iota(jnp.int32, (2 * count, 1), 0)
    sums = jnp.zeros(sum_ref.shape[1:], f32)
    for image in range(count):
        chooser = jnp.broadcast_to(present_ref[image : image + 1, :], (2 * count, padded))
        total = dot(chooser.astype(bf16), active[image * padded : (image + 1) * padded])
        sums = jnp.where(row % count == image, total, sums)
    sum_ref[0] = sums
    steep = hidden * (2.0 * first + 6.0 * first * second * square)
    slope = half * (1.0 + steep * (1.0 - half))
    slope_ref[0] = (slope * column_ref[...]).astype(bf16)


def expand_back_kernel(
    place_ref,
    weight,
    turned_ref,
    slope_ref,
    d_active_ref,
    far_ref,
    near_ref,
    bias_ref,
    d_rows_ref,
    d_hidden_low,
):
    step = pl.program_id(0)
    count = d_active_ref.shape[1] // 2
    padded = slope_ref.shape[1] // count
    bias = jnp.zeros((1, d_hidden_low.shape[1]), f32)
    for image in range(count):
        span = slice(image * padded, (image + 1) * padded)
        d_hidden = slope_ref[0, span, :].astype(f32) * d_active_ref[0, image : image + 1, :]
        bias = bias + jnp.sum(d_hidden, 0, keepdims=True)
        d_hidden_low[span, :] = d_hidden.astype(bf16)
    bias_ref[0] = bias
    grad = dot(turned_ref[...], d_hidden_low[...]).astype(bf16)
    half = pl.num_programs(0) // 2

    @pl.when(step < half)
    def _():
        far_ref[0] = grad

    @pl.when(step >= half)
    def _():
        near_ref[0] = grad

    part = dot(d_hidden_low[...], weight(), 1, 1)

    @pl.when(step == 0)
    def _():
        d_rows_ref[...] = part

    @pl.when(step > 0)
    def _():
        d_rows_ref[...] += part


def between_kernel(
    place_ref,
    d_rows_ref,
    d_row_ref,
    column_ref,
    stream_ref,
    vectors_ref,
    d_stream_ref,
    d_low_ref,
    turned_ref,
    vector_ref,
    *,
    blocks,
):
    count = d_row_ref.shape[0] // 2
    padded = stream_ref.shape[0] // count
    gain = line(vectors_ref, GAIN_TWO)
    below, gain, shift = pull_normal(stream_ref[...], gain, d_rows_ref[...])
    vector_ref[1:2, :] = gain
    vector_ref[2:3, :] = shift
    bias = jnp.zeros((1, below.shape[1]), f32)
    for image in range(count):
        span = slice(image * padded, (image + 1) * padded)
        d_stream = below[span] + d_row_ref[image : image + 1, :] * column_ref[span, :]
        bias = bias + jnp.sum(d_stream, 0, keepdims=True)
        d_stream_ref[span, :] = d_stream
        d_low_ref[span, :] = d_stream.astype(bf16)
    vector_ref[0:1, :] = bias
    turn(place_ref, d_low_ref[...], turned_ref, blocks)


def attend_back_kernel(
    place_ref,
    weight,
    turned_ref,
    qkv_ref,
    attended_ref,
    column_ref,
    d_low_ref,
    d_turned_ref,
    *refs,
):
    grad_ref, bias_ref, d_rows_ref, d_projected = refs[-4:]
    step = pl.program_id(0)
    share = attended_ref.shape[2]
    count = bias_ref.shape[1] // 2
    padded = attended_ref.shape[1] // count
    scale = HEAD_DIM ** (-0.5)
    d_attended = dot(d_low_ref[...], weight(3 * share, 4 * share)).astype(bf16)
    masks = head_masks(share)
    for image in range(count):
        span = slice(image * padded, (image + 1) * padded)
        hidden = column_ref[span, :] < 0.5
        query, key, value = (qkv_ref[0, part, span, :] for part in range(3))
        query = query * jnp.asarray(scale, bf16)
        queries = stacked(query, masks)
        d_images = stacked(d_attended[span], masks)
        scores = jnp.where(hidden, -1e30, dot(key, queries, 1, 1))
        raised = jnp.exp(scores - jnp.max(scores, 0, keepdims=True))
        probs = raised * (1.0 / jnp.sum(raised, 0, keepdims=True))
        d_probs = dot(value, d_images, 1, 1)
        inner = jnp.sum(probs * d_probs, 0, keepdims=True)
        d_scores = (probs * (d_probs - inner)).astype(bf16)
        d_value = dot(probs.astype(bf16), d_images)
        d_key = dot(d_scores, queries)
        d_query = unstacked(dot(d_scores, key, 0, 0), masks) * scale
        bias_ref[0, image : image + 1, :] = jnp.sum(d_query, 0, keepdims=True)
        bias_ref[0, count + image : count + image + 1, :] = jnp.sum(d_value, 0, keepdims=True)
        d_projected[span, :share] = d_query.astype(bf16)
        d_projected[span, share : 2 * share] = d_key.astype(bf16)
        d_projected[span, 2 * share :] = d_value.astype(bf16)
    grad_ref[0, :, : 3 * share] = dot(turned_ref[...], d_projected[...]).astype(bf16)
    grad_ref[0, :, 3 * share :] = dot(d_turned_ref[...], attended_ref[0]).astype(bf16)
    part = dot(d_projected[...], weight(0, 3 * share), 1, 1)

    @pl.when(step == 0)
    def _():
        d_rows_ref[...] = part + refs[0][...] if len(refs) > 4 else part

    @pl.when(step > 0)
    def _():
        d_rows_ref[...] += part


def stem_back_kernel(
    place_ref,
    d_rows_ref,
    d_stream_ref,
    stream_ref,
    vectors_ref,
    pixels_ref,
    far_ref,
    near_ref,
    vector_ref,
):
    rows, width = pixels_ref.shape
    gain = line(vectors_ref, GAIN_ONE)
    below, gain, shift = pull_normal(stream_ref[...], gain, d_rows_ref[...])
    vector_ref[0:1, :] = gain
    vector_ref[1:2, :] = shift
    below = below + d_stream_ref[...]
    slots = vector_ref.shape[0] - 8
    table = below[:slots]
    for image in range(1, rows // slots):
        table = table + below[image * slots : (image + 1) * slots]
    vector_ref[8:, :] = table
    stem = dot(pixels_ref[...].T, below.astype(bf16)).astype(bf16)
    half, size, columns = near_ref.shape
    empty = jnp.zeros((2 * half * size - width - slots, columns), bf16)
    whole = jnp.concatenate([stem, table.astype(bf16), empty])
    for chunk in range(2 * half):
        near, far = place_ref[6] ^ chunk, place_ref[7] ^ chunk

        @pl.when(near < half)
        def _(chunk=chunk, near=near):
            near_ref[near] = whole[chunk * size : (chunk + 1) * size]

        @pl.when(far < half)
        def _(chunk=chunk, far=far):
            far_ref[far] = whole[chunk * size : (chunk + 1) * size]


def head_vectors(vectors_ref):
    rest = CLASSES - vectors_ref.shape[1]
    bias = jnp.concatenate(
        [line(vectors_ref, HEAD_BIAS), vectors_ref[HEAD_BIAS + 1 : HEAD_BIAS + 2, :rest]], 1
    )
    return line(vectors_ref, GAIN_LAST), line(vectors_ref, SHIFT_LAST), bias


def classify(pooled, labels, head, gain, shift, bias, inverse_count):
    hat, inverse = normal_parts(pooled)
    low = (hat * gain + shift).astype(bf16)
    logits = dot(low, head, 1, 1) + bias
    logits = logits - jnp.max(logits, -1, keepdims=True)
    raised = jnp.exp(logits)
    total = jnp.sum(raised, -1, keepdims=True)
    lane = lax.broadcasted_iota(jnp.int32, logits.shape, 1)
    target = jnp.where(lane == labels.astype(jnp.int32), 1.0 - smoothing, 0.0) + smoothing / CLASSES
    score = jnp.sum(target * (logits - jnp.log(total)), -1, keepdims=True)
    d_logits = (raised * (1.0 / total) - target) * inverse_count
    d_final = dot(d_logits.astype(bf16), head)
    scaled = d_final * gain
    mean_one = jnp.mean(scaled, -1, keepdims=True)
    mean_two = jnp.mean(scaled * hat, -1, keepdims=True)
    return score, low, d_logits, d_final, hat, (scaled - mean_one - hat * mean_two) * inverse


def split(values):
    high = values.astype(bf16)
    return high, (values - high.astype(f32)).astype(bf16)


def own_head_kernel(
    place_ref,
    active_ref,
    sum_ref,
    facts_ref,
    vectors_ref,
    head_ref,
    *refs,
    inverse_count,
):
    groups, twice, width = active_ref.shape
    rows = sum_ref.shape[1]
    if len(refs) == 4:
        full_ref, piece_ref, d_row_ref, d_active_ref = refs
        chosen = []
    else:
        piece_ref, d_row_ref, d_active_ref, full_ref, sems = refs[4:]
        chosen = [
            (r, group_copies(place_ref, refs[:4], full_ref.at[r], sems.at[r], r))
            for r in range(groups)
        ]
    for distance, choices in chosen:
        each_copy(place_ref, distance, choices, start_copy)
    mixed = jnp.zeros((2 * twice, rows), f32)
    for group in range(groups):
        for distance, choices in chosen[group : group + 1]:
            each_copy(place_ref, distance, choices, wait_copy)
        weight = full_ref[group].reshape(rows, width)
        mixed = mixed + dot(jnp.concatenate(split(active_ref[group])), weight, 1, 1)
    mixed = mixed[:twice] + mixed[twice:]
    kept, labels = facts_ref[:, 0:1], facts_ref[:, 1:2]
    pooled = (sum_ref[...] + mixed) / kept + line(vectors_ref, CONTRACT_BIAS)
    d_pooled = classify(
        pooled, labels, head_ref[...], *head_vectors(vectors_ref), inverse_count
    )[-1]
    d_row = d_pooled / kept
    d_row_ref[...] = d_row
    d_row_low = d_row.astype(bf16)
    first = lax.broadcasted_iota(jnp.int32, (twice, 1), 0) < twice // 2
    for group in range(groups):
        d_active_ref[group] = dot(d_row_low, full_ref[group].reshape(rows, width))
    for part, (pool, fact) in enumerate(zip(split(pooled), split(facts_ref[...]))):
        piece_ref[part * twice : (part + 1) * twice, :rows] = pool
        piece_ref[part * twice : (part + 1) * twice, rows:] = fact
    own = place_ref[2] * 2 + place_ref[3]
    for half in range(groups // 2):
        sums = jnp.where(first, active_ref[own ^ (2 * half)], active_ref[own ^ (2 * half + 1)])
        span = slice((2 + half) * twice, (3 + half) * twice)
        piece_ref[span, :rows] = sums.astype(bf16)
        piece_ref[span, rows:] = jnp.zeros((twice, piece_ref.shape[1] - rows), bf16)


def all_head_kernel(
    place_ref,
    pieces_ref,
    vectors_ref,
    head_ref,
    weight_ref,
    old_rows_ref,
    old_cols_ref,
    new_ref,
    new_rows_ref,
    new_cols_ref,
    contract_ref,
    vector_ref,
    bias_ref,
    grad_ref,
    *,
    inverse_count,
):
    pieces = pieces_ref[0].astype(f32)
    count, rows = pieces.shape[0], vectors_ref.shape[1]
    twice = pieces.shape[1] // 4

    def part(index):
        return pieces[:, index * twice : (index + 1) * twice].reshape(count * twice, -1)

    lines = part(0) + part(1)
    pooled, kept, labels = lines[:, :rows], lines[:, rows : rows + 1], lines[:, rows + 1 : rows + 2]
    score, low, d_logits, d_final, hat, d_pooled = classify(
        pooled, labels, head_ref[...], *head_vectors(vectors_ref), inverse_count
    )
    half = lax.broadcasted_iota(jnp.int32, (count * twice, 1), 0) % twice // (twice // 2)
    once = half == 0
    d_logits = jnp.where(once, d_logits, 0.0)
    own = place_ref[5]
    active = jnp.where(own // 2 == 0, part(2)[:, :rows], part(3)[:, :rows]).astype(bf16)
    d_row = jnp.where(half == own % 2, d_pooled / kept, 0.0).astype(bf16)
    share = contract_ref.shape[0]
    place = lax.broadcasted_iota(jnp.int32, (rows, share), 0)
    lane = lax.broadcasted_iota(jnp.int32, (rows, share), 1)
    chooser = (place == lane + place_ref[4] * share).astype(f32).astype(bf16)
    d_row = dot(d_row, chooser).astype(bf16)

    def total(values):
        return jnp.sum(jnp.where(once, values, 0.0), 0, keepdims=True)

    results = (
        (grad_ref, slice(None), dot(d_logits.astype(bf16), low, 0, 0)),
        (contract_ref, slice(None), dot(d_row, active, 0, 0)),
        (vector_ref, slice(0, 1), total(d_pooled)),
        (vector_ref, slice(1, 2), total(d_final * hat)),
        (vector_ref, slice(2, 3), total(d_final)),
        (bias_ref, slice(0, 1), jnp.sum(d_logits, 0, keepdims=True)),
        (bias_ref, slice(1, 2), -total(score) + jnp.zeros((1, bias_ref.shape[1]), f32)),
    )
    for ref, span, value in results:

        @pl.when(pl.program_id(0) == 0)
        def _(ref=ref, span=span, value=value):
            ref[span, :] = value

        @pl.when(pl.program_id(0) > 0)
        def _(ref=ref, span=span, value=value):
            ref[span, :] += value

    @pl.when(pl.program_id(0) == pl.num_programs(0) - 1)
    def _():
        new_ref[...], new_cols_ref[...], new_rows_ref[...] = factored(
            weight_ref[...], grad_ref[...], old_cols_ref[...], old_rows_ref[...], True
        )


def factored(weight, grad, down_old, across_old, turned, valid=None, count=None):
    down_old = upright(down_old)
    squared = grad * grad + eps_one
    n, m = grad.shape
    if valid is not None:
        squared = jnp.where(valid, squared, 0.0)
        n = count
    down_new = decay_rate * down_old + (1.0 - decay_rate) * (
        jnp.sum(squared, 1, keepdims=True) / m
    )
    across_new = decay_rate * across_old + (1.0 - decay_rate) * (
        jnp.sum(squared, 0, keepdims=True) / n
    )
    if turned:
        mean = jnp.sum(across_new, keepdims=True) / m
    else:
        mean = jnp.sum(down_new, keepdims=True) / n
    divisor = down_new if valid is None else jnp.where(valid, down_new, 1.0)
    update = grad * lax.rsqrt(divisor * across_new / mean)
    size = n * m
    clip = jnp.sqrt(jnp.sum(update * update, keepdims=True) / size) / clip_level
    magnitude = jnp.sqrt(jnp.sum(weight * weight, keepdims=True) / size)
    scale = step_rate * jnp.maximum(eps_two, magnitude) / jnp.maximum(1.0, clip)
    return weight - scale * update, lying(down_new), across_new


def stem_step_kernel(
    place_ref,
    near_ref,
    far_ref,
    stem_ref,
    stem_rows_ref,
    stem_cols_ref,
    table_ref,
    table_rows_ref,
    table_cols_ref,
    stem_new_ref,
    stem_rows_new_ref,
    stem_cols_new_ref,
    table_new_ref,
    table_rows_new_ref,
    table_cols_new_ref,
    both_ref,
    *,
    slots,
):
    n, padded = stem_ref.shape[0], table_ref.shape[0]
    half, size = near_ref.shape[:2]
    for chunk in range(2 * half):
        near, far = place_ref[6] ^ chunk, place_ref[7] ^ chunk
        span = slice(chunk * size, (chunk + 1) * size)

        @pl.when(near < half)
        def _(span=span, near=near):
            both_ref[span, :] = near_ref[near]

        @pl.when(far < half)
        def _(span=span, far=far):
            both_ref[span, :] = far_ref[far]

    stem_new_ref[...], stem_rows_new_ref[...], stem_cols_new_ref[...] = factored(
        stem_ref[...], both_ref[:n, :].astype(f32), stem_rows_ref[...], stem_cols_ref[...], False
    )
    valid = lax.broadcasted_iota(jnp.int32, (padded, 1), 0) < slots
    table_new_ref[...], table_rows_new_ref[...], table_cols_new_ref[...] = factored(
        table_ref[...],
        both_ref[n : n + padded, :].astype(f32),
        table_rows_ref[...],
        table_cols_ref[...],
        False,
        valid,
        slots,
    )


def layout(data, groups):
    return 0, data, data + 4 * groups, -(-(data + 4 * groups + 6) // 8) * 8


def across(column):
    n = column.shape[0]
    wide = jnp.broadcast_to(column, (n, 128))
    if n < 128:
        wide = jnp.concatenate([wide, jnp.zeros((128 - n, 128), f32)])
    return wide.T[0:1]


def down(row, n):
    return jnp.broadcast_to(row, (128, 128)).T[:n, 0:1]


def sums_kernel(
    place_ref,
    attend_ref,
    expand_ref,
    contract_ref,
    squares_ref,
    vector_one_ref,
    vector_two_ref,
    expand_bias_ref,
    heads_far_ref,
    heads_near_ref,
    sums_ref,
    *,
    data,
    groups,
    share,
    patch_count,
):
    block, group = place_ref[4], place_ref[5]
    own = place_ref[2] * 2 + place_ref[3]
    _, at_group, at_single, _ = layout(data, groups)
    sums_ref[...] = jnp.zeros(sums_ref.shape, f32)
    lane = lax.broadcasted_iota(jnp.int32, (1, attend_ref.shape[1]), 1)
    for index, ref in enumerate((attend_ref, expand_ref, contract_ref)):
        grad = ref[...]
        squared = grad * grad + eps_one
        span = slice(at_group + index * groups, at_group + (index + 1) * groups)
        sums_ref[span, :] = put(groups, group, jnp.sum(squared, 0, keepdims=True))
        if index == 0:
            lines = (
                jnp.sum(jnp.where(lane < 3 * share, squared, 0.0), 1, keepdims=True),
                jnp.sum(jnp.where(lane < 3 * share, 0.0, squared), 1, keepdims=True),
            )
        else:
            lines = (jnp.sum(squared, 1, keepdims=True),)
        for part, line in enumerate(lines):
            spot = (index + (index > 0) + part) * 128
            sums_ref[:data, spot : spot + 128] = put(data, block, across(line))
    sums_ref[:data, 512:640] = put(data, block, squares_ref[...])
    at_group += 3 * groups
    lines = jnp.zeros((groups, expand_bias_ref.shape[2]), f32)
    for distance in range(groups):
        lines = lines + put(groups, own ^ distance, expand_bias_ref[distance])
    sums_ref[at_group : at_group + groups, :] = lines
    count = heads_far_ref.shape[1] // 2
    for part in range(2):
        lines = jnp.zeros((groups, share), f32)
        for ref, order in ((heads_far_ref, (3, 1)), (heads_near_ref, (2, 0))):
            for step, distance in enumerate(order):
                lines = lines + put(
                    groups,
                    own ^ distance,
                    jnp.sum(ref[step][part * count : (part + 1) * count], 0, keepdims=True),
                )
        sums_ref[part * groups : (part + 1) * groups, 3 * share :] = lines
    stem_bias = jnp.sum(vector_one_ref[8 : 8 + patch_count, :], 0, keepdims=True)
    singles = (stem_bias, vector_one_ref[0:2, :], vector_two_ref[0:3, :])
    for line in singles:
        sums_ref[at_single : at_single + line.shape[0], :] = line
        at_single += line.shape[0]


def vector_kernel(
    place_ref,
    sums_ref,
    last_ref,
    head_ref,
    vectors_ref,
    second_ref,
    grad_ref,
    new_ref,
    second_new_ref,
    *,
    data,
    groups,
    share,
    length,
):
    _, at_group, at_single, _ = layout(data, groups)
    width = vectors_ref.shape[1]

    def single(index):
        return sums_ref[at_single + index : at_single + index + 1, :]

    def joined(part):
        lines = sums_ref[part * groups : (part + 1) * groups, 3 * share :]
        return jnp.concatenate([lines[g : g + 1] for g in range(groups)], 1)

    grad_ref[...] = jnp.zeros(grad_ref.shape, f32)
    spot = at_group + 3 * groups
    rest = CLASSES - width
    for index, value in (
        (STEM_BIAS, single(0)),
        (GAIN_ONE, single(1)),
        (SHIFT_ONE, single(2)),
        (QUERY_BIAS, joined(0)),
        (VALUE_BIAS, joined(1)),
        (ATTEND_BIAS, single(3)),
        (GAIN_TWO, single(4)),
        (SHIFT_TWO, single(5)),
        (EXPAND_BIAS, sums_ref[spot : spot + groups, :]),
        (CONTRACT_BIAS, last_ref[0:3, :]),
        (HEAD_BIAS, head_ref[0:1, :width]),
    ):
        grad_ref[index : index + value.shape[0], :] = value
    grad_ref[HEAD_BIAS + 1 : HEAD_BIAS + 2, :rest] = head_ref[0:1, width:]
    grad = grad_ref[...]
    row = lax.broadcasted_iota(jnp.int32, grad.shape, 0)
    lane = lax.broadcasted_iota(jnp.int32, grad.shape, 1)
    valid = row * width + lane < length
    second = decay_rate * second_ref[...] + (1.0 - decay_rate) * (grad * grad + eps_one)
    update = grad * lax.rsqrt(jnp.where(valid, second, 1.0))
    total = jnp.sum(update * update, keepdims=True) / length
    square = jnp.sum(vectors_ref[...] * vectors_ref[...], keepdims=True) / length
    scale = step_rate * jnp.maximum(eps_two, jnp.sqrt(square))
    scale = scale / jnp.maximum(1.0, jnp.sqrt(total) / clip_level)
    new_ref[...] = vectors_ref[...] - scale * update
    second_new_ref[...] = second


def renew_kernel(
    place_ref,
    sums_ref,
    rows_ref,
    cols_ref,
    attend_ref,
    expand_ref,
    contract_ref,
    rows_new_ref,
    cols_new_ref,
    update_ref,
    scalar_ref,
    square_ref,
    *,
    data,
    groups,
    share,
):
    block, group = place_ref[4], place_ref[5]
    size = attend_ref.shape[0]
    width = attend_ref.shape[1]
    _, at_group, _, _ = layout(data, groups)
    length, hidden = data * size, groups * width
    lane = lax.broadcasted_iota(jnp.int32, (1, width), 1)
    first = lane < 3 * share
    spare = lax.broadcasted_iota(jnp.int32, (1, 128), 1) < size
    counts = (3 * length, length, hidden, hidden)
    means = []
    for index, count in enumerate(counts):
        span = slice(index * 128, (index + 1) * 128)
        new = decay_rate * rows_ref[:, span] + (1.0 - decay_rate) * (sums_ref[:data, span] / count)
        rows_new_ref[:, span] = new
        means.append(jnp.sum(jnp.where(spare, new, 0.0), keepdims=True) / length)
    for index, count in enumerate((length, length, length)):
        span = slice(index * groups, (index + 1) * groups)
        lines = sums_ref[at_group + index * groups : at_group + (index + 1) * groups, :]
        new = decay_rate * cols_ref[span, :] + (1.0 - decay_rate) * (lines / count)
        cols_new_ref[span, :] = new
        if index == 0:
            means[1] = jnp.sum(jnp.where(first, 0.0, new), keepdims=True) / length
        if index == 2:
            means[3] = jnp.sum(new, keepdims=True) / hidden
    scalars = jnp.zeros((1, 128), f32)
    place_lane = lax.broadcasted_iota(jnp.int32, (1, 128), 1)
    for index, ref in enumerate((attend_ref, expand_ref, contract_ref)):
        across_row = pick(cols_new_ref[index * groups : (index + 1) * groups, :], group)

        def row(which):
            span = slice(which * 128, (which + 1) * 128)
            return down(pick(rows_new_ref[:, span], block), size)

        if index == 0:
            denominator = jnp.where(
                first, row(0) * across_row / means[0], row(1) * across_row / means[1]
            )
        else:
            denominator = row(index + 1) * across_row / means[index + 1]
        update = ref[...] * lax.rsqrt(denominator)
        update_ref[index] = update
        squared = update * update
        if index == 0:
            totals = (jnp.where(first, squared, 0.0), jnp.where(first, 0.0, squared))
        else:
            totals = (squared,)
        for part, total in enumerate(totals):
            spot = index + (index > 0) + part
            scalars = jnp.where(place_lane == spot, jnp.sum(total, keepdims=True), scalars)
    scalar_ref[...] = jnp.broadcast_to(scalars, scalar_ref.shape)
    squares = jnp.sum(sums_ref[:data, 512:640], 0, keepdims=True)
    square_ref[...] = jnp.broadcast_to(squares, square_ref.shape)


def step_kernel(
    place_ref,
    update_ref,
    scalar_ref,
    square_ref,
    attend_ref,
    expand_ref,
    contract_ref,
    in_ref,
    in_low_ref,
    out_ref,
    out_low_ref,
    expand_new_ref,
    expand_low_ref,
    contract_new_ref,
    contract_low_ref,
    *,
    sizes,
):
    share = in_ref.shape[2]
    scales = []
    for index, size in enumerate(sizes):
        total = scalar_ref[0:1, index : index + 1]
        square = square_ref[0:1, index : index + 1]
        clip = jnp.maximum(1.0, jnp.sqrt(total / size) / clip_level)
        scales.append(step_rate * jnp.maximum(eps_two, jnp.sqrt(square / size)) / clip)
    lane = lax.broadcasted_iota(jnp.int32, (1, attend_ref.shape[1]), 1)
    scale = jnp.where(lane < 3 * share, scales[0], scales[1])
    attend = attend_ref[...] - scale * update_ref[0]
    for part in range(3):
        lines = attend[:, part * share : (part + 1) * share]
        in_ref[part] = lines
        in_low_ref[part] = lines.astype(bf16)
    out = attend[:, 3 * share :].T
    out_ref[...] = out
    out_low_ref[...] = out.astype(bf16)
    expand = expand_ref[...] - scales[2] * update_ref[1]
    expand_new_ref[...] = expand
    expand_low_ref[...] = expand.astype(bf16)
    contract = contract_ref[...] - scales[3] * update_ref[2]
    contract_new_ref[...] = contract
    contract_low_ref[...] = contract.astype(bf16)


def call(
    body, order, place, operands, results, scratch=(), flops=0, weights=None
):
    steps = len(order)
    pieces = weights is not None and len(weights) == 4

    def distance(step):
        at = order[0]
        for index, value in enumerate(order[1:], 1):
            at = jnp.where(step == index, value, at)
        return at

    def spec(shape, mark):
        zeros = (0,) * (len(shape) - 1)
        if mark == "any":
            return pl.BlockSpec(memory_space=pl.ANY)
        if mark == "smem":
            return pl.BlockSpec(memory_space=pltpu.SMEM)
        if mark is False:
            return pl.BlockSpec(shape, lambda g, p: (0,) + zeros)
        if mark is True:
            return pl.BlockSpec(
                (1,) + shape[1:], lambda g, p: ((p[2] * 2 + p[3]) ^ distance(g),) + zeros
            )
        if mark == "far":
            return pl.BlockSpec((1,) + shape[1:], lambda g, p: (distance(g),) + zeros)
        return pl.BlockSpec((1,) + shape[1:], lambda g, p: (mark(g),) + zeros)

    operands, scratch = tuple(operands), tuple(scratch)
    kernel = body
    if weights is not None:
        operands = tuple((weight, "any" if pieces else True) for weight in weights) + operands
    if pieces:
        some = weights[0]
        height, width = some.shape[0] * some.shape[1] * some.shape[2], some.shape[3]
        full = (steps, some.shape[1], some.shape[0]) + some.shape[2:]
        scratch += ((full, some.dtype), ((steps, 2), None))

        def kernel(place_ref, *refs):
            full_ref, sems = refs[-2:]
            step = pl.program_id(0)
            copies = [
                (r, group_copies(place_ref, refs[:4], full_ref.at[i], sems.at[i], r))
                for i, r in enumerate(order)
            ]

            @pl.when(step == 0)
            def _():
                for distance, choices in copies:
                    each_copy(place_ref, distance, choices, start_copy)

            for index in range(steps):

                @pl.when(step == index)
                def _(index=index):
                    each_copy(place_ref, *copies[index], wait_copy)

            def weight(start=0, stop=width):
                return full_ref[step, :, :, :, start:stop].reshape(height, stop - start)

            body(place_ref, weight, *refs[4:-2])

    elif weights is not None:

        def kernel(place_ref, weight_ref, *refs):
            def weight(start=0, stop=weight_ref.shape[2]):
                return weight_ref[0, :, start:stop]

            body(place_ref, weight, *refs)

    return pl.pallas_call(
        kernel,
        grid_spec=pltpu.PrefetchScalarGridSpec(
            num_scalar_prefetch=1,
            grid=(steps,),
            in_specs=[spec(value.shape, mark) for value, mark in operands],
            out_specs=[spec(shape, mark) for shape, _, mark in results],
            scratch_shapes=[
                pltpu.SemaphoreType.DMA(shape) if kind is None else pltpu.VMEM(shape, kind)
                for shape, kind in scratch
            ],
        ),
        out_shape=[jax.ShapeDtypeStruct(shape, kind) for shape, kind, _ in results],
        compiler_params=pltpu.CompilerParams(vmem_limit_bytes=48 * 1024 * 1024),
        cost_estimate=pl.CostEstimate(flops=flops, bytes_accessed=16_000_000, transcendentals=0),
    )(place, *[value for value, _ in operands])


def local(
    patches,
    keep_mask,
    labels,
    stem_weight,
    position_table,
    attend_in,
    attend_out,
    expand,
    contract,
    head_weight,
    vectors,
    stem_rows,
    stem_cols,
    table_rows,
    table_cols,
    attend_in_rows,
    attend_in_cols,
    attend_out_rows,
    attend_out_cols,
    expand_rows,
    expand_cols,
    contract_rows,
    contract_cols,
    head_rows,
    head_cols,
    vector_second,
):
    data_size, model_size = lax.axis_size("dp"), lax.axis_size("mp")
    links = Grid() if (data_size, model_size) == (8, 4) else Plain(data_size, model_size)
    here = links.place
    count, patch_count, _ = patches.shape
    groups = model_size
    pair = groups // 2
    image_count = count * data_size * model_size
    inverse_count = 1.0 / image_count
    row_share, _, head_share = attend_in.shape
    hidden_share = expand.shape[1]
    in_share = 3 * head_share
    slots = patch_count + 1
    padded = -(-slots // 16) * 16
    rows = count * padded
    contract_own = contract.T
    attend_own, attend_piece, expand_piece, contract_piece, squares = call(
        pieces_kernel,
        (0,),
        here,
        (
            (attend_in.swapaxes(0, 1), False),
            (attend_out, False),
            (expand, False),
            (contract_own, False),
        ),
        (((row_share, D), f32, False),)
        + (((row_share, D), bf16, False),) * 3
        + (((1, 128), f32, False),),
    )
    attend_chain = Chain(links.gather(attend_piece))
    pixels = jnp.pad(patches, ((0, 0), (0, padded - patch_count), (0, 0))).reshape(rows, -1)
    empty = jnp.zeros((padded - slots, D), f32)
    table = jnp.concatenate([position_table[1:], position_table[:1], empty])
    vector_lines = jnp.pad(vectors, (0, 24 * D - vectors.shape[0])).reshape(24, D)
    (
        pixels,
        table,
        vector_lines,
        expand_piece,
        contract_piece,
        head_weight,
    ) = sync(
        [attend_chain],
        pixels,
        table,
        vector_lines,
        expand_piece,
        contract_piece,
        head_weight,
    )
    expand_chain = Chain(links.gather(expand_piece))
    stream_zero, rows_one, present, column, facts = call(
        stem_kernel,
        (0,),
        here,
        (
            (labels, "smem"),
            (after(pixels, attend_chain.sent), False),
            (stem_weight, False),
            (table, False),
            (vector_lines, False),
            (keep_mask, False),
        ),
        (
            ((rows, D), f32, False),
            ((rows, D), bf16, False),
            ((count, padded), f32, False),
            ((rows, 1), f32, False),
            ((2 * count, 128), f32, False),
        ),
        flops=2 * rows * D * D,
    )
    stream_zero, rows_one, contract_piece, head_weight = sync(
        [attend_chain, expand_chain],
        stream_zero,
        rows_one,
        contract_piece,
        head_weight,
    )
    contract_chain = Chain(links.gather(contract_piece))
    head_turned = head_weight.T
    head_low = head_turned.astype(bf16)

    head_low, _ = sync([attend_chain, contract_chain], head_low, expand_chain.sent)
    sync([attend_chain, expand_chain], contract_chain.sent)
    attend_all = attend_chain.result
    every = tuple(range(groups))

    qkv, attended, stream_one, rows_two, turned_one, turned_two, stream_sum = call(
        functools.partial(attend_kernel, blocks=links.blocks, order=every),
        every,
        here,
        (
            (rows_one, False),
            (vector_lines, False),
            (present, False),
            (stream_zero, False),
            (column, False),
        ),
        (
            ((groups, 3, rows, head_share), bf16, "far"),
            ((groups, rows, head_share), bf16, "far"),
            ((rows, D), f32, False),
            ((rows, D), bf16, False),
            ((D, rows), bf16, False),
            ((D, rows), bf16, False),
            ((2 * count, D), f32, False),
        ),
        flops=2 * rows * D * 4 * D,
        weights=attend_all,
    )
    rows_two, stream_sum = sync([expand_chain, contract_chain], rows_two, stream_sum)
    rows_two = sync([expand_chain], rows_two)
    expand_all = expand_chain.result
    active_sum, slope = call(
        functools.partial(hidden_kernel, order=every),
        every,
        here,
        (
            (rows_two, False),
            (vector_lines, False),
            (present, False),
            (column, False),
        ),
        (
            ((groups, 2 * count, hidden_share), f32, "far"),
            ((groups, rows, hidden_share), bf16, "far"),
        ),
        flops=2 * rows * D * FF,
        weights=expand_all,
    )
    active_sum, slope = sync([contract_chain], active_sum, slope)
    active_sum, slope = sync([contract_chain], active_sum, slope)

    contract_all = contract_chain.result
    scratch = ()
    if len(contract_all) == 4:
        scratch = (
            ((groups, data_size // 2, 2, row_share, hidden_share), bf16),
            ((groups, 2), None),
        )
    piece, d_row, d_active_row = call(
        functools.partial(own_head_kernel, inverse_count=inverse_count),
        (0,),
        here,
        tuple((value, False) for value in (active_sum, stream_sum, facts, vector_lines, head_low))
        + tuple((value, "any" if scratch else False) for value in contract_all),
        (
            ((8 * count, D + 128), bf16, False),
            ((2 * count, D), f32, False),
            ((groups, 2 * count, hidden_share), f32, False),
        ),
        scratch,
    )

    pieces_chain = Chain(links.gather(piece))
    far_grad, near_grad, expand_bias_grad, d_rows_two = call(
        expand_back_kernel,
        (3, 1, 2, 0),
        here,
        (
            (turned_two, False),
            (slope, "far"),
            (d_active_row, "far"),
        ),
        (
            ((pair, D, hidden_share), bf16, lambda g: jnp.minimum(g, pair - 1)),
            ((pair, D, hidden_share), bf16, lambda g: jnp.maximum(g - pair, 0)),
            ((groups, 1, hidden_share), f32, "far"),
            ((rows, D), f32, False),
        ),
        (((rows, hidden_share), bf16),),
        flops=4 * rows * D * FF,
        weights=expand_all,
    )
    far_grad, near_grad, d_rows_two = sync([pieces_chain], far_grad, near_grad, d_rows_two)
    expand_sum = Chain(links.reduce(far_grad))
    d_stream, d_attend_low, d_turned, vector_two = call(
        functools.partial(between_kernel, blocks=links.blocks),
        (0,),
        here,
        (
            (d_rows_two, False),
            (d_row, False),
            (column, False),
            (stream_one, False),
            (vector_lines, False),
        ),
        (
            ((rows, D), f32, False),
            ((rows, D), bf16, False),
            ((D, rows), bf16, False),
            ((8, D), f32, False),
        ),
    )

    d_stream, d_attend_low, d_turned = sync(
        [pieces_chain, (expand_sum, near_grad)], d_stream, d_attend_low, d_turned
    )

    def attend_back(order, *before):
        return call(
            attend_back_kernel,
            order,
            here,
            (
                (turned_one, False),
                (qkv, "far"),
                (attended, "far"),
                (column, False),
                (d_attend_low, False),
                (d_turned, False),
            )
            + tuple((value, False) for value in before),
            (
                ((pair, D, D), bf16, lambda g: g),
                ((pair, 2 * count, head_share), f32, lambda g: g),
                ((rows, D), f32, False),
            ),
            (((rows, 3 * head_share), bf16),),
            flops=2 * rows * D * 4 * D,
            weights=attend_all,
        )

    far_grad, heads_far, d_rows_one = attend_back((3, 1))
    far_grad, d_rows_one = sync([pieces_chain, expand_sum], far_grad, d_rows_one)
    attend_sum = Chain(links.reduce(far_grad))
    near_grad, heads_near, d_rows_one = attend_back((2, 0), d_rows_one)
    d_rows_one = sync([pieces_chain, expand_sum, (attend_sum, near_grad)], d_rows_one)
    both_far, both_near, vector_one = call(
        stem_back_kernel,
        (0,),
        here,
        (
            (after(d_rows_one, attend_sum.sent, expand_sum.sent), False),
            (d_stream, False),
            (stream_zero, False),
            (vector_lines, False),
            (pixels, False),
        ),
        (
            ((4, 128, D), bf16, False),
            ((4, 128, D), bf16, False),
            ((8 + padded, D), f32, False),
        ),
        flops=2 * rows * D * D,
    )
    pieces, both_far, both_near = sync(
        [attend_sum, expand_sum], pieces_chain.result, both_far, both_near
    )
    grad_expand = expand_sum.result
    both_sum = Chain(links.add_large(both_far, both_near))
    pieces = links.whole(*pieces).reshape((-1,) + piece.shape)
    pieces, grad_expand = sync([attend_sum, both_sum], pieces, grad_expand)
    steps = max(1, pieces.shape[0] // 32)
    head_new, head_rows_new, head_cols_new, grad_contract, vector_last, vector_head = call(
        functools.partial(all_head_kernel, inverse_count=inverse_count),
        (0,) * steps,
        here,
        (
            (pieces.reshape((steps, -1) + piece.shape), lambda g: g),
            (vector_lines, False),
            (head_low, False),
            (head_turned, False),
            (head_rows[None], False),
            (head_cols[None], False),
        ),
        (
            ((CLASSES, D), f32, False),
            ((1, D), f32, False),
            ((1, CLASSES), f32, False),
            ((row_share, hidden_share), f32, False),
            ((8, D), f32, False),
            ((8, CLASSES), f32, False),
        ),
        (((CLASSES, D), f32),),
    )
    loss_sum = vector_head[1, 0]
    grad_expand, grad_contract = sync([attend_sum, both_sum], grad_expand, grad_contract)
    grad_attend = attend_sum.result

    names = dict(data=data_size, groups=groups, share=head_share)
    lines = layout(data_size, groups)[3]
    (sums,) = call(
        functools.partial(sums_kernel, patch_count=patch_count, **names),
        (0,),
        here,
        tuple(
            (value, False)
            for value in (
                grad_attend,
                grad_expand,
                grad_contract,
                squares,
                vector_one,
                vector_two,
                expand_bias_grad,
                heads_far,
                heads_near,
            )
        ),
        (((lines, D), f32, False),),
    )
    sums_chain = Chain(links.add(sums))
    sync([sums_chain, both_sum])
    (
        attend_in_rows,
        attend_out_cols,
        expand_rows,
        contract_cols,
        attend_in_cols,
        attend_out_rows,
        expand_cols,
        contract_rows,
    ) = sync(
        [sums_chain, both_sum],
        attend_in_rows,
        attend_out_cols,
        expand_rows,
        contract_cols,
        attend_in_cols,
        attend_out_rows,
        expand_cols,
        contract_rows,
    )
    def by_block(values):
        return jnp.pad(values.reshape(data_size, row_share), ((0, 0), (0, 128 - row_share)))

    old_rows = jnp.concatenate(
        [by_block(v) for v in (attend_in_rows, attend_out_cols, expand_rows, contract_cols)], 1
    )
    in_cols = attend_in_cols.reshape(3, groups, head_share).swapaxes(0, 1)
    old_cols = jnp.concatenate(
        [
            jnp.concatenate(
                [in_cols.reshape(groups, -1), attend_out_rows.reshape(groups, -1)], 1
            ),
            expand_cols.reshape(groups, -1),
            contract_rows.reshape(groups, -1),
        ]
    )
    old_rows, old_cols, table_rows, vector_second = sync(
        [sums_chain, both_sum], old_rows, old_cols, table_rows, vector_second
    )
    table_down = jnp.concatenate(
        [table_rows[1:], table_rows[:1], jnp.zeros((padded - slots,), f32)]
    )
    downs = (stem_rows[None], table_down[None])
    second_lines = jnp.pad(vector_second, (0, 24 * D - vectors.shape[0])).reshape(24, D)
    second_lines, downs = sync([sums_chain, both_sum], second_lines, downs)
    sync([sums_chain, both_sum])
    sums = sums_chain.result
    rows_new, cols_new, update, scalars, square_totals = call(
        functools.partial(renew_kernel, **names),
        (0,),
        here,
        tuple(
            (value, False)
            for value in (sums, old_rows, old_cols, grad_attend, grad_expand, grad_contract)
        ),
        (
            (old_rows.shape, f32, False),
            (old_cols.shape, f32, False),
            ((3, row_share, D), f32, False),
            ((8, 128), f32, False),
            ((8, 128), f32, False),
        ),
    )
    scalars_chain = Chain(links.add(scalars))
    rows_new, cols_new, sums = sync([scalars_chain, both_sum], rows_new, cols_new, sums)
    stem_new, stem_rows_new, stem_cols_new, table_new, table_rows_new, table_cols_new = call(
        functools.partial(stem_step_kernel, slots=slots),
        (0,),
        here,
        tuple(
            (value, False)
            for value in both_sum.result
            + (stem_weight, downs[0], stem_cols[None], table, downs[1], table_cols[None])
        ),
        tuple(
            (shape, f32, False)
            for shape in ((D, D), (1, D), (1, D), (padded, D), (1, padded), (1, D))
        ),
        (((1024, D), bf16),),
    )
    stem_new, table_new, table_rows_new, rows_new, cols_new, sums = sync(
        [scalars_chain], stem_new, table_new, table_rows_new, rows_new, cols_new, sums
    )

    vector_lines_new = call(
        functools.partial(vector_kernel, length=vectors.shape[0], **names),
        (0,),
        here,
        tuple(
            (value, False) for value in (sums, vector_last, vector_head, vector_lines, second_lines)
        ),
        (((24, D), f32, False),) * 3,
    )
    vector_lines_new, table_new, table_rows_new, rows_new, cols_new = sync(
        [scalars_chain], vector_lines_new, table_new, table_rows_new, rows_new, cols_new
    )
    grad_vector, vectors_new, second_new = (
        lines.reshape(-1)[: vectors.shape[0]] for lines in vector_lines_new
    )
    table_rows_new = table_rows_new.reshape(-1)
    table_new = jnp.concatenate([table_new[patch_count:slots], table_new[:patch_count]])
    table_rows_new = jnp.concatenate(
        [table_rows_new[patch_count:slots], table_rows_new[:patch_count]]
    )
    table_new, rows_new, cols_new = sync([scalars_chain], table_new, rows_new, cols_new)

    def of_blocks(index):
        return rows_new[:, index * 128 : index * 128 + row_share].reshape(-1)

    in_cols_new = cols_new[:groups, :in_share].reshape(groups, 3, head_share).swapaxes(0, 1)
    statistics = (
        of_blocks(0),
        in_cols_new.reshape(3, D),
        cols_new[:groups, in_share:].reshape(-1),
        of_blocks(1),
        of_blocks(2),
        cols_new[groups : 2 * groups].reshape(-1),
        cols_new[2 * groups :].reshape(-1),
        of_blocks(3),
    )
    statistics = sync([scalars_chain], statistics)
    block = call(
        functools.partial(step_kernel, sizes=(3 * D * D, D * D, D * FF, FF * D)),
        (0,),
        here,
        tuple(
            (value, False)
            for value in (
                update,
                scalars_chain.result,
                square_totals,
                attend_own,
                expand,
                contract_own,
            )
        ),
        tuple(
            (shape, kind, False)
            for shape in (
                (3, row_share, head_share),
                (head_share, row_share),
                (row_share, hidden_share),
                (row_share, hidden_share),
            )
            for kind in (f32, bf16)
        ),
    )
    in_new, in_copy, out_new, out_copy, expand_new, expand_copy, contract_new, contract_copy = block

    return (
        loss_sum,
        stem_new,
        stem_rows_new.reshape(-1),
        stem_cols_new.reshape(-1),
        table_new,
        table_rows_new,
        table_cols_new.reshape(-1),
        in_new.swapaxes(0, 1),
        in_copy.swapaxes(0, 1),
        statistics[0],
        statistics[1],
        out_new,
        out_copy,
        statistics[2],
        statistics[3],
        expand_new,
        expand_copy,
        statistics[4],
        statistics[5],
        contract_new.T,
        contract_copy.T,
        statistics[6],
        statistics[7],
        head_new.T,
        head_rows_new.reshape(-1),
        head_cols_new.reshape(-1),
        vectors_new,
        grad_vector,
        second_new,
    )


def solution(mesh):
    placed = (
        P(ALL, None, None),
        P(ALL, None),
        P(ALL),
        P(),
        P(),
        P("dp", None, "mp"),
        P("mp", "dp"),
        P("dp", "mp"),
        P("mp", "dp"),
    ) + (P(),) * 17
    block = (P("dp", None, "mp"), P("mp", "dp"), P("dp", "mp"), P("mp", "dp"))
    given = [P()] * 7
    for spec in block:
        given += [spec, spec, P(), P()]
    given += [P()] * 6
    return jax.shard_map(
        local, mesh=mesh, in_specs=placed, out_specs=tuple(given), check_vma=False
    )
```

```python
import functools

import jax
import jax.numpy as jnp
from jax import lax
from jax.experimental import pallas as pl
from jax.experimental.pallas import tpu as pltpu
from jax.sharding import PartitionSpec as P

D = 768
HEAD_DIM = 64
FF = 3072
CLASSES = 1000

eps_norm = 1e-06
eps_one = 1e-30
eps_two = 0.001
decay_rate = 0.5
clip_level = 0.3
step_rate = 1.0
smoothing = 0.1

ALL = ("dp", "mp")
f32 = jnp.float32
bf16 = jnp.bfloat16


def after(value, *others):
    return lax.optimization_barrier((value,) + others)[0]


class Chain:
    def __init__(self, stages):
        self.stages = stages
        self.result = None
        self.sent, self.flight = next(stages)

    def advance(self, arrived):
        try:
            self.sent, self.flight = self.stages.send(arrived)
        except StopIteration as end:
            self.sent, self.flight, self.result = (), (), end.value


def sync(chains, *values):
    chains = [chain if isinstance(chain, tuple) else (chain,) for chain in chains]
    flights = [(chain[0].flight,) + chain[1:] for chain in chains]
    flights, values = lax.optimization_barrier((flights, values))
    for chain, flight in zip(chains, flights):
        chain[0].advance(flight if len(flight) > 1 else flight[0])
    return values[0] if len(values) == 1 else values


class Plain:
    blocks = None

    def __init__(self, rows, cols):
        self.rows, self.cols = rows, cols
        self.place = jnp.stack(
            [jnp.zeros((), jnp.int32)] * 4
            + [lax.axis_index("dp"), lax.axis_index("mp"), jnp.zeros((), jnp.int32)]
            + [jnp.full((), 4, jnp.int32)]
        ).astype(jnp.int32)

    def gather(self, piece):
        full = lax.all_gather(piece, ALL, axis=0)
        full = full.reshape((self.rows, self.cols) + piece.shape).swapaxes(0, 1)
        for _ in range(4):
            yield (), ()
        return (full.reshape(self.cols, self.rows * piece.shape[0], piece.shape[1]),)

    def whole(self, full):
        return full

    def reduce(self, far):
        _, near = yield (), ()
        grads = jnp.stack([near[1], far[1], near[0], far[0]])
        grads = grads.reshape(self.cols, self.rows, -1, grads.shape[2])
        grads = grads.swapaxes(0, 1).reshape((-1,) + grads.shape[2:])
        total = lax.psum_scatter(grads, ALL, scatter_dimension=0).astype(f32)
        for _ in range(3):
            total = yield (), total
        return total

    def add(self, values):
        values = lax.psum(values, ALL)
        for _ in range(5):
            values = yield (), values
        return values

    def add_large(self, far, near):
        values = lax.psum((near, far), ALL)
        for _ in range(8):
            values = yield (), values
        return values


def group_copies(place_ref, piece_refs, full_ref, sems, distance):
    near_ref, far_ref = piece_refs[2:] if distance % 2 else piece_refs[:2]
    flip = distance // 2
    x = place_ref[1]
    source = far_ref if flip else near_ref
    along_y = [
        pltpu.make_async_copy(source.at[0], full_ref.at[:, x], sems.at[0]),
        pltpu.make_async_copy(source.at[1], full_ref.at[:, 1 - x], sems.at[1]),
    ]
    along_x = [
        pltpu.make_async_copy(near_ref.at[flip], full_ref.at[:, x], sems.at[0]),
        pltpu.make_async_copy(far_ref.at[flip], full_ref.at[:, 1 - x], sems.at[1]),
    ]
    return along_y, along_x


def each_copy(place_ref, distance, choices, act):
    owner = place_ref[3] ^ (distance % 2)
    for core in range(2):

        @pl.when(owner == core)
        def _(copies=choices[core]):
            for copy in copies:
                act(copy)


def start_copy(copy):
    copy.start()


def wait_copy(copy):
    copy.wait()


def column_kernel(place_ref, *refs):
    *piece_refs, column_ref = refs
    for step, ref in enumerate(piece_refs):
        column_ref[0, lax.rem(place_ref[0] + step, len(piece_refs))] = ref[...]


class Grid:
    deep, devices, blocks = 4, 32, 8

    def __init__(self):
        dp, mp = lax.axis_index("dp"), lax.axis_index("mp")
        self.z, self.x, self.y, self.core = dp // 2, dp % 2, mp // 2, mp % 2
        self.at_first = jnp.where(self.core == 0, self.y, self.x)
        self.at_second = jnp.where(self.core == 0, self.x, self.y)
        chunk = self.core * 4 + self.at_first * 2 + self.at_second
        other_chunk = (1 - self.core) * 4 + self.at_second * 2 + self.at_first
        self.place = jnp.stack([self.z, self.x, self.y, self.core, dp, mp, chunk, other_chunk])
        self.place = self.place.astype(jnp.int32)
        self.other = self.pairs(lambda z, x, y, c: (z, x, y, 1 - c))
        self.first = self.pairs(lambda z, x, y, c: (z, x ^ c, y ^ (1 - c), c))
        self.second = self.pairs(lambda z, x, y, c: (z, x ^ (1 - c), y ^ c, c))
        self.along_x = self.pairs(lambda z, x, y, c: (z, 1 - x, y, c))
        self.along_y = self.pairs(lambda z, x, y, c: (z, x, 1 - y, c))
        self.up = [self.pairs(lambda z, x, y, c, s=s: ((z + s) % 4, x, y, c)) for s in range(4)]
        self.flip_z = [self.pairs(lambda z, x, y, c, s=s: (z ^ s, x, y, c)) for s in range(4)]

    def pairs(self, move):
        table = []
        for index in range(self.devices):
            z, x, y, c = move(index // 8, index // 4 % 2, index // 2 % 2, index % 2)
            table.append((index, ((z * 2 + x) * 2 + y) * 2 + c))
        return table

    @staticmethod
    def send(values, table):
        return lax.ppermute(values, ALL, table)

    def gather(self, piece):
        got = yield piece, [self.send(piece, self.up[-s]) for s in (1, 2, 3)]
        column = pl.pallas_call(
            column_kernel,
            in_specs=[pl.BlockSpec(memory_space=pltpu.SMEM)]
            + [pl.BlockSpec(memory_space=pltpu.VMEM)] * self.deep,
            out_specs=pl.BlockSpec(memory_space=pltpu.VMEM),
            out_shape=jax.ShapeDtypeStruct((1, self.deep) + piece.shape, piece.dtype),
        )(self.place, piece, *got)
        got = yield column, self.send(column, self.second)
        pair = jnp.concatenate([column, got])
        rest, theirs = yield pair, (self.send(pair, self.first), self.send(pair, self.other))
        rest_theirs = yield rest, self.send(rest, self.other)
        return pair, rest, theirs, rest_theirs

    def whole(self, *pieces):
        blocks, (r, c) = self.blocks, pieces[0].shape[2:]

        def body(place_ref, *refs):
            full_ref, sems = refs[-2:]
            own = place_ref[2] * 2 + place_ref[3]
            groups = [
                (i, group_copies(place_ref, refs[:4], full_ref.at[own ^ i], sems.at[i], i))
                for i in range(4)
            ]
            for act in (start_copy, wait_copy):
                for distance, choices in groups:
                    each_copy(place_ref, distance, choices, act)

        full = pl.pallas_call(
            body,
            in_specs=[pl.BlockSpec(memory_space=pltpu.SMEM)]
            + [pl.BlockSpec(memory_space=pl.ANY)] * 4,
            out_specs=pl.BlockSpec(memory_space=pltpu.VMEM),
            out_shape=jax.ShapeDtypeStruct((4, self.deep, 2, r, c), pieces[0].dtype),
            scratch_shapes=[pltpu.SemaphoreType.DMA((4, 2))],
            compiler_params=pltpu.CompilerParams(vmem_limit_bytes=16 * 1024 * 1024),
        )(self.place, *pieces)
        return full.reshape(4, blocks * r, c)

    def reduce(self, far):
        theirs, near = yield far, self.send(far, self.other)
        size, width = near.shape[1] // self.blocks, near.shape[2]
        near = near.reshape(2, self.deep, 2, size, width)
        theirs = theirs.reshape(near.shape)

        def chip(y, x):
            spot, part = (y, 0, x, 0, 0), (1, self.deep, 1, size, width)
            total = lax.dynamic_slice(near, spot, part).astype(f32)
            total = total + lax.dynamic_slice(theirs, spot, part).astype(f32)
            return total.reshape(self.deep, size, width)

        sent = jnp.stack(
            [chip(0, 1 - self.x), chip(self.core, jnp.where(self.core == 0, self.x, 1 - self.x))]
        ).astype(bf16)
        got = yield sent, self.send(sent, self.first)
        kept = chip(1 - self.core, jnp.where(self.core == 0, 1 - self.x, self.x))
        away = (kept + got[0].astype(f32)).astype(bf16)
        came = yield away, self.send(away, self.second)
        column = chip(1, self.x) + got[1].astype(f32) + came.astype(f32)
        low = column.astype(bf16)

        def level(values, step):
            return lax.dynamic_index_in_dim(values, (self.z + step) % 4, 0, keepdims=False)

        total = level(column, 0)
        for part in (yield low, [self.send(level(low, s), self.up[s]) for s in (1, 2, 3)]):
            total = total + part.astype(f32)
        return total

    def add(self, values):
        for table in (self.other, self.along_y, self.along_x, self.flip_z[1], self.flip_z[2]):
            values = values + (yield values, self.send(values, table))
        return values

    def add_large(self, far, near):
        values = near.astype(f32) + (yield far, self.send(far, self.other)).astype(f32)
        for table in (self.first, self.second):
            half = values.shape[0] // 2
            sent = values[half:].astype(bf16)
            got = yield sent, self.send(sent, table)
            values = values[:half] + got.astype(f32)
        pile = values.astype(bf16)
        for table in (self.flip_z[1], self.flip_z[2]):
            got = yield pile, self.send(pile, table)
            pile = (pile.astype(f32) + got.astype(f32)).astype(bf16)
        for table in (self.second, self.first):
            pile = jnp.concatenate([pile, (yield pile, self.send(pile, table))])
        return pile, (yield pile, self.send(pile, self.other))


def normal_parts(values):
    centred = values - jnp.mean(values, -1, keepdims=True)
    inverse = lax.rsqrt(jnp.mean(centred * centred, -1, keepdims=True) + eps_norm)
    return centred * inverse, inverse


def pull_normal(values, gain, grads):
    hat, inverse = normal_parts(values)
    scaled = grads * gain
    mean_one = jnp.mean(scaled, -1, keepdims=True)
    mean_two = jnp.mean(scaled * hat, -1, keepdims=True)
    below = (scaled - mean_one - hat * mean_two) * inverse
    return below, jnp.sum(grads * hat, 0, keepdims=True), jnp.sum(grads, 0, keepdims=True)


STEM_BIAS, GAIN_ONE, SHIFT_ONE, QUERY_BIAS, VALUE_BIAS, ATTEND_BIAS, GAIN_TWO, SHIFT_TWO = range(8)
EXPAND_BIAS, CONTRACT_BIAS, GAIN_LAST, SHIFT_LAST, HEAD_BIAS = 8, 12, 13, 14, 15


def line(vectors_ref, index):
    return vectors_ref[index : index + 1, :]


def to_column(present_ref, column_ref):
    padded = present_ref.shape[1]
    for image in range(present_ref.shape[0]):
        span = slice(image * padded, (image + 1) * padded)
        column_ref[span, :] = upright(present_ref[image : image + 1, :])


def to_lines(flat_ref, lines_ref):
    width = lines_ref.shape[1]
    lines_ref[...] = jnp.zeros(lines_ref.shape, f32)
    for row, start in enumerate(range(0, flat_ref.shape[0], width)):
        extent = min(width, flat_ref.shape[0] - start)
        values = flat_ref[pl.ds(start, extent)]
        lines_ref[row : row + 1, :extent] = values.reshape(1, extent)


def from_lines(lines, flat_ref):
    width = lines.shape[1]
    for row, start in enumerate(range(0, flat_ref.shape[0], width)):
        extent = min(width, flat_ref.shape[0] - start)
        flat_ref[pl.ds(start, extent)] = lines[row, :extent]


def share_of(vectors_ref, index, group, share):
    result = vectors_ref[index : index + 1, :share]
    for other in range(1, vectors_ref.shape[1] // share):
        part = vectors_ref[index : index + 1, other * share : (other + 1) * share]
        result = jnp.where(group == other, part, result)
    return result


def own_group(place_ref, order):
    step = pl.program_id(0)
    distance = order[0]
    for index, value in enumerate(order[1:], 1):
        distance = jnp.where(step == index, value, distance)
    return (place_ref[2] * 2 + place_ref[3]) ^ distance


def dot(left, right, left_dim=1, right_dim=0):
    return lax.dot_general(
        left, right, (((left_dim,), (right_dim,)), ((), ())), preferred_element_type=f32
    )


def put(count, index, line):
    spot = lax.broadcasted_iota(jnp.int32, (count, 1), 0)
    return jnp.where(spot == index, line, 0.0)


def pick(lines, index):
    spot = lax.broadcasted_iota(jnp.int32, (lines.shape[0], 1), 0)
    return jnp.sum(jnp.where(spot == index, lines, 0.0), 0, keepdims=True)


def upright(row):
    n = row.shape[1]
    more = -n % 128
    if more:
        row = jnp.concatenate([row, jnp.zeros((1, more), f32)], 1)
    return jnp.broadcast_to(row, (128, n + more)).T[:n, 0:1]


def lying(column):
    n = column.shape[0]
    wide = jnp.broadcast_to(column, (n, 128))
    more = -n % 128
    if more:
        wide = jnp.concatenate([wide, jnp.zeros((more, 128), f32)])
    return wide.T[0:1, :n]


def probabilities(query, key, visible):
    scores = dot(query, key, 1, 1) * HEAD_DIM ** (-0.5)
    scores = jnp.where(visible, scores, -1e30)
    raised = jnp.exp(scores - jnp.max(scores, -1, keepdims=True))
    return raised * (1.0 / jnp.sum(raised, -1, keepdims=True))


def head_masks(share):
    lane = lax.broadcasted_iota(jnp.int32, (1, share), 1) // HEAD_DIM
    return [lane == head for head in range(share // HEAD_DIM)]


def stacked(rows, masks):
    return jnp.concatenate([jnp.where(mask, rows, jnp.zeros((), rows.dtype)) for mask in masks])


def unstacked(every, masks):
    size = every.shape[0] // len(masks)
    result = every[:size]
    for head, mask in enumerate(masks[1:], 1):
        result = jnp.where(mask, every[head * size : (head + 1) * size], result)
    return result


def pieces_kernel(
    place_ref,
    in_ref,
    out_ref,
    expand_ref,
    contract_ref,
    vectors_ref,
    own_ref,
    attend_low_ref,
    expand_low_ref,
    contract_low_ref,
    square_ref,
    lines_ref,
):
    to_lines(vectors_ref, lines_ref)
    share = out_ref.shape[0]
    lane = lax.broadcasted_iota(jnp.int32, (1, 128), 1)
    for part in range(3):
        own_ref[:, part * share : (part + 1) * share] = in_ref[part]
    own_ref[:, 3 * share :] = out_ref[...].T
    attend_low_ref[...] = own_ref[...].astype(bf16)
    expand_low_ref[...] = expand_ref[...].astype(bf16)
    contract_low_ref[...] = contract_ref[...].astype(bf16)
    totals = jnp.zeros((1, 128), f32)
    for index, ref in enumerate((in_ref, out_ref, expand_ref, contract_ref)):
        values = ref[...]
        total = jnp.sum(values * values, keepdims=True).reshape(1, 1)
        totals = jnp.where(lane == index, total, totals)
    square_ref[...] = totals


def in_slots(table_ref, padded):
    empty = jnp.zeros((padded - table_ref.shape[0], table_ref.shape[1]), f32)
    return jnp.concatenate([table_ref[1:], table_ref[0:1], empty])


def stem_kernel(
    place_ref,
    labels_ref,
    pixels_ref,
    stem_ref,
    table_ref,
    vectors_ref,
    mask_ref,
    stream_ref,
    rows_ref,
    present_ref,
    facts_ref,
):
    count, patch_count = mask_ref.shape
    padded = present_ref.shape[1]
    low = stem_ref[...].astype(bf16)
    slot = lax.broadcasted_iota(jnp.int32, (padded, 1), 0)
    table = in_slots(table_ref, padded)
    table = table + jnp.where(slot < patch_count, line(vectors_ref, STEM_BIAS), 0.0)
    for image in range(count):
        span = slice(image * padded, (image + 1) * padded)
        stream = dot(pixels_ref[span, :], low) + table
        stream_ref[span, :] = stream
        hat, _ = normal_parts(stream)
        normed = hat * line(vectors_ref, GAIN_ONE) + line(vectors_ref, SHIFT_ONE)
        rows_ref[span, :] = normed.astype(bf16)
    lane = lax.broadcasted_iota(jnp.int32, (count, padded), 1)
    present_ref[...] = jnp.where(lane == patch_count, 1.0, 0.0)
    present_ref[:, :patch_count] = mask_ref[...].astype(f32)
    lane = lax.broadcasted_iota(jnp.int32, (1, 128), 1)
    for image in range(count):
        present = present_ref[image : image + 1, :]
        kept = jnp.sum(present, 1, keepdims=True)
        label = labels_ref[image].astype(f32)
        fact = jnp.where(lane == 0, kept, jnp.where(lane == 1, label, 0.0))
        facts_ref[image : image + 1, :] = fact
        facts_ref[count + image : count + image + 1, :] = fact


def attend_kernel(
    place_ref,
    weight,
    rows_ref,
    vectors_ref,
    present_ref,
    stream_ref,
    qkv_ref,
    attended_ref,
    stream_out_ref,
    rows_out_ref,
    sum_ref,
    *,
    order,
):
    step = pl.program_id(0)
    count, padded = present_ref.shape
    share = attended_ref.shape[2]

    group = own_group(place_ref, order)
    projected = dot(rows_ref[...], weight(0, 3 * share))
    query = projected[:, :share] + share_of(vectors_ref, QUERY_BIAS, group, share)
    query = query.astype(bf16)
    key = projected[:, share : 2 * share].astype(bf16)
    value = projected[:, 2 * share :] + share_of(vectors_ref, VALUE_BIAS, group, share)
    value = value.astype(bf16)
    qkv_ref[0, 0] = query
    qkv_ref[0, 1] = key
    qkv_ref[0, 2] = value
    masks = head_masks(share)
    for image in range(count):
        span = slice(image * padded, (image + 1) * padded)
        visible = present_ref[image : image + 1, :] > 0.5
        low = probabilities(stacked(query[span], masks), key[span], visible).astype(bf16)
        every = dot(low, value[span])
        attended_ref[0, span, :] = unstacked(every, masks).astype(bf16)
    part = dot(attended_ref[0], weight(3 * share, 4 * share), 1, 1)

    @pl.when(step == 0)
    def _():
        stream_out_ref[...] = stream_ref[...] + line(vectors_ref, ATTEND_BIAS) + part

    @pl.when(step > 0)
    def _():
        stream_out_ref[...] += part

    @pl.when(step == pl.num_programs(0) - 1)
    def _():
        hat, _ = normal_parts(stream_out_ref[...])
        rows_two = hat * line(vectors_ref, GAIN_TWO) + line(vectors_ref, SHIFT_TWO)
        rows_out_ref[...] = rows_two.astype(bf16)
        for image in range(count):
            span = slice(image * padded, (image + 1) * padded)
            here = upright(present_ref[image : image + 1, :])
            total = jnp.sum(stream_out_ref[span, :] * here, 0, keepdims=True)
            sum_ref[image : image + 1, :] = total
            sum_ref[image + count : image + count + 1, :] = total


def hidden_kernel(
    place_ref,
    weight,
    rows_ref,
    vectors_ref,
    present_ref,
    sum_ref,
    slope_ref,
    column_ref,
    *,
    order,
):
    bias = pick(vectors_ref[EXPAND_BIAS : EXPAND_BIAS + len(order), :], own_group(place_ref, order))
    hidden = dot(rows_ref[...], weight()) + bias
    first, second = 0.7978845608028654, 0.044715
    square = hidden * hidden
    half = 0.5 + 0.5 * jnp.tanh(hidden * (first + first * second * square))
    active = (hidden * half).astype(bf16)
    count, padded = present_ref.shape

    @pl.when(pl.program_id(0) == 0)
    def _():
        to_column(present_ref, column_ref)

    row = lax.broadcasted_iota(jnp.int32, (2 * count, 1), 0)
    sums = jnp.zeros(sum_ref.shape[1:], f32)
    for image in range(count):
        chooser = jnp.broadcast_to(present_ref[image : image + 1, :], (2 * count, padded))
        total = dot(chooser.astype(bf16), active[image * padded : (image + 1) * padded])
        sums = jnp.where(row % count == image, total, sums)
    sum_ref[0] = sums
    steep = hidden * (2.0 * first + 6.0 * first * second * square)
    slope = half * (1.0 + steep * (1.0 - half))
    slope_ref[0] = (slope * column_ref[...]).astype(bf16)


def expand_back_kernel(
    place_ref,
    weight,
    rows_ref,
    slope_ref,
    d_active_ref,
    far_ref,
    near_ref,
    bias_ref,
    d_rows_ref,
    d_hidden_low,
):
    step = pl.program_id(0)
    count = d_active_ref.shape[1] // 2
    padded = slope_ref.shape[1] // count
    bias = jnp.zeros((1, d_hidden_low.shape[1]), f32)
    for image in range(count):
        span = slice(image * padded, (image + 1) * padded)
        d_hidden = slope_ref[0, span, :].astype(f32) * d_active_ref[0, image : image + 1, :]
        bias = bias + jnp.sum(d_hidden, 0, keepdims=True)
        d_hidden_low[span, :] = d_hidden.astype(bf16)
    bias_ref[0] = bias
    half = pl.num_programs(0) // 2

    @pl.when(step < half)
    def _():
        far_ref[0] = dot(rows_ref[...], d_hidden_low[...], 0, 0).astype(bf16)

    @pl.when(step >= half)
    def _():
        near_ref[0] = dot(rows_ref[...], d_hidden_low[...], 0, 0).astype(bf16)

    part = dot(d_hidden_low[...], weight(), 1, 1)

    @pl.when(step == 0)
    def _():
        d_rows_ref[...] = part

    @pl.when(step > 0)
    def _():
        d_rows_ref[...] += part


def between_kernel(
    place_ref,
    d_rows_ref,
    d_row_ref,
    present_ref,
    stream_ref,
    vectors_ref,
    d_stream_ref,
    d_low_ref,
    vector_ref,
):
    count = d_row_ref.shape[0] // 2
    padded = stream_ref.shape[0] // count
    gain = line(vectors_ref, GAIN_TWO)
    below, gain, shift = pull_normal(stream_ref[...], gain, d_rows_ref[...])
    vector_ref[1:2, :] = gain
    vector_ref[2:3, :] = shift
    bias = jnp.zeros((1, below.shape[1]), f32)
    for image in range(count):
        span = slice(image * padded, (image + 1) * padded)
        here = upright(present_ref[image : image + 1, :])
        d_stream = below[span] + d_row_ref[image : image + 1, :] * here
        bias = bias + jnp.sum(d_stream, 0, keepdims=True)
        d_stream_ref[span, :] = d_stream
        d_low_ref[span, :] = d_stream.astype(bf16)
    vector_ref[0:1, :] = bias


def attend_back_kernel(
    place_ref,
    weight,
    rows_ref,
    qkv_ref,
    attended_ref,
    present_ref,
    d_low_ref,
    *refs,
):
    grad_ref, bias_ref, d_rows_ref, d_projected, column_ref = refs[-5:]
    step = pl.program_id(0)
    share = attended_ref.shape[2]
    count = bias_ref.shape[1] // 2
    padded = attended_ref.shape[1] // count
    scale = HEAD_DIM ** (-0.5)
    d_attended = dot(d_low_ref[...], weight(3 * share, 4 * share)).astype(bf16)

    @pl.when(step == 0)
    def _():
        to_column(present_ref, column_ref)

    masks = head_masks(share)
    for image in range(count):
        span = slice(image * padded, (image + 1) * padded)
        hidden = column_ref[span, :] < 0.5
        query, key, value = (qkv_ref[0, part, span, :] for part in range(3))
        query = query * jnp.asarray(scale, bf16)
        queries = stacked(query, masks)
        d_images = stacked(d_attended[span], masks)
        scores = jnp.where(hidden, -1e30, dot(key, queries, 1, 1))
        raised = jnp.exp(scores - jnp.max(scores, 0, keepdims=True))
        probs = raised * (1.0 / jnp.sum(raised, 0, keepdims=True))
        d_probs = dot(value, d_images, 1, 1)
        inner = jnp.sum(probs * d_probs, 0, keepdims=True)
        d_scores = (probs * (d_probs - inner)).astype(bf16)
        d_value = dot(probs.astype(bf16), d_images)
        d_key = dot(d_scores, queries)
        d_query = unstacked(dot(d_scores, key, 0, 0), masks) * scale
        bias_ref[0, image : image + 1, :] = jnp.sum(d_query, 0, keepdims=True)
        bias_ref[0, count + image : count + image + 1, :] = jnp.sum(d_value, 0, keepdims=True)
        d_projected[span, :share] = d_query.astype(bf16)
        d_projected[span, share : 2 * share] = d_key.astype(bf16)
        d_projected[span, 2 * share :] = d_value.astype(bf16)
    grad_ref[0, :, : 3 * share] = dot(rows_ref[...], d_projected[...], 0, 0).astype(bf16)
    grad_ref[0, :, 3 * share :] = dot(d_low_ref[...], attended_ref[0], 0, 0).astype(bf16)
    part = dot(d_projected[...], weight(0, 3 * share), 1, 1)

    @pl.when(step == 0)
    def _():
        d_rows_ref[...] = part + refs[0][...] if len(refs) > 5 else part

    @pl.when(step > 0)
    def _():
        d_rows_ref[...] += part


def stem_back_kernel(
    place_ref,
    d_rows_ref,
    d_stream_ref,
    stream_ref,
    vectors_ref,
    pixels_ref,
    far_ref,
    near_ref,
    vector_ref,
):
    rows, width = pixels_ref.shape
    gain = line(vectors_ref, GAIN_ONE)
    below, gain, shift = pull_normal(stream_ref[...], gain, d_rows_ref[...])
    vector_ref[0:1, :] = gain
    vector_ref[1:2, :] = shift
    below = below + d_stream_ref[...]
    slots = vector_ref.shape[0] - 8
    table = below[:slots]
    for image in range(1, rows // slots):
        table = table + below[image * slots : (image + 1) * slots]
    vector_ref[8:, :] = table
    stem = dot(pixels_ref[...], below.astype(bf16), 0, 0).astype(bf16)
    half, size, columns = near_ref.shape
    empty = jnp.zeros((2 * half * size - width - slots, columns), bf16)
    whole = jnp.concatenate([stem, table.astype(bf16), empty])
    for chunk in range(2 * half):
        near, far = place_ref[6] ^ chunk, place_ref[7] ^ chunk

        @pl.when(near < half)
        def _(chunk=chunk, near=near):
            near_ref[near] = whole[chunk * size : (chunk + 1) * size]

        @pl.when(far < half)
        def _(chunk=chunk, far=far):
            far_ref[far] = whole[chunk * size : (chunk + 1) * size]


def head_vectors(vectors_ref):
    rest = CLASSES - vectors_ref.shape[1]
    bias = jnp.concatenate(
        [line(vectors_ref, HEAD_BIAS), vectors_ref[HEAD_BIAS + 1 : HEAD_BIAS + 2, :rest]], 1
    )
    return line(vectors_ref, GAIN_LAST), line(vectors_ref, SHIFT_LAST), bias


def classify(pooled, labels, head, gain, shift, bias, inverse_count):
    hat, inverse = normal_parts(pooled)
    low = (hat * gain + shift).astype(bf16)
    logits = dot(low, head, 1, 1) + bias
    logits = logits - jnp.max(logits, -1, keepdims=True)
    raised = jnp.exp(logits)
    total = jnp.sum(raised, -1, keepdims=True)
    lane = lax.broadcasted_iota(jnp.int32, logits.shape, 1)
    target = jnp.where(lane == labels.astype(jnp.int32), 1.0 - smoothing, 0.0) + smoothing / CLASSES
    score = jnp.sum(target * (logits - jnp.log(total)), -1, keepdims=True)
    d_logits = (raised * (1.0 / total) - target) * inverse_count
    d_final = dot(d_logits.astype(bf16), head)
    scaled = d_final * gain
    mean_one = jnp.mean(scaled, -1, keepdims=True)
    mean_two = jnp.mean(scaled * hat, -1, keepdims=True)
    return score, low, d_logits, d_final, hat, (scaled - mean_one - hat * mean_two) * inverse


def split(values):
    high = values.astype(bf16)
    return high, (values - high.astype(f32)).astype(bf16)


def own_head_kernel(
    place_ref,
    active_ref,
    sum_ref,
    facts_ref,
    vectors_ref,
    head_ref,
    *refs,
    inverse_count,
):
    groups, twice, width = active_ref.shape
    rows = sum_ref.shape[1]
    if len(refs) == 4:
        full_ref, piece_ref, d_row_ref, d_active_ref = refs
        chosen = []
    else:
        piece_ref, d_row_ref, d_active_ref, full_ref, sems = refs[4:]
        chosen = [
            (r, group_copies(place_ref, refs[:4], full_ref.at[r], sems.at[r], r))
            for r in range(groups)
        ]
    for distance, choices in chosen:
        each_copy(place_ref, distance, choices, start_copy)
    mixed = jnp.zeros((2 * twice, rows), f32)
    for group in range(groups):
        for distance, choices in chosen[group : group + 1]:
            each_copy(place_ref, distance, choices, wait_copy)
        weight = full_ref[group].reshape(rows, width)
        mixed = mixed + dot(jnp.concatenate(split(active_ref[group])), weight, 1, 1)
    mixed = mixed[:twice] + mixed[twice:]
    kept, labels = facts_ref[:, 0:1], facts_ref[:, 1:2]
    pooled = (sum_ref[...] + mixed) / kept + line(vectors_ref, CONTRACT_BIAS)
    d_pooled = classify(
        pooled, labels, head_ref[...], *head_vectors(vectors_ref), inverse_count
    )[-1]
    d_row = d_pooled / kept
    d_row_ref[...] = d_row
    d_row_low = d_row.astype(bf16)
    first = lax.broadcasted_iota(jnp.int32, (twice, 1), 0) < twice // 2
    for group in range(groups):
        d_active_ref[group] = dot(d_row_low, full_ref[group].reshape(rows, width))
    for part, (pool, fact) in enumerate(zip(split(pooled), split(facts_ref[...]))):
        piece_ref[part * twice : (part + 1) * twice, :rows] = pool
        piece_ref[part * twice : (part + 1) * twice, rows:] = fact
    own = place_ref[2] * 2 + place_ref[3]
    for half in range(groups // 2):
        sums = jnp.where(first, active_ref[own ^ (2 * half)], active_ref[own ^ (2 * half + 1)])
        span = slice((2 + half) * twice, (3 + half) * twice)
        piece_ref[span, :rows] = sums.astype(bf16)
        piece_ref[span, rows:] = jnp.zeros((twice, piece_ref.shape[1] - rows), bf16)


def all_head_kernel(
    place_ref,
    pieces_ref,
    vectors_ref,
    head_ref,
    weight_ref,
    old_rows_ref,
    old_cols_ref,
    new_ref,
    new_rows_ref,
    new_cols_ref,
    contract_ref,
    vector_ref,
    bias_ref,
    grad_ref,
    *,
    inverse_count,
):
    pieces = pieces_ref[0].astype(f32)
    count, rows = pieces.shape[0], vectors_ref.shape[1]
    twice = pieces.shape[1] // 4

    def part(index):
        return pieces[:, index * twice : (index + 1) * twice].reshape(count * twice, -1)

    lines = part(0) + part(1)
    pooled, kept, labels = lines[:, :rows], lines[:, rows : rows + 1], lines[:, rows + 1 : rows + 2]
    score, low, d_logits, d_final, hat, d_pooled = classify(
        pooled, labels, head_ref[...], *head_vectors(vectors_ref), inverse_count
    )
    half = lax.broadcasted_iota(jnp.int32, (count * twice, 1), 0) % twice // (twice // 2)
    once = half == 0
    d_logits = jnp.where(once, d_logits, 0.0)
    own = place_ref[5]
    active = jnp.where(own // 2 == 0, part(2)[:, :rows], part(3)[:, :rows]).astype(bf16)
    d_row = jnp.where(half == own % 2, d_pooled / kept, 0.0).astype(bf16)
    share = contract_ref.shape[0]
    place = lax.broadcasted_iota(jnp.int32, (rows, share), 0)
    lane = lax.broadcasted_iota(jnp.int32, (rows, share), 1)
    chooser = (place == lane + place_ref[4] * share).astype(f32).astype(bf16)
    d_row = dot(d_row, chooser).astype(bf16)

    def total(values):
        return jnp.sum(jnp.where(once, values, 0.0), 0, keepdims=True)

    results = (
        (grad_ref, slice(None), dot(d_logits.astype(bf16), low, 0, 0)),
        (contract_ref, slice(None), dot(d_row, active, 0, 0)),
        (vector_ref, slice(0, 1), total(d_pooled)),
        (vector_ref, slice(1, 2), total(d_final * hat)),
        (vector_ref, slice(2, 3), total(d_final)),
        (bias_ref, slice(0, 1), jnp.sum(d_logits, 0, keepdims=True)),
        (bias_ref, slice(1, 2), -total(score) + jnp.zeros((1, bias_ref.shape[1]), f32)),
    )
    for ref, span, value in results:

        @pl.when(pl.program_id(0) == 0)
        def _(ref=ref, span=span, value=value):
            ref[span, :] = value

        @pl.when(pl.program_id(0) > 0)
        def _(ref=ref, span=span, value=value):
            ref[span, :] += value

    @pl.when(pl.program_id(0) == pl.num_programs(0) - 1)
    def _():
        new_ref[...], cols, rows_ = factored(
            weight_ref[...],
            grad_ref[...],
            old_cols_ref[...].reshape(1, -1),
            old_rows_ref[...].reshape(1, -1),
            True,
        )
        new_cols_ref[...] = cols[0]
        new_rows_ref[...] = rows_[0]


def factored(weight, grad, down_old, across_old, turned, valid=None, count=None):
    down_old = upright(down_old)
    squared = grad * grad + eps_one
    n, m = grad.shape
    if valid is not None:
        squared = jnp.where(valid, squared, 0.0)
        n = count
    down_new = decay_rate * down_old + (1.0 - decay_rate) * (
        jnp.sum(squared, 1, keepdims=True) / m
    )
    across_new = decay_rate * across_old + (1.0 - decay_rate) * (
        jnp.sum(squared, 0, keepdims=True) / n
    )
    if turned:
        mean = jnp.sum(across_new, keepdims=True) / m
    else:
        mean = jnp.sum(down_new, keepdims=True) / n
    divisor = down_new if valid is None else jnp.where(valid, down_new, 1.0)
    update = grad * lax.rsqrt(divisor * across_new / mean)
    size = n * m
    clip = jnp.sqrt(jnp.sum(update * update, keepdims=True) / size) / clip_level
    magnitude = jnp.sqrt(jnp.sum(weight * weight, keepdims=True) / size)
    scale = step_rate * jnp.maximum(eps_two, magnitude) / jnp.maximum(1.0, clip)
    return weight - scale * update, lying(down_new), across_new


def stem_step_kernel(
    place_ref,
    near_ref,
    far_ref,
    stem_ref,
    stem_rows_ref,
    stem_cols_ref,
    table_ref,
    table_rows_ref,
    table_cols_ref,
    stem_new_ref,
    stem_rows_new_ref,
    stem_cols_new_ref,
    table_new_ref,
    table_rows_new_ref,
    table_cols_new_ref,
    both_ref,
    *,
    padded,
):
    n, slots = stem_ref.shape[0], table_ref.shape[0]
    half, size = near_ref.shape[:2]
    for chunk in range(2 * half):
        near, far = place_ref[6] ^ chunk, place_ref[7] ^ chunk
        span = slice(chunk * size, (chunk + 1) * size)

        @pl.when(near < half)
        def _(span=span, near=near):
            both_ref[span, :] = near_ref[near]

        @pl.when(far < half)
        def _(span=span, far=far):
            both_ref[span, :] = far_ref[far]

    stem_new_ref[...], rows, cols = factored(
        stem_ref[...],
        both_ref[:n, :].astype(f32),
        stem_rows_ref[...].reshape(1, -1),
        stem_cols_ref[...].reshape(1, -1),
        False,
    )
    stem_rows_new_ref[...] = rows[0]
    stem_cols_new_ref[...] = cols[0]
    old = table_rows_ref[...].reshape(1, slots)
    empty = jnp.zeros((1, padded - slots), f32)
    table, rows, cols = factored(
        in_slots(table_ref, padded),
        both_ref[n : n + padded, :].astype(f32),
        jnp.concatenate([old[:, 1:], old[:, 0:1], empty], 1),
        table_cols_ref[...].reshape(1, -1),
        False,
        lax.broadcasted_iota(jnp.int32, (padded, 1), 0) < slots,
        slots,
    )
    table_new_ref[1:] = table[: slots - 1]
    table_new_ref[0:1] = table[slots - 1 : slots]
    table_rows_new_ref[...] = jnp.concatenate(
        [rows[:, slots - 1 : slots], rows[:, : slots - 1]], 1
    )[0]
    table_cols_new_ref[...] = cols[0]


def layout(data, groups):
    return 0, data, data + 4 * groups, -(-(data + 4 * groups + 6) // 8) * 8


def across(column):
    n = column.shape[0]
    wide = jnp.broadcast_to(column, (n, 128))
    if n < 128:
        wide = jnp.concatenate([wide, jnp.zeros((128 - n, 128), f32)])
    return wide.T[0:1]


def down(row, n):
    return jnp.broadcast_to(row, (128, 128)).T[:n, 0:1]


def sums_kernel(
    place_ref,
    attend_ref,
    expand_ref,
    contract_ref,
    squares_ref,
    vector_one_ref,
    vector_two_ref,
    expand_bias_ref,
    heads_far_ref,
    heads_near_ref,
    sums_ref,
    *,
    data,
    groups,
    share,
    patch_count,
):
    block, group = place_ref[4], place_ref[5]
    own = place_ref[2] * 2 + place_ref[3]
    _, at_group, at_single, _ = layout(data, groups)
    sums_ref[...] = jnp.zeros(sums_ref.shape, f32)
    lane = lax.broadcasted_iota(jnp.int32, (1, attend_ref.shape[1]), 1)
    for index, ref in enumerate((attend_ref, expand_ref, contract_ref)):
        grad = ref[...]
        squared = grad * grad + eps_one
        span = slice(at_group + index * groups, at_group + (index + 1) * groups)
        sums_ref[span, :] = put(groups, group, jnp.sum(squared, 0, keepdims=True))
        if index == 0:
            lines = (
                jnp.sum(jnp.where(lane < 3 * share, squared, 0.0), 1, keepdims=True),
                jnp.sum(jnp.where(lane < 3 * share, 0.0, squared), 1, keepdims=True),
            )
        else:
            lines = (jnp.sum(squared, 1, keepdims=True),)
        for part, line in enumerate(lines):
            spot = (index + (index > 0) + part) * 128
            sums_ref[:data, spot : spot + 128] = put(data, block, across(line))
    sums_ref[:data, 512:640] = put(data, block, squares_ref[...])
    at_group += 3 * groups
    lines = jnp.zeros((groups, expand_bias_ref.shape[2]), f32)
    for distance in range(groups):
        lines = lines + put(groups, own ^ distance, expand_bias_ref[distance])
    sums_ref[at_group : at_group + groups, :] = lines
    count = heads_far_ref.shape[1] // 2
    for part in range(2):
        span = slice(part * count, (part + 1) * count)
        lines = jnp.zeros((groups, share), f32)
        for ref, order in ((heads_far_ref, (3, 1)), (heads_near_ref, (2, 0))):
            for step, distance in enumerate(order):
                total = jnp.sum(ref[step][span], 0, keepdims=True)
                lines = lines + put(groups, own ^ distance, total)
        sums_ref[part * groups : (part + 1) * groups, 3 * share :] = lines
    stem_bias = jnp.sum(vector_one_ref[8 : 8 + patch_count, :], 0, keepdims=True)
    singles = (stem_bias, vector_one_ref[0:2, :], vector_two_ref[0:3, :])
    for line in singles:
        sums_ref[at_single : at_single + line.shape[0], :] = line
        at_single += line.shape[0]


def vector_kernel(
    place_ref,
    sums_ref,
    last_ref,
    head_ref,
    vectors_ref,
    second_ref,
    grad_out,
    new_out,
    second_out,
    grad_ref,
    lines_ref,
    *,
    data,
    groups,
    share,
):
    to_lines(second_ref, lines_ref)
    length = second_ref.shape[0]
    _, at_group, at_single, _ = layout(data, groups)
    width = vectors_ref.shape[1]

    def single(index):
        return sums_ref[at_single + index : at_single + index + 1, :]

    def joined(part):
        lines = sums_ref[part * groups : (part + 1) * groups, 3 * share :]
        return jnp.concatenate([lines[g : g + 1] for g in range(groups)], 1)

    grad_ref[...] = jnp.zeros(grad_ref.shape, f32)
    spot = at_group + 3 * groups
    rest = CLASSES - width
    for index, value in (
        (STEM_BIAS, single(0)),
        (GAIN_ONE, single(1)),
        (SHIFT_ONE, single(2)),
        (QUERY_BIAS, joined(0)),
        (VALUE_BIAS, joined(1)),
        (ATTEND_BIAS, single(3)),
        (GAIN_TWO, single(4)),
        (SHIFT_TWO, single(5)),
        (EXPAND_BIAS, sums_ref[spot : spot + groups, :]),
        (CONTRACT_BIAS, last_ref[0:3, :]),
        (HEAD_BIAS, head_ref[0:1, :width]),
    ):
        grad_ref[index : index + value.shape[0], :] = value
    grad_ref[HEAD_BIAS + 1 : HEAD_BIAS + 2, :rest] = head_ref[0:1, width:]
    grad = grad_ref[...]
    row = lax.broadcasted_iota(jnp.int32, grad.shape, 0)
    lane = lax.broadcasted_iota(jnp.int32, grad.shape, 1)
    valid = row * width + lane < length
    second = decay_rate * lines_ref[...] + (1.0 - decay_rate) * (grad * grad + eps_one)
    update = grad * lax.rsqrt(jnp.where(valid, second, 1.0))
    total = jnp.sum(update * update, keepdims=True) / length
    square = jnp.sum(vectors_ref[...] * vectors_ref[...], keepdims=True) / length
    scale = step_rate * jnp.maximum(eps_two, jnp.sqrt(square))
    scale = scale / jnp.maximum(1.0, jnp.sqrt(total) / clip_level)
    from_lines(grad, grad_out)
    from_lines(vectors_ref[...] - scale * update, new_out)
    from_lines(second, second_out)


def renew_kernel(
    place_ref,
    sums_ref,
    in_rows_ref,
    out_cols_ref,
    expand_rows_ref,
    contract_cols_ref,
    in_cols_ref,
    out_rows_ref,
    expand_cols_ref,
    contract_rows_ref,
    attend_ref,
    expand_ref,
    contract_ref,
    in_rows_out,
    out_cols_out,
    expand_rows_out,
    contract_cols_out,
    in_cols_out,
    out_rows_out,
    expand_cols_out,
    contract_rows_out,
    update_ref,
    scalar_ref,
    square_ref,
    rows_new_ref,
    cols_new_ref,
    *,
    data,
    groups,
    share,
):
    block, group = place_ref[4], place_ref[5]
    size = attend_ref.shape[0]
    width = attend_ref.shape[1]
    _, at_group, _, _ = layout(data, groups)
    length, hidden = data * size, groups * width
    lane = lax.broadcasted_iota(jnp.int32, (1, width), 1)
    first = lane < 3 * share
    spare = lax.broadcasted_iota(jnp.int32, (1, 128), 1) < size
    for index, ref in enumerate((in_rows_ref, out_cols_ref, expand_rows_ref, contract_cols_ref)):
        for part in range(data):
            values = ref[pl.ds(part * size, size)].reshape(1, size)
            rows_new_ref[part : part + 1, index * 128 : index * 128 + size] = values
    for part in range(groups):
        span = slice(part * share, (part + 1) * share)
        for which in range(3):
            cols_new_ref[part : part + 1, which * share : (which + 1) * share] = in_cols_ref[
                which : which + 1, span
            ]
        values = out_rows_ref[pl.ds(part * share, share)].reshape(1, share)
        cols_new_ref[part : part + 1, 3 * share :] = values
        for index, ref in enumerate((expand_cols_ref, contract_rows_ref), 1):
            values = ref[pl.ds(part * width, width)].reshape(1, width)
            cols_new_ref[index * groups + part : index * groups + part + 1, :] = values
    counts = (3 * length, length, hidden, hidden)
    means = []
    for index, count in enumerate(counts):
        span = slice(index * 128, (index + 1) * 128)
        new = decay_rate * rows_new_ref[:, span]
        new = new + (1.0 - decay_rate) * (sums_ref[:data, span] / count)
        rows_new_ref[:, span] = new
        means.append(jnp.sum(jnp.where(spare, new, 0.0), keepdims=True) / length)
        out = (in_rows_out, out_cols_out, expand_rows_out, contract_cols_out)[index]
        for part in range(data):
            out[pl.ds(part * size, size)] = new[part, :size]
    for index, count in enumerate((length, length, length)):
        span = slice(index * groups, (index + 1) * groups)
        lines = sums_ref[at_group + index * groups : at_group + (index + 1) * groups, :]
        new = decay_rate * cols_new_ref[span, :] + (1.0 - decay_rate) * (lines / count)
        cols_new_ref[span, :] = new
        for part in range(groups):
            if index == 0:
                for which in range(3):
                    in_cols_out[which : which + 1, part * share : (part + 1) * share] = new[
                        part : part + 1, which * share : (which + 1) * share
                    ]
                out_rows_out[pl.ds(part * share, share)] = new[part, 3 * share :]
            else:
                out = (expand_cols_out, contract_rows_out)[index - 1]
                out[pl.ds(part * width, width)] = new[part]
        if index == 0:
            means[1] = jnp.sum(jnp.where(first, 0.0, new), keepdims=True) / length
        if index == 2:
            means[3] = jnp.sum(new, keepdims=True) / hidden
    scalars = jnp.zeros((1, 128), f32)
    place_lane = lax.broadcasted_iota(jnp.int32, (1, 128), 1)
    for index, ref in enumerate((attend_ref, expand_ref, contract_ref)):
        across_row = pick(cols_new_ref[index * groups : (index + 1) * groups, :], group)

        def row(which):
            span = slice(which * 128, (which + 1) * 128)
            return down(pick(rows_new_ref[:, span], block), size)

        if index == 0:
            denominator = jnp.where(
                first, row(0) * across_row / means[0], row(1) * across_row / means[1]
            )
        else:
            denominator = row(index + 1) * across_row / means[index + 1]
        update = ref[...] * lax.rsqrt(denominator)
        update_ref[index] = update
        squared = update * update
        if index == 0:
            totals = (jnp.where(first, squared, 0.0), jnp.where(first, 0.0, squared))
        else:
            totals = (squared,)
        for part, total in enumerate(totals):
            spot = index + (index > 0) + part
            scalars = jnp.where(place_lane == spot, jnp.sum(total, keepdims=True), scalars)
    scalar_ref[...] = jnp.broadcast_to(scalars, scalar_ref.shape)
    squares = jnp.sum(sums_ref[:data, 512:640], 0, keepdims=True)
    square_ref[...] = jnp.broadcast_to(squares, square_ref.shape)


def step_kernel(
    place_ref,
    update_ref,
    scalar_ref,
    square_ref,
    attend_ref,
    expand_ref,
    contract_ref,
    in_ref,
    in_low_ref,
    out_ref,
    out_low_ref,
    expand_new_ref,
    expand_low_ref,
    contract_new_ref,
    contract_low_ref,
    *,
    sizes,
):
    share = in_ref.shape[2]
    scales = []
    for index, size in enumerate(sizes):
        total = scalar_ref[0:1, index : index + 1]
        square = square_ref[0:1, index : index + 1]
        clip = jnp.maximum(1.0, jnp.sqrt(total / size) / clip_level)
        scales.append(step_rate * jnp.maximum(eps_two, jnp.sqrt(square / size)) / clip)
    lane = lax.broadcasted_iota(jnp.int32, (1, attend_ref.shape[1]), 1)
    scale = jnp.where(lane < 3 * share, scales[0], scales[1])
    attend = attend_ref[...] - scale * update_ref[0]
    for part in range(3):
        lines = attend[:, part * share : (part + 1) * share]
        in_ref[part] = lines
        in_low_ref[part] = lines.astype(bf16)
    out = attend[:, 3 * share :].T
    out_ref[...] = out
    out_low_ref[...] = out.astype(bf16)
    expand = expand_ref[...] - scales[2] * update_ref[1]
    expand_new_ref[...] = expand
    expand_low_ref[...] = expand.astype(bf16)
    contract = contract_ref[...] - scales[3] * update_ref[2]
    contract_new_ref[...] = contract
    contract_low_ref[...] = contract.astype(bf16)


def call(
    body, order, place, operands, results, scratch=(), flops=0, weights=None, limit=48
):
    steps = len(order)
    pieces = weights is not None and len(weights) == 4

    def distance(step):
        at = order[0]
        for index, value in enumerate(order[1:], 1):
            at = jnp.where(step == index, value, at)
        return at

    def spec(shape, mark):
        zeros = (0,) * (len(shape) - 1)
        if mark == "any":
            return pl.BlockSpec(memory_space=pl.ANY)
        if mark == "smem":
            return pl.BlockSpec(memory_space=pltpu.SMEM)
        if mark is False:
            return pl.BlockSpec(shape, lambda g, p: (0,) + zeros)
        if mark is True:
            return pl.BlockSpec(
                (1,) + shape[1:], lambda g, p: ((p[2] * 2 + p[3]) ^ distance(g),) + zeros
            )
        if mark == "far":
            return pl.BlockSpec((1,) + shape[1:], lambda g, p: (distance(g),) + zeros)
        return pl.BlockSpec((1,) + shape[1:], lambda g, p: (mark(g),) + zeros)

    operands, scratch = tuple(operands), tuple(scratch)
    kernel = body
    if weights is not None:
        operands = tuple((weight, "any" if pieces else True) for weight in weights) + operands
    if pieces:
        some = weights[0]
        height, width = some.shape[0] * some.shape[1] * some.shape[2], some.shape[3]
        full = (steps, some.shape[1], some.shape[0]) + some.shape[2:]
        scratch += ((full, some.dtype), ((steps, 2), None))

        def kernel(place_ref, *refs):
            full_ref, sems = refs[-2:]
            step = pl.program_id(0)
            copies = [
                (r, group_copies(place_ref, refs[:4], full_ref.at[i], sems.at[i], r))
                for i, r in enumerate(order)
            ]

            @pl.when(step == 0)
            def _():
                for distance, choices in copies:
                    each_copy(place_ref, distance, choices, start_copy)

            for index in range(steps):

                @pl.when(step == index)
                def _(index=index):
                    each_copy(place_ref, *copies[index], wait_copy)

            def weight(start=0, stop=width):
                return full_ref[step, :, :, :, start:stop].reshape(height, stop - start)

            body(place_ref, weight, *refs[4:-2])

    elif weights is not None:

        def kernel(place_ref, weight_ref, *refs):
            def weight(start=0, stop=weight_ref.shape[2]):
                return weight_ref[0, :, start:stop]

            body(place_ref, weight, *refs)

    return pl.pallas_call(
        kernel,
        grid_spec=pltpu.PrefetchScalarGridSpec(
            num_scalar_prefetch=1,
            grid=(steps,),
            in_specs=[spec(value.shape, mark) for value, mark in operands],
            out_specs=[spec(shape, mark) for shape, _, mark in results],
            scratch_shapes=[
                pltpu.SemaphoreType.DMA(shape) if kind is None else pltpu.VMEM(shape, kind)
                for shape, kind in scratch
            ],
        ),
        out_shape=[jax.ShapeDtypeStruct(shape, kind) for shape, kind, _ in results],
        compiler_params=pltpu.CompilerParams(vmem_limit_bytes=limit * 1024 * 1024),
        cost_estimate=pl.CostEstimate(flops=flops, bytes_accessed=16_000_000, transcendentals=0),
    )(place, *[value for value, _ in operands])


def local(
    patches,
    keep_mask,
    labels,
    stem_weight,
    position_table,
    attend_in,
    attend_out,
    expand,
    contract,
    head_weight,
    vectors,
    stem_rows,
    stem_cols,
    table_rows,
    table_cols,
    attend_in_rows,
    attend_in_cols,
    attend_out_rows,
    attend_out_cols,
    expand_rows,
    expand_cols,
    contract_rows,
    contract_cols,
    head_rows,
    head_cols,
    vector_second,
):
    data_size, model_size = lax.axis_size("dp"), lax.axis_size("mp")
    links = Grid() if (data_size, model_size) == (8, 4) else Plain(data_size, model_size)
    here = links.place
    count, patch_count, _ = patches.shape
    groups = model_size
    pair = groups // 2
    image_count = count * data_size * model_size
    inverse_count = 1.0 / image_count
    row_share, _, head_share = attend_in.shape
    hidden_share = expand.shape[1]
    in_share = 3 * head_share
    slots = patch_count + 1
    padded = -(-slots // 16) * 16
    rows = count * padded
    contract_own = contract.T
    attend_own, attend_piece, expand_piece, contract_piece, squares, vector_lines = call(
        pieces_kernel,
        (0,),
        here,
        (
            (attend_in.swapaxes(0, 1), False),
            (attend_out, False),
            (expand, False),
            (contract_own, False),
            (vectors, False),
        ),
        (((row_share, D), f32, False),)
        + (((row_share, D), bf16, False),) * 3
        + (((1, 128), f32, False), ((24, D), f32, False)),
        limit=60,
    )
    attend_chain = Chain(links.gather(attend_piece))
    pixels = jnp.pad(patches, ((0, 0), (0, padded - patch_count), (0, 0))).reshape(rows, -1)
    pixels, vector_lines, expand_piece, contract_piece, head_weight = sync(
        [attend_chain], pixels, vector_lines, expand_piece, contract_piece, head_weight
    )
    expand_chain = Chain(links.gather(expand_piece))
    stream_zero, rows_one, present, facts = call(
        stem_kernel,
        (0,),
        here,
        (
            (labels, "smem"),
            (after(pixels, attend_chain.sent), False),
            (stem_weight, False),
            (position_table, False),
            (vector_lines, False),
            (keep_mask, False),
        ),
        (
            ((rows, D), f32, False),
            ((rows, D), bf16, False),
            ((count, padded), f32, False),
            ((2 * count, 128), f32, False),
        ),
        flops=2 * rows * D * D,
    )
    stream_zero, rows_one, contract_piece, head_weight = sync(
        [attend_chain, expand_chain],
        stream_zero,
        rows_one,
        contract_piece,
        head_weight,
    )
    contract_chain = Chain(links.gather(contract_piece))
    head_turned = head_weight.T
    head_low = head_turned.astype(bf16)

    head_low = sync([attend_chain, expand_chain, contract_chain], head_low)
    sync([attend_chain], contract_chain.sent, expand_chain.sent)
    attend_all = attend_chain.result
    every = tuple(range(groups))

    qkv, attended, stream_one, rows_two, stream_sum = call(
        functools.partial(attend_kernel, order=every),
        every,
        here,
        (
            (rows_one, False),
            (vector_lines, False),
            (present, False),
            (stream_zero, False),
        ),
        (
            ((groups, 3, rows, head_share), bf16, "far"),
            ((groups, rows, head_share), bf16, "far"),
            ((rows, D), f32, False),
            ((rows, D), bf16, False),
            ((2 * count, D), f32, False),
        ),
        flops=2 * rows * D * 4 * D,
        weights=attend_all,
    )
    rows_two, stream_sum = sync([expand_chain, contract_chain], rows_two, stream_sum)
    rows_two = sync([expand_chain], rows_two)
    expand_all = expand_chain.result
    active_sum, slope = call(
        functools.partial(hidden_kernel, order=every),
        every,
        here,
        (
            (rows_two, False),
            (vector_lines, False),
            (present, False),
        ),
        (
            ((groups, 2 * count, hidden_share), f32, "far"),
            ((groups, rows, hidden_share), bf16, "far"),
        ),
        (((rows, 1), f32),),
        flops=2 * rows * D * FF,
        weights=expand_all,
    )
    active_sum, slope = sync([contract_chain], active_sum, slope)
    active_sum, slope = sync([contract_chain], active_sum, slope)

    contract_all = contract_chain.result
    scratch = ()
    if len(contract_all) == 4:
        scratch = (
            ((groups, data_size // 2, 2, row_share, hidden_share), bf16),
            ((groups, 2), None),
        )
    piece, d_row, d_active_row = call(
        functools.partial(own_head_kernel, inverse_count=inverse_count),
        (0,),
        here,
        tuple((value, False) for value in (active_sum, stream_sum, facts, vector_lines, head_low))
        + tuple((value, "any" if scratch else False) for value in contract_all),
        (
            ((8 * count, D + 128), bf16, False),
            ((2 * count, D), f32, False),
            ((groups, 2 * count, hidden_share), f32, False),
        ),
        scratch,
    )

    pieces_chain = Chain(links.gather(piece))
    far_grad, near_grad, expand_bias_grad, d_rows_two = call(
        expand_back_kernel,
        (3, 1, 2, 0),
        here,
        (
            (rows_two, False),
            (slope, "far"),
            (d_active_row, "far"),
        ),
        (
            ((pair, D, hidden_share), bf16, lambda g: jnp.minimum(g, pair - 1)),
            ((pair, D, hidden_share), bf16, lambda g: jnp.maximum(g - pair, 0)),
            ((groups, 1, hidden_share), f32, "far"),
            ((rows, D), f32, False),
        ),
        (((rows, hidden_share), bf16),),
        flops=4 * rows * D * FF,
        weights=expand_all,
    )
    far_grad, near_grad, d_rows_two = sync([pieces_chain], far_grad, near_grad, d_rows_two)
    expand_sum = Chain(links.reduce(far_grad))
    d_stream, d_attend_low, vector_two = call(
        between_kernel,
        (0,),
        here,
        (
            (d_rows_two, False),
            (d_row, False),
            (present, False),
            (stream_one, False),
            (vector_lines, False),
        ),
        (
            ((rows, D), f32, False),
            ((rows, D), bf16, False),
            ((8, D), f32, False),
        ),
    )

    d_stream, d_attend_low = sync(
        [pieces_chain, (expand_sum, near_grad)], d_stream, d_attend_low
    )

    def attend_back(order, *before):
        return call(
            attend_back_kernel,
            order,
            here,
            (
                (rows_one, False),
                (qkv, "far"),
                (attended, "far"),
                (present, False),
                (d_attend_low, False),
            )
            + tuple((value, False) for value in before),
            (
                ((pair, D, D), bf16, lambda g: g),
                ((pair, 2 * count, head_share), f32, lambda g: g),
                ((rows, D), f32, False),
            ),
            (((rows, 3 * head_share), bf16), ((rows, 1), f32)),
            flops=2 * rows * D * 4 * D,
            weights=attend_all,
        )

    far_grad, heads_far, d_rows_one = attend_back((3, 1))
    far_grad, d_rows_one = sync([pieces_chain, expand_sum], far_grad, d_rows_one)
    attend_sum = Chain(links.reduce(far_grad))
    near_grad, heads_near, d_rows_one = attend_back((2, 0), d_rows_one)
    d_rows_one = sync([pieces_chain, expand_sum, (attend_sum, near_grad)], d_rows_one)
    both_far, both_near, vector_one = call(
        stem_back_kernel,
        (0,),
        here,
        (
            (after(d_rows_one, attend_sum.sent, expand_sum.sent), False),
            (d_stream, False),
            (stream_zero, False),
            (vector_lines, False),
            (pixels, False),
        ),
        (
            ((4, 128, D), bf16, False),
            ((4, 128, D), bf16, False),
            ((8 + padded, D), f32, False),
        ),
        flops=2 * rows * D * D,
    )
    pieces, both_far, both_near = sync(
        [attend_sum, expand_sum], pieces_chain.result, both_far, both_near
    )
    grad_expand = expand_sum.result
    both_sum = Chain(links.add_large(both_far, both_near))
    pieces = links.whole(*pieces).reshape((-1,) + piece.shape)
    pieces, grad_expand = sync([attend_sum, both_sum], pieces, grad_expand)
    steps = max(1, pieces.shape[0] // 32)
    head_new, head_rows_new, head_cols_new, grad_contract, vector_last, vector_head = call(
        functools.partial(all_head_kernel, inverse_count=inverse_count),
        (0,) * steps,
        here,
        (
            (pieces.reshape((steps, -1) + piece.shape), lambda g: g),
            (vector_lines, False),
            (head_low, False),
            (head_turned, False),
            (head_rows, False),
            (head_cols, False),
        ),
        (
            ((CLASSES, D), f32, False),
            ((D,), f32, False),
            ((CLASSES,), f32, False),
            ((row_share, hidden_share), f32, False),
            ((8, D), f32, False),
            ((8, CLASSES), f32, False),
        ),
        (((CLASSES, D), f32),),
    )
    loss_sum = vector_head[1, 0]
    grad_expand, grad_contract = sync([attend_sum, both_sum], grad_expand, grad_contract)
    grad_attend = attend_sum.result

    names = dict(data=data_size, groups=groups, share=head_share)
    lines = layout(data_size, groups)[3]
    (sums,) = call(
        functools.partial(sums_kernel, patch_count=patch_count, **names),
        (0,),
        here,
        tuple(
            (value, False)
            for value in (
                grad_attend,
                grad_expand,
                grad_contract,
                squares,
                vector_one,
                vector_two,
                expand_bias_grad,
                heads_far,
                heads_near,
            )
        ),
        (((lines, D), f32, False),),
    )
    sums_chain = Chain(links.add(sums))
    for _ in range(5):
        sync([sums_chain, both_sum])
    sums = sums_chain.result
    statistics = (
        attend_in_rows,
        attend_out_cols,
        expand_rows,
        contract_cols,
        attend_in_cols,
        attend_out_rows,
        expand_cols,
        contract_rows,
    )
    *statistics, update, scalars, square_totals = call(
        functools.partial(renew_kernel, **names),
        (0,),
        here,
        tuple(
            (value, False)
            for value in (sums,) + statistics + (grad_attend, grad_expand, grad_contract)
        ),
        tuple((value.shape, f32, False) for value in statistics)
        + (
            ((3, row_share, D), f32, False),
            ((8, 128), f32, False),
            ((8, 128), f32, False),
        ),
        (((data_size, 512), f32), ((3 * groups, D), f32)),
    )
    (
        in_rows_new,
        out_cols_new,
        expand_rows_new,
        contract_cols_new,
        in_cols_new,
        out_rows_new,
        expand_cols_new,
        contract_rows_new,
    ) = statistics
    scalars_chain = Chain(links.add(scalars))
    sums = sync([scalars_chain, both_sum], sums)
    stem_new, stem_rows_new, stem_cols_new, table_new, table_rows_new, table_cols_new = call(
        functools.partial(stem_step_kernel, padded=padded),
        (0,),
        here,
        tuple(
            (value, False)
            for value in both_sum.result
            + (stem_weight, stem_rows, stem_cols, position_table, table_rows, table_cols)
        ),
        tuple(
            (value.shape, f32, False)
            for value in (stem_weight, stem_rows, stem_cols, position_table, table_rows, table_cols)
        ),
        (((1024, D), bf16),),
    )
    stem_new, sums = sync([scalars_chain], stem_new, sums)
    grad_vector, vectors_new, second_new = call(
        functools.partial(vector_kernel, **names),
        (0,),
        here,
        tuple(
            (value, False) for value in (sums, vector_last, vector_head, vector_lines, vector_second)
        ),
        ((vectors.shape, f32, False),) * 3,
        (((24, D), f32), ((24, D), f32)),
    )
    vectors_new = sync([scalars_chain], vectors_new)
    sync([scalars_chain])
    sync([scalars_chain])
    block = call(
        functools.partial(step_kernel, sizes=(3 * D * D, D * D, D * FF, FF * D)),
        (0,),
        here,
        tuple(
            (value, False)
            for value in (
                update,
                scalars_chain.result,
                square_totals,
                attend_own,
                expand,
                contract_own,
            )
        ),
        tuple(
            (shape, kind, False)
            for shape in (
                (3, row_share, head_share),
                (head_share, row_share),
                (row_share, hidden_share),
                (row_share, hidden_share),
            )
            for kind in (f32, bf16)
        ),
    )
    in_new, in_copy, out_new, out_copy, expand_new, expand_copy, contract_new, contract_copy = block

    return (
        loss_sum,
        stem_new,
        stem_rows_new,
        stem_cols_new,
        table_new,
        table_rows_new,
        table_cols_new,
        in_new.swapaxes(0, 1),
        in_copy.swapaxes(0, 1),
        in_rows_new,
        in_cols_new,
        out_new,
        out_copy,
        out_rows_new,
        out_cols_new,
        expand_new,
        expand_copy,
        expand_rows_new,
        expand_cols_new,
        contract_new.T,
        contract_copy.T,
        contract_rows_new,
        contract_cols_new,
        head_new.T,
        head_rows_new,
        head_cols_new,
        vectors_new,
        grad_vector,
        second_new,
    )


def solution(mesh):
    placed = (
        P(ALL, None, None),
        P(ALL, None),
        P(ALL),
        P(),
        P(),
        P("dp", None, "mp"),
        P("mp", "dp"),
        P("dp", "mp"),
        P("mp", "dp"),
    ) + (P(),) * 17
    block = (P("dp", None, "mp"), P("mp", "dp"), P("dp", "mp"), P("mp", "dp"))
    given = [P()] * 7
    for spec in block:
        given += [spec, spec, P(), P()]
    given += [P()] * 6
    return jax.shard_map(
        local, mesh=mesh, in_specs=placed, out_specs=tuple(given), check_vma=False
    )
```

```python
import functools

import jax
import jax.numpy as jnp
from jax import lax
from jax.experimental import pallas as pl
from jax.experimental.pallas import tpu as pltpu
from jax.sharding import PartitionSpec as P

D = 768
HEAD_DIM = 64
FF = 3072
CLASSES = 1000

eps_norm = 1e-06
eps_one = 1e-30
eps_two = 0.001
decay_rate = 0.5
clip_level = 0.3
step_rate = 1.0
smoothing = 0.1

ALL = ("dp", "mp")
f32 = jnp.float32
bf16 = jnp.bfloat16


def after(value, *others):
    return lax.optimization_barrier((value,) + others)[0]


class Chain:
    def __init__(self, stages):
        self.stages = stages
        self.result = None
        self.sent, self.flight = next(stages)

    def advance(self, arrived):
        try:
            self.sent, self.flight = self.stages.send(arrived)
        except StopIteration as end:
            self.sent, self.flight, self.result = (), (), end.value


def sync(chains, *values):
    chains = [chain if isinstance(chain, tuple) else (chain,) for chain in chains]
    flights = [(chain[0].flight,) + chain[1:] for chain in chains]
    flights, values = lax.optimization_barrier((flights, values))
    for chain, flight in zip(chains, flights):
        chain[0].advance(flight if len(flight) > 1 else flight[0])
    return values[0] if len(values) == 1 else values


class Plain:
    blocks = None

    def __init__(self, rows, cols):
        self.rows, self.cols = rows, cols
        self.place = jnp.stack(
            [jnp.zeros((), jnp.int32)] * 4
            + [lax.axis_index("dp"), lax.axis_index("mp"), jnp.zeros((), jnp.int32)]
            + [jnp.full((), 4, jnp.int32)]
        ).astype(jnp.int32)

    def gather(self, piece):
        full = lax.all_gather(piece, ALL, axis=0)
        full = full.reshape((self.rows, self.cols) + piece.shape).swapaxes(0, 1)
        for _ in range(4):
            yield (), ()
        return (full.reshape(self.cols, self.rows * piece.shape[0], piece.shape[1]),)

    def whole(self, full):
        return full

    def reduce(self, far):
        _, near = yield (), ()
        grads = jnp.stack([near[1], far[1], near[0], far[0]])
        grads = grads.reshape(self.cols, self.rows, -1, grads.shape[2])
        grads = grads.swapaxes(0, 1).reshape((-1,) + grads.shape[2:])
        total = lax.psum_scatter(grads, ALL, scatter_dimension=0).astype(f32)
        for _ in range(3):
            total = yield (), total
        return total

    def add(self, values):
        values = lax.psum(values, ALL)
        for _ in range(5):
            values = yield (), values
        return values

    def add_large(self, far, near):
        values = lax.psum((near, far), ALL)
        for _ in range(8):
            values = yield (), values
        return values


def group_copies(place_ref, piece_refs, full_ref, sems, distance):
    near_ref, far_ref = piece_refs[2:] if distance % 2 else piece_refs[:2]
    flip = distance // 2
    x = place_ref[1]
    source = far_ref if flip else near_ref
    along_y = [
        pltpu.make_async_copy(source.at[0], full_ref.at[:, x], sems.at[0]),
        pltpu.make_async_copy(source.at[1], full_ref.at[:, 1 - x], sems.at[1]),
    ]
    along_x = [
        pltpu.make_async_copy(near_ref.at[flip], full_ref.at[:, x], sems.at[0]),
        pltpu.make_async_copy(far_ref.at[flip], full_ref.at[:, 1 - x], sems.at[1]),
    ]
    return along_y, along_x


def each_copy(place_ref, distance, choices, act):
    owner = place_ref[3] ^ (distance % 2)
    for core in range(2):

        @pl.when(owner == core)
        def _(copies=choices[core]):
            for copy in copies:
                act(copy)


def start_copy(copy):
    copy.start()


def wait_copy(copy):
    copy.wait()


def column_kernel(place_ref, *refs):
    *piece_refs, column_ref = refs
    for step, ref in enumerate(piece_refs):
        column_ref[0, lax.rem(place_ref[0] + step, len(piece_refs))] = ref[...]


class Grid:
    deep, devices, blocks = 4, 32, 8

    def __init__(self):
        dp, mp = lax.axis_index("dp"), lax.axis_index("mp")
        self.z, self.x, self.y, self.core = dp // 2, dp % 2, mp // 2, mp % 2
        self.at_first = jnp.where(self.core == 0, self.y, self.x)
        self.at_second = jnp.where(self.core == 0, self.x, self.y)
        chunk = self.core * 4 + self.at_first * 2 + self.at_second
        other_chunk = (1 - self.core) * 4 + self.at_second * 2 + self.at_first
        self.place = jnp.stack([self.z, self.x, self.y, self.core, dp, mp, chunk, other_chunk])
        self.place = self.place.astype(jnp.int32)
        self.other = self.pairs(lambda z, x, y, c: (z, x, y, 1 - c))
        self.first = self.pairs(lambda z, x, y, c: (z, x ^ c, y ^ (1 - c), c))
        self.second = self.pairs(lambda z, x, y, c: (z, x ^ (1 - c), y ^ c, c))
        self.along_x = self.pairs(lambda z, x, y, c: (z, 1 - x, y, c))
        self.along_y = self.pairs(lambda z, x, y, c: (z, x, 1 - y, c))
        self.up = [self.pairs(lambda z, x, y, c, s=s: ((z + s) % 4, x, y, c)) for s in range(4)]
        self.flip_z = [self.pairs(lambda z, x, y, c, s=s: (z ^ s, x, y, c)) for s in range(4)]

    def pairs(self, move):
        table = []
        for index in range(self.devices):
            z, x, y, c = move(index // 8, index // 4 % 2, index // 2 % 2, index % 2)
            table.append((index, ((z * 2 + x) * 2 + y) * 2 + c))
        return table

    @staticmethod
    def send(values, table):
        return lax.ppermute(values, ALL, table)

    def gather(self, piece):
        got = yield piece, [self.send(piece, self.up[-s]) for s in (1, 2, 3)]
        column = pl.pallas_call(
            column_kernel,
            in_specs=[pl.BlockSpec(memory_space=pltpu.SMEM)]
            + [pl.BlockSpec(memory_space=pltpu.VMEM)] * self.deep,
            out_specs=pl.BlockSpec(memory_space=pltpu.VMEM),
            out_shape=jax.ShapeDtypeStruct((1, self.deep) + piece.shape, piece.dtype),
        )(self.place, piece, *got)
        got = yield column, self.send(column, self.second)
        pair = jnp.concatenate([column, got])
        rest, theirs = yield pair, (self.send(pair, self.first), self.send(pair, self.other))
        rest_theirs = yield rest, self.send(rest, self.other)
        return pair, rest, theirs, rest_theirs

    def whole(self, *pieces):
        blocks, (r, c) = self.blocks, pieces[0].shape[2:]

        def body(place_ref, *refs):
            full_ref, sems = refs[-2:]
            own = place_ref[2] * 2 + place_ref[3]
            groups = [
                (i, group_copies(place_ref, refs[:4], full_ref.at[own ^ i], sems.at[i], i))
                for i in range(4)
            ]
            for act in (start_copy, wait_copy):
                for distance, choices in groups:
                    each_copy(place_ref, distance, choices, act)

        full = pl.pallas_call(
            body,
            in_specs=[pl.BlockSpec(memory_space=pltpu.SMEM)]
            + [pl.BlockSpec(memory_space=pl.ANY)] * 4,
            out_specs=pl.BlockSpec(memory_space=pltpu.VMEM),
            out_shape=jax.ShapeDtypeStruct((4, self.deep, 2, r, c), pieces[0].dtype),
            scratch_shapes=[pltpu.SemaphoreType.DMA((4, 2))],
            compiler_params=pltpu.CompilerParams(vmem_limit_bytes=60 * 1024 * 1024),
        )(self.place, *pieces)
        return full.reshape(4, blocks * r, c)

    def reduce(self, far):
        theirs, near = yield far, self.send(far, self.other)
        size, width = near.shape[1] // self.blocks, near.shape[2]
        near = near.reshape(2, self.deep, 2, size, width)
        theirs = theirs.reshape(near.shape)

        def chip(y, x):
            spot, part = (y, 0, x, 0, 0), (1, self.deep, 1, size, width)
            total = lax.dynamic_slice(near, spot, part).astype(f32)
            total = total + lax.dynamic_slice(theirs, spot, part).astype(f32)
            return total.reshape(self.deep, size, width)

        sent = jnp.stack(
            [chip(0, 1 - self.x), chip(self.core, jnp.where(self.core == 0, self.x, 1 - self.x))]
        ).astype(bf16)
        got = yield sent, self.send(sent, self.first)
        kept = chip(1 - self.core, jnp.where(self.core == 0, 1 - self.x, self.x))
        away = (kept + got[0].astype(f32)).astype(bf16)
        came = yield away, self.send(away, self.second)
        column = chip(1, self.x) + got[1].astype(f32) + came.astype(f32)
        low = column.astype(bf16)

        def level(values, step):
            return lax.dynamic_index_in_dim(values, (self.z + step) % 4, 0, keepdims=False)

        total = level(column, 0)
        for part in (yield low, [self.send(level(low, s), self.up[s]) for s in (1, 2, 3)]):
            total = total + part.astype(f32)
        return total

    def add(self, values):
        for table in (self.other, self.along_y, self.along_x, self.flip_z[1], self.flip_z[2]):
            values = values + (yield values, self.send(values, table))
        return values

    def add_large(self, far, near):
        parts = [near, (yield far, self.send(far, self.other))]

        def total(start, stop):
            return sum(part[start:stop].astype(f32) for part in parts)

        for table, half in ((self.first, 2), (self.second, 1)):
            sent = total(half, 2 * half).astype(bf16)
            parts = [part[:half] for part in parts] + [(yield sent, self.send(sent, table))]
        pile = total(0, 1).astype(bf16)
        for table in (self.flip_z[1], self.flip_z[2]):
            got = yield pile, self.send(pile, table)
            pile = (pile.astype(f32) + got.astype(f32)).astype(bf16)
        for table in (self.second, self.first):
            pile = jnp.concatenate([pile, (yield pile, self.send(pile, table))])
        return pile, (yield pile, self.send(pile, self.other))


def normal_parts(values):
    centred = values - jnp.mean(values, -1, keepdims=True)
    inverse = lax.rsqrt(jnp.mean(centred * centred, -1, keepdims=True) + eps_norm)
    return centred * inverse, inverse


def pull_normal(values, gain, grads):
    hat, inverse = normal_parts(values)
    scaled = grads * gain
    mean_one = jnp.mean(scaled, -1, keepdims=True)
    mean_two = jnp.mean(scaled * hat, -1, keepdims=True)
    below = (scaled - mean_one - hat * mean_two) * inverse
    return below, jnp.sum(grads * hat, 0, keepdims=True), jnp.sum(grads, 0, keepdims=True)


STEM_BIAS, GAIN_ONE, SHIFT_ONE, QUERY_BIAS, VALUE_BIAS, ATTEND_BIAS, GAIN_TWO, SHIFT_TWO = range(8)
EXPAND_BIAS, CONTRACT_BIAS, GAIN_LAST, SHIFT_LAST, HEAD_BIAS = 8, 12, 13, 14, 15


def line(vectors_ref, index):
    return vectors_ref[index : index + 1, :]


def to_column(present_ref, column_ref):
    padded = present_ref.shape[1]
    for image in range(present_ref.shape[0]):
        span = slice(image * padded, (image + 1) * padded)
        column_ref[span, :] = upright(present_ref[image : image + 1, :])


def to_lines(flat_ref, lines_ref):
    width = lines_ref.shape[1]
    lines_ref[...] = jnp.zeros(lines_ref.shape, f32)
    for row, start in enumerate(range(0, flat_ref.shape[0], width)):
        extent = min(width, flat_ref.shape[0] - start)
        values = flat_ref[pl.ds(start, extent)]
        lines_ref[row : row + 1, :extent] = values.reshape(1, extent)


def from_lines(lines, flat_ref):
    width = lines.shape[1]
    for row, start in enumerate(range(0, flat_ref.shape[0], width)):
        extent = min(width, flat_ref.shape[0] - start)
        flat_ref[pl.ds(start, extent)] = lines[row, :extent]


def share_of(vectors_ref, index, group, share):
    result = vectors_ref[index : index + 1, :share]
    for other in range(1, vectors_ref.shape[1] // share):
        part = vectors_ref[index : index + 1, other * share : (other + 1) * share]
        result = jnp.where(group == other, part, result)
    return result


def own_group(place_ref, order):
    step = pl.program_id(0)
    distance = order[0]
    for index, value in enumerate(order[1:], 1):
        distance = jnp.where(step == index, value, distance)
    return (place_ref[2] * 2 + place_ref[3]) ^ distance


def dot(left, right, left_dim=1, right_dim=0):
    return lax.dot_general(
        left, right, (((left_dim,), (right_dim,)), ((), ())), preferred_element_type=f32
    )


def put(count, index, line):
    spot = lax.broadcasted_iota(jnp.int32, (count, 1), 0)
    return jnp.where(spot == index, line, 0.0)


def pick(lines, index):
    spot = lax.broadcasted_iota(jnp.int32, (lines.shape[0], 1), 0)
    return jnp.sum(jnp.where(spot == index, lines, 0.0), 0, keepdims=True)


def upright(row):
    n = row.shape[1]
    more = -n % 128
    if more:
        row = jnp.concatenate([row, jnp.zeros((1, more), f32)], 1)
    return jnp.broadcast_to(row, (128, n + more)).T[:n, 0:1]


def lying(column):
    n = column.shape[0]
    wide = jnp.broadcast_to(column, (n, 128))
    more = -n % 128
    if more:
        wide = jnp.concatenate([wide, jnp.zeros((more, 128), f32)])
    return wide.T[0:1, :n]


def probabilities(query, key, visible):
    scores = dot(query, key, 1, 1) * HEAD_DIM ** (-0.5)
    scores = jnp.where(visible, scores, -1e30)
    raised = jnp.exp(scores - jnp.max(scores, -1, keepdims=True))
    return raised * (1.0 / jnp.sum(raised, -1, keepdims=True))


def head_masks(share):
    lane = lax.broadcasted_iota(jnp.int32, (1, share), 1) // HEAD_DIM
    return [lane == head for head in range(share // HEAD_DIM)]


def stacked(rows, masks):
    return jnp.concatenate([jnp.where(mask, rows, jnp.zeros((), rows.dtype)) for mask in masks])


def unstacked(every, masks):
    size = every.shape[0] // len(masks)
    result = every[:size]
    for head, mask in enumerate(masks[1:], 1):
        result = jnp.where(mask, every[head * size : (head + 1) * size], result)
    return result


def pieces_kernel(
    place_ref,
    in_ref,
    out_ref,
    expand_ref,
    contract_ref,
    vectors_ref,
    own_ref,
    attend_low_ref,
    expand_low_ref,
    contract_low_ref,
    square_ref,
    lines_ref,
):
    to_lines(vectors_ref, lines_ref)
    share = out_ref.shape[0]
    lane = lax.broadcasted_iota(jnp.int32, (1, 128), 1)
    for part in range(3):
        own_ref[:, part * share : (part + 1) * share] = in_ref[part]
    own_ref[:, 3 * share :] = out_ref[...].T
    attend_low_ref[...] = own_ref[...].astype(bf16)
    expand_low_ref[...] = expand_ref[...].astype(bf16)
    contract_low_ref[...] = contract_ref[...].astype(bf16)
    totals = jnp.zeros((1, 128), f32)
    for index, ref in enumerate((in_ref, out_ref, expand_ref, contract_ref)):
        values = ref[...]
        total = jnp.sum(values * values, keepdims=True).reshape(1, 1)
        totals = jnp.where(lane == index, total, totals)
    square_ref[...] = totals


def in_slots(table_ref, padded):
    empty = jnp.zeros((padded - table_ref.shape[0], table_ref.shape[1]), f32)
    return jnp.concatenate([table_ref[1:], table_ref[0:1], empty])


def stem_kernel(
    place_ref,
    labels_ref,
    pixels_ref,
    stem_ref,
    table_ref,
    vectors_ref,
    mask_ref,
    stream_ref,
    rows_ref,
    present_ref,
    facts_ref,
):
    count, patch_count = mask_ref.shape
    padded = present_ref.shape[1]
    low = stem_ref[...].astype(bf16)
    slot = lax.broadcasted_iota(jnp.int32, (padded, 1), 0)
    table = in_slots(table_ref, padded)
    table = table + jnp.where(slot < patch_count, line(vectors_ref, STEM_BIAS), 0.0)
    for image in range(count):
        span = slice(image * padded, (image + 1) * padded)
        stream = dot(pixels_ref[span, :], low) + table
        stream_ref[span, :] = stream
        hat, _ = normal_parts(stream)
        normed = hat * line(vectors_ref, GAIN_ONE) + line(vectors_ref, SHIFT_ONE)
        rows_ref[span, :] = normed.astype(bf16)
    lane = lax.broadcasted_iota(jnp.int32, (count, padded), 1)
    present_ref[...] = jnp.where(lane == patch_count, 1.0, 0.0)
    present_ref[:, :patch_count] = mask_ref[...].astype(f32)
    lane = lax.broadcasted_iota(jnp.int32, (1, 128), 1)
    for image in range(count):
        present = present_ref[image : image + 1, :]
        kept = jnp.sum(present, 1, keepdims=True)
        label = labels_ref[image].astype(f32)
        fact = jnp.where(lane == 0, kept, jnp.where(lane == 1, label, 0.0))
        facts_ref[image : image + 1, :] = fact
        facts_ref[count + image : count + image + 1, :] = fact


def attend_kernel(
    place_ref,
    weight,
    rows_ref,
    vectors_ref,
    present_ref,
    stream_ref,
    qkv_ref,
    attended_ref,
    stream_out_ref,
    rows_out_ref,
    sum_ref,
    *,
    order,
):
    step = pl.program_id(0)
    count, padded = present_ref.shape
    share = attended_ref.shape[2]

    group = own_group(place_ref, order)
    projected = dot(rows_ref[...], weight(0, 3 * share))
    query = projected[:, :share] + share_of(vectors_ref, QUERY_BIAS, group, share)
    query = query.astype(bf16)
    key = projected[:, share : 2 * share].astype(bf16)
    value = projected[:, 2 * share :] + share_of(vectors_ref, VALUE_BIAS, group, share)
    value = value.astype(bf16)
    qkv_ref[0, 0] = query
    qkv_ref[0, 1] = key
    qkv_ref[0, 2] = value
    masks = head_masks(share)
    for image in range(count):
        span = slice(image * padded, (image + 1) * padded)
        visible = present_ref[image : image + 1, :] > 0.5
        low = probabilities(stacked(query[span], masks), key[span], visible).astype(bf16)
        every = dot(low, value[span])
        attended_ref[0, span, :] = unstacked(every, masks).astype(bf16)
    part = dot(attended_ref[0], weight(3 * share, 4 * share), 1, 1)

    @pl.when(step == 0)
    def _():
        stream_out_ref[...] = stream_ref[...] + line(vectors_ref, ATTEND_BIAS) + part

    @pl.when(step > 0)
    def _():
        stream_out_ref[...] += part

    @pl.when(step == pl.num_programs(0) - 1)
    def _():
        hat, _ = normal_parts(stream_out_ref[...])
        rows_two = hat * line(vectors_ref, GAIN_TWO) + line(vectors_ref, SHIFT_TWO)
        rows_out_ref[...] = rows_two.astype(bf16)
        for image in range(count):
            span = slice(image * padded, (image + 1) * padded)
            here = upright(present_ref[image : image + 1, :])
            total = jnp.sum(stream_out_ref[span, :] * here, 0, keepdims=True)
            sum_ref[image : image + 1, :] = total
            sum_ref[image + count : image + count + 1, :] = total


def hidden_kernel(
    place_ref,
    weight,
    rows_ref,
    vectors_ref,
    present_ref,
    sum_ref,
    slope_ref,
    column_ref,
    *,
    order,
):
    bias = pick(vectors_ref[EXPAND_BIAS : EXPAND_BIAS + len(order), :], own_group(place_ref, order))
    hidden = dot(rows_ref[...], weight()) + bias
    first, second = 0.7978845608028654, 0.044715
    square = hidden * hidden
    half = 0.5 + 0.5 * jnp.tanh(hidden * (first + first * second * square))
    active = (hidden * half).astype(bf16)
    count, padded = present_ref.shape

    @pl.when(pl.program_id(0) == 0)
    def _():
        to_column(present_ref, column_ref)

    row = lax.broadcasted_iota(jnp.int32, (2 * count, 1), 0)
    sums = jnp.zeros(sum_ref.shape[1:], f32)
    for image in range(count):
        chooser = jnp.broadcast_to(present_ref[image : image + 1, :], (2 * count, padded))
        total = dot(chooser.astype(bf16), active[image * padded : (image + 1) * padded])
        sums = jnp.where(row % count == image, total, sums)
    sum_ref[0] = sums
    steep = hidden * (2.0 * first + 6.0 * first * second * square)
    slope = half * (1.0 + steep * (1.0 - half))
    slope_ref[0] = (slope * column_ref[...]).astype(bf16)


def expand_back_kernel(
    place_ref,
    weight,
    rows_ref,
    slope_ref,
    d_active_ref,
    far_ref,
    near_ref,
    bias_ref,
    d_rows_ref,
    d_hidden_low,
):
    step = pl.program_id(0)
    count = d_active_ref.shape[1] // 2
    padded = slope_ref.shape[1] // count
    bias = jnp.zeros((1, d_hidden_low.shape[1]), f32)
    for image in range(count):
        span = slice(image * padded, (image + 1) * padded)
        d_hidden = slope_ref[0, span, :].astype(f32) * d_active_ref[0, image : image + 1, :]
        bias = bias + jnp.sum(d_hidden, 0, keepdims=True)
        d_hidden_low[span, :] = d_hidden.astype(bf16)
    bias_ref[0] = bias
    half = pl.num_programs(0) // 2

    @pl.when(step < half)
    def _():
        far_ref[0] = dot(rows_ref[...], d_hidden_low[...], 0, 0).astype(bf16)

    @pl.when(step >= half)
    def _():
        near_ref[0] = dot(rows_ref[...], d_hidden_low[...], 0, 0).astype(bf16)

    part = dot(d_hidden_low[...], weight(), 1, 1)

    @pl.when(step == 0)
    def _():
        d_rows_ref[...] = part

    @pl.when(step > 0)
    def _():
        d_rows_ref[...] += part


def between_kernel(
    place_ref,
    d_rows_ref,
    d_row_ref,
    present_ref,
    stream_ref,
    vectors_ref,
    d_stream_ref,
    d_low_ref,
    vector_ref,
):
    count = d_row_ref.shape[0] // 2
    padded = stream_ref.shape[0] // count
    gain = line(vectors_ref, GAIN_TWO)
    below, gain, shift = pull_normal(stream_ref[...], gain, d_rows_ref[...])
    vector_ref[1:2, :] = gain
    vector_ref[2:3, :] = shift
    bias = jnp.zeros((1, below.shape[1]), f32)
    for image in range(count):
        span = slice(image * padded, (image + 1) * padded)
        here = upright(present_ref[image : image + 1, :])
        d_stream = below[span] + d_row_ref[image : image + 1, :] * here
        bias = bias + jnp.sum(d_stream, 0, keepdims=True)
        d_stream_ref[span, :] = d_stream
        d_low_ref[span, :] = d_stream.astype(bf16)
    vector_ref[0:1, :] = bias


def attend_back_kernel(
    place_ref,
    weight,
    rows_ref,
    qkv_ref,
    attended_ref,
    present_ref,
    d_low_ref,
    *refs,
):
    grad_ref, bias_ref, d_rows_ref, d_projected, column_ref = refs[-5:]
    step = pl.program_id(0)
    share = attended_ref.shape[2]
    count = bias_ref.shape[1] // 2
    padded = attended_ref.shape[1] // count
    scale = HEAD_DIM ** (-0.5)
    d_attended = dot(d_low_ref[...], weight(3 * share, 4 * share)).astype(bf16)

    @pl.when(step == 0)
    def _():
        to_column(present_ref, column_ref)

    masks = head_masks(share)
    for image in range(count):
        span = slice(image * padded, (image + 1) * padded)
        hidden = column_ref[span, :] < 0.5
        query, key, value = (qkv_ref[0, part, span, :] for part in range(3))
        query = query * jnp.asarray(scale, bf16)
        queries = stacked(query, masks)
        d_images = stacked(d_attended[span], masks)
        scores = jnp.where(hidden, -1e30, dot(key, queries, 1, 1))
        raised = jnp.exp(scores - jnp.max(scores, 0, keepdims=True))
        probs = raised * (1.0 / jnp.sum(raised, 0, keepdims=True))
        d_probs = dot(value, d_images, 1, 1)
        inner = jnp.sum(probs * d_probs, 0, keepdims=True)
        d_scores = (probs * (d_probs - inner)).astype(bf16)
        d_value = dot(probs.astype(bf16), d_images)
        d_key = dot(d_scores, queries)
        d_query = unstacked(dot(d_scores, key, 0, 0), masks) * scale
        bias_ref[0, image : image + 1, :] = jnp.sum(d_query, 0, keepdims=True)
        bias_ref[0, count + image : count + image + 1, :] = jnp.sum(d_value, 0, keepdims=True)
        d_projected[span, :share] = d_query.astype(bf16)
        d_projected[span, share : 2 * share] = d_key.astype(bf16)
        d_projected[span, 2 * share :] = d_value.astype(bf16)
    grad_ref[0, :, : 3 * share] = dot(rows_ref[...], d_projected[...], 0, 0).astype(bf16)
    grad_ref[0, :, 3 * share :] = dot(d_low_ref[...], attended_ref[0], 0, 0).astype(bf16)
    part = dot(d_projected[...], weight(0, 3 * share), 1, 1)

    @pl.when(step == 0)
    def _():
        d_rows_ref[...] = part + refs[0][...] if len(refs) > 5 else part

    @pl.when(step > 0)
    def _():
        d_rows_ref[...] += part


def stem_back_kernel(
    place_ref,
    d_rows_ref,
    d_stream_ref,
    stream_ref,
    vectors_ref,
    pixels_ref,
    far_ref,
    near_ref,
    vector_ref,
):
    rows, width = pixels_ref.shape
    gain = line(vectors_ref, GAIN_ONE)
    below, gain, shift = pull_normal(stream_ref[...], gain, d_rows_ref[...])
    vector_ref[0:1, :] = gain
    vector_ref[1:2, :] = shift
    below = below + d_stream_ref[...]
    slots = vector_ref.shape[0] - 8
    table = below[:slots]
    for image in range(1, rows // slots):
        table = table + below[image * slots : (image + 1) * slots]
    vector_ref[8:, :] = table
    stem = dot(pixels_ref[...], below.astype(bf16), 0, 0).astype(bf16)
    half, size, columns = near_ref.shape
    empty = jnp.zeros((2 * half * size - width - slots, columns), bf16)
    whole = jnp.concatenate([stem, table.astype(bf16), empty])
    for chunk in range(2 * half):
        near, far = place_ref[6] ^ chunk, place_ref[7] ^ chunk

        @pl.when(near < half)
        def _(chunk=chunk, near=near):
            near_ref[near] = whole[chunk * size : (chunk + 1) * size]

        @pl.when(far < half)
        def _(chunk=chunk, far=far):
            far_ref[far] = whole[chunk * size : (chunk + 1) * size]


def head_vectors(vectors_ref):
    rest = CLASSES - vectors_ref.shape[1]
    bias = jnp.concatenate(
        [line(vectors_ref, HEAD_BIAS), vectors_ref[HEAD_BIAS + 1 : HEAD_BIAS + 2, :rest]], 1
    )
    return line(vectors_ref, GAIN_LAST), line(vectors_ref, SHIFT_LAST), bias


def classify(pooled, labels, head, gain, shift, bias, inverse_count):
    hat, inverse = normal_parts(pooled)
    low = (hat * gain + shift).astype(bf16)
    logits = dot(low, head, 1, 1) + bias
    logits = logits - jnp.max(logits, -1, keepdims=True)
    raised = jnp.exp(logits)
    total = jnp.sum(raised, -1, keepdims=True)
    lane = lax.broadcasted_iota(jnp.int32, logits.shape, 1)
    target = jnp.where(lane == labels.astype(jnp.int32), 1.0 - smoothing, 0.0) + smoothing / CLASSES
    score = jnp.sum(target * (logits - jnp.log(total)), -1, keepdims=True)
    d_logits = (raised * (1.0 / total) - target) * inverse_count
    d_final = dot(d_logits.astype(bf16), head)
    scaled = d_final * gain
    mean_one = jnp.mean(scaled, -1, keepdims=True)
    mean_two = jnp.mean(scaled * hat, -1, keepdims=True)
    return score, low, d_logits, d_final, hat, (scaled - mean_one - hat * mean_two) * inverse


def split(values):
    high = values.astype(bf16)
    return high, (values - high.astype(f32)).astype(bf16)


def own_head_kernel(
    place_ref,
    active_ref,
    sum_ref,
    facts_ref,
    vectors_ref,
    head_ref,
    *refs,
    inverse_count,
):
    groups, twice, width = active_ref.shape
    rows = sum_ref.shape[1]
    if len(refs) == 4:
        full_ref, piece_ref, d_row_ref, d_active_ref = refs
        chosen = []
    else:
        piece_ref, d_row_ref, d_active_ref, full_ref, sems = refs[4:]
        chosen = [
            (r, group_copies(place_ref, refs[:4], full_ref.at[r], sems.at[r], r))
            for r in range(groups)
        ]
    for distance, choices in chosen:
        each_copy(place_ref, distance, choices, start_copy)
    mixed = jnp.zeros((2 * twice, rows), f32)
    for group in range(groups):
        for distance, choices in chosen[group : group + 1]:
            each_copy(place_ref, distance, choices, wait_copy)
        weight = full_ref[group].reshape(rows, width)
        mixed = mixed + dot(jnp.concatenate(split(active_ref[group])), weight, 1, 1)
    mixed = mixed[:twice] + mixed[twice:]
    kept, labels = facts_ref[:, 0:1], facts_ref[:, 1:2]
    pooled = (sum_ref[...] + mixed) / kept + line(vectors_ref, CONTRACT_BIAS)
    d_pooled = classify(
        pooled, labels, head_ref[...], *head_vectors(vectors_ref), inverse_count
    )[-1]
    d_row = d_pooled / kept
    d_row_ref[...] = d_row
    d_row_low = d_row.astype(bf16)
    first = lax.broadcasted_iota(jnp.int32, (twice, 1), 0) < twice // 2
    for group in range(groups):
        d_active_ref[group] = dot(d_row_low, full_ref[group].reshape(rows, width))
    for part, (pool, fact) in enumerate(zip(split(pooled), split(facts_ref[...]))):
        piece_ref[part * twice : (part + 1) * twice, :rows] = pool
        piece_ref[part * twice : (part + 1) * twice, rows:] = fact
    own = place_ref[2] * 2 + place_ref[3]
    for half in range(groups // 2):
        sums = jnp.where(first, active_ref[own ^ (2 * half)], active_ref[own ^ (2 * half + 1)])
        span = slice((2 + half) * twice, (3 + half) * twice)
        piece_ref[span, :rows] = sums.astype(bf16)
        piece_ref[span, rows:] = jnp.zeros((twice, piece_ref.shape[1] - rows), bf16)


def all_head_kernel(
    place_ref,
    pieces_ref,
    vectors_ref,
    head_ref,
    grad_ref,
    contract_ref,
    vector_ref,
    bias_ref,
    *,
    inverse_count,
):
    pieces = pieces_ref[0].astype(f32)
    count, rows = pieces.shape[0], vectors_ref.shape[1]
    twice = pieces.shape[1] // 4

    def part(index):
        return pieces[:, index * twice : (index + 1) * twice].reshape(count * twice, -1)

    lines = part(0) + part(1)
    pooled, kept, labels = lines[:, :rows], lines[:, rows : rows + 1], lines[:, rows + 1 : rows + 2]
    score, low, d_logits, d_final, hat, d_pooled = classify(
        pooled, labels, head_ref[...], *head_vectors(vectors_ref), inverse_count
    )
    half = lax.broadcasted_iota(jnp.int32, (count * twice, 1), 0) % twice // (twice // 2)
    once = half == 0
    d_logits = jnp.where(once, d_logits, 0.0)
    own = place_ref[5]
    active = jnp.where(own // 2 == 0, part(2)[:, :rows], part(3)[:, :rows]).astype(bf16)
    d_row = jnp.where(half == own % 2, d_pooled / kept, 0.0).astype(bf16)
    share = contract_ref.shape[0]
    place = lax.broadcasted_iota(jnp.int32, (rows, share), 0)
    lane = lax.broadcasted_iota(jnp.int32, (rows, share), 1)
    chooser = (place == lane + place_ref[4] * share).astype(f32).astype(bf16)
    d_row = dot(d_row, chooser).astype(bf16)

    def total(values):
        return jnp.sum(jnp.where(once, values, 0.0), 0, keepdims=True)

    results = (
        (grad_ref, slice(None), dot(d_logits.astype(bf16), low, 0, 0)),
        (contract_ref, slice(None), dot(d_row, active, 0, 0)),
        (vector_ref, slice(0, 1), total(d_pooled)),
        (vector_ref, slice(1, 2), total(d_final * hat)),
        (vector_ref, slice(2, 3), total(d_final)),
        (bias_ref, slice(0, 1), jnp.sum(d_logits, 0, keepdims=True)),
        (bias_ref, slice(1, 2), -total(score) + jnp.zeros((1, bias_ref.shape[1]), f32)),
    )
    for ref, span, value in results:

        @pl.when(pl.program_id(0) == 0)
        def _(ref=ref, span=span, value=value):
            ref[span, :] = value

        @pl.when(pl.program_id(0) > 0)
        def _(ref=ref, span=span, value=value):
            ref[span, :] += value


def head_step_kernel(
    place_ref,
    weight_ref,
    grad_ref,
    old_rows_ref,
    old_cols_ref,
    new_ref,
    new_rows_ref,
    new_cols_ref,
):
    new_ref[...], cols, rows = factored(
        weight_ref[...],
        grad_ref[...],
        old_cols_ref[...].reshape(1, -1),
        old_rows_ref[...].reshape(1, -1),
        True,
    )
    new_cols_ref[...] = cols[0]
    new_rows_ref[...] = rows[0]


def factored(weight, grad, down_old, across_old, turned, valid=None, count=None):
    down_old = upright(down_old)
    squared = grad * grad + eps_one
    n, m = grad.shape
    if valid is not None:
        squared = jnp.where(valid, squared, 0.0)
        n = count
    down_new = decay_rate * down_old + (1.0 - decay_rate) * (
        jnp.sum(squared, 1, keepdims=True) / m
    )
    across_new = decay_rate * across_old + (1.0 - decay_rate) * (
        jnp.sum(squared, 0, keepdims=True) / n
    )
    if turned:
        mean = jnp.sum(across_new, keepdims=True) / m
    else:
        mean = jnp.sum(down_new, keepdims=True) / n
    divisor = down_new if valid is None else jnp.where(valid, down_new, 1.0)
    update = grad * lax.rsqrt(divisor * across_new / mean)
    size = n * m
    clip = jnp.sqrt(jnp.sum(update * update, keepdims=True) / size) / clip_level
    magnitude = jnp.sqrt(jnp.sum(weight * weight, keepdims=True) / size)
    scale = step_rate * jnp.maximum(eps_two, magnitude) / jnp.maximum(1.0, clip)
    return weight - scale * update, lying(down_new), across_new


def stem_step_kernel(
    place_ref,
    near_ref,
    far_ref,
    stem_ref,
    stem_rows_ref,
    stem_cols_ref,
    table_ref,
    table_rows_ref,
    table_cols_ref,
    stem_new_ref,
    stem_rows_new_ref,
    stem_cols_new_ref,
    table_new_ref,
    table_rows_new_ref,
    table_cols_new_ref,
    both_ref,
    *,
    padded,
):
    n, slots = stem_ref.shape[0], table_ref.shape[0]
    half, size = near_ref.shape[:2]
    for chunk in range(2 * half):
        near, far = place_ref[6] ^ chunk, place_ref[7] ^ chunk
        span = slice(chunk * size, (chunk + 1) * size)

        @pl.when(near < half)
        def _(span=span, near=near):
            both_ref[span, :] = near_ref[near]

        @pl.when(far < half)
        def _(span=span, far=far):
            both_ref[span, :] = far_ref[far]

    stem_new_ref[...], rows, cols = factored(
        stem_ref[...],
        both_ref[:n, :].astype(f32),
        stem_rows_ref[...].reshape(1, -1),
        stem_cols_ref[...].reshape(1, -1),
        False,
    )
    stem_rows_new_ref[...] = rows[0]
    stem_cols_new_ref[...] = cols[0]
    old = table_rows_ref[...].reshape(1, slots)
    empty = jnp.zeros((1, padded - slots), f32)
    table, rows, cols = factored(
        in_slots(table_ref, padded),
        both_ref[n : n + padded, :].astype(f32),
        jnp.concatenate([old[:, 1:], old[:, 0:1], empty], 1),
        table_cols_ref[...].reshape(1, -1),
        False,
        lax.broadcasted_iota(jnp.int32, (padded, 1), 0) < slots,
        slots,
    )
    table_new_ref[1:] = table[: slots - 1]
    table_new_ref[0:1] = table[slots - 1 : slots]
    table_rows_new_ref[...] = jnp.concatenate(
        [rows[:, slots - 1 : slots], rows[:, : slots - 1]], 1
    )[0]
    table_cols_new_ref[...] = cols[0]


def layout(data, groups):
    return 0, data, data + 4 * groups, -(-(data + 4 * groups + 6) // 8) * 8


def across(column):
    n = column.shape[0]
    wide = jnp.broadcast_to(column, (n, 128))
    if n < 128:
        wide = jnp.concatenate([wide, jnp.zeros((128 - n, 128), f32)])
    return wide.T[0:1]


def down(row, n):
    return jnp.broadcast_to(row, (128, 128)).T[:n, 0:1]


def sums_kernel(
    place_ref,
    attend_ref,
    expand_ref,
    contract_ref,
    squares_ref,
    vector_one_ref,
    vector_two_ref,
    expand_bias_ref,
    heads_far_ref,
    heads_near_ref,
    sums_ref,
    *,
    data,
    groups,
    share,
    patch_count,
):
    block, group = place_ref[4], place_ref[5]
    own = place_ref[2] * 2 + place_ref[3]
    _, at_group, at_single, _ = layout(data, groups)
    sums_ref[...] = jnp.zeros(sums_ref.shape, f32)
    lane = lax.broadcasted_iota(jnp.int32, (1, attend_ref.shape[1]), 1)
    for index, ref in enumerate((attend_ref, expand_ref, contract_ref)):
        grad = ref[...]
        squared = grad * grad + eps_one
        span = slice(at_group + index * groups, at_group + (index + 1) * groups)
        sums_ref[span, :] = put(groups, group, jnp.sum(squared, 0, keepdims=True))
        if index == 0:
            lines = (
                jnp.sum(jnp.where(lane < 3 * share, squared, 0.0), 1, keepdims=True),
                jnp.sum(jnp.where(lane < 3 * share, 0.0, squared), 1, keepdims=True),
            )
        else:
            lines = (jnp.sum(squared, 1, keepdims=True),)
        for part, line in enumerate(lines):
            spot = (index + (index > 0) + part) * 128
            sums_ref[:data, spot : spot + 128] = put(data, block, across(line))
    sums_ref[:data, 512:640] = put(data, block, squares_ref[...])
    at_group += 3 * groups
    lines = jnp.zeros((groups, expand_bias_ref.shape[2]), f32)
    for distance in range(groups):
        lines = lines + put(groups, own ^ distance, expand_bias_ref[distance])
    sums_ref[at_group : at_group + groups, :] = lines
    count = heads_far_ref.shape[1] // 2
    for part in range(2):
        span = slice(part * count, (part + 1) * count)
        lines = jnp.zeros((groups, share), f32)
        for ref, order in ((heads_far_ref, (3, 1)), (heads_near_ref, (2, 0))):
            for step, distance in enumerate(order):
                total = jnp.sum(ref[step][span], 0, keepdims=True)
                lines = lines + put(groups, own ^ distance, total)
        sums_ref[part * groups : (part + 1) * groups, 3 * share :] = lines
    stem_bias = jnp.sum(vector_one_ref[8 : 8 + patch_count, :], 0, keepdims=True)
    singles = (stem_bias, vector_one_ref[0:2, :], vector_two_ref[0:3, :])
    for line in singles:
        sums_ref[at_single : at_single + line.shape[0], :] = line
        at_single += line.shape[0]


def vector_kernel(
    place_ref,
    sums_ref,
    last_ref,
    head_ref,
    vectors_ref,
    second_ref,
    grad_out,
    new_out,
    second_out,
    grad_ref,
    lines_ref,
    *,
    data,
    groups,
    share,
):
    to_lines(second_ref, lines_ref)
    length = second_ref.shape[0]
    _, at_group, at_single, _ = layout(data, groups)
    width = vectors_ref.shape[1]

    def single(index):
        return sums_ref[at_single + index : at_single + index + 1, :]

    def joined(part):
        lines = sums_ref[part * groups : (part + 1) * groups, 3 * share :]
        return jnp.concatenate([lines[g : g + 1] for g in range(groups)], 1)

    grad_ref[...] = jnp.zeros(grad_ref.shape, f32)
    spot = at_group + 3 * groups
    rest = CLASSES - width
    for index, value in (
        (STEM_BIAS, single(0)),
        (GAIN_ONE, single(1)),
        (SHIFT_ONE, single(2)),
        (QUERY_BIAS, joined(0)),
        (VALUE_BIAS, joined(1)),
        (ATTEND_BIAS, single(3)),
        (GAIN_TWO, single(4)),
        (SHIFT_TWO, single(5)),
        (EXPAND_BIAS, sums_ref[spot : spot + groups, :]),
        (CONTRACT_BIAS, last_ref[0:3, :]),
        (HEAD_BIAS, head_ref[0:1, :width]),
    ):
        grad_ref[index : index + value.shape[0], :] = value
    grad_ref[HEAD_BIAS + 1 : HEAD_BIAS + 2, :rest] = head_ref[0:1, width:]
    grad = grad_ref[...]
    row = lax.broadcasted_iota(jnp.int32, grad.shape, 0)
    lane = lax.broadcasted_iota(jnp.int32, grad.shape, 1)
    valid = row * width + lane < length
    second = decay_rate * lines_ref[...] + (1.0 - decay_rate) * (grad * grad + eps_one)
    update = grad * lax.rsqrt(jnp.where(valid, second, 1.0))
    total = jnp.sum(update * update, keepdims=True) / length
    square = jnp.sum(vectors_ref[...] * vectors_ref[...], keepdims=True) / length
    scale = step_rate * jnp.maximum(eps_two, jnp.sqrt(square))
    scale = scale / jnp.maximum(1.0, jnp.sqrt(total) / clip_level)
    from_lines(grad, grad_out)
    from_lines(vectors_ref[...] - scale * update, new_out)
    from_lines(second, second_out)


def renew_kernel(
    place_ref,
    sums_ref,
    in_rows_ref,
    out_cols_ref,
    expand_rows_ref,
    contract_cols_ref,
    in_cols_ref,
    out_rows_ref,
    expand_cols_ref,
    contract_rows_ref,
    attend_ref,
    expand_ref,
    contract_ref,
    in_rows_out,
    out_cols_out,
    expand_rows_out,
    contract_cols_out,
    in_cols_out,
    out_rows_out,
    expand_cols_out,
    contract_rows_out,
    update_ref,
    scalar_ref,
    square_ref,
    rows_new_ref,
    cols_new_ref,
    *,
    data,
    groups,
    share,
):
    block, group = place_ref[4], place_ref[5]
    size = attend_ref.shape[0]
    width = attend_ref.shape[1]
    _, at_group, _, _ = layout(data, groups)
    length, hidden = data * size, groups * width
    lane = lax.broadcasted_iota(jnp.int32, (1, width), 1)
    first = lane < 3 * share
    spare = lax.broadcasted_iota(jnp.int32, (1, 128), 1) < size
    for index, ref in enumerate((in_rows_ref, out_cols_ref, expand_rows_ref, contract_cols_ref)):
        for part in range(data):
            values = ref[pl.ds(part * size, size)].reshape(1, size)
            rows_new_ref[part : part + 1, index * 128 : index * 128 + size] = values
    for part in range(groups):
        span = slice(part * share, (part + 1) * share)
        for which in range(3):
            cols_new_ref[part : part + 1, which * share : (which + 1) * share] = in_cols_ref[
                which : which + 1, span
            ]
        values = out_rows_ref[pl.ds(part * share, share)].reshape(1, share)
        cols_new_ref[part : part + 1, 3 * share :] = values
        for index, ref in enumerate((expand_cols_ref, contract_rows_ref), 1):
            values = ref[pl.ds(part * width, width)].reshape(1, width)
            cols_new_ref[index * groups + part : index * groups + part + 1, :] = values
    counts = (3 * length, length, hidden, hidden)
    means = []
    for index, count in enumerate(counts):
        span = slice(index * 128, (index + 1) * 128)
        new = decay_rate * rows_new_ref[:, span]
        new = new + (1.0 - decay_rate) * (sums_ref[:data, span] / count)
        rows_new_ref[:, span] = new
        means.append(jnp.sum(jnp.where(spare, new, 0.0), keepdims=True) / length)
        out = (in_rows_out, out_cols_out, expand_rows_out, contract_cols_out)[index]
        for part in range(data):
            out[pl.ds(part * size, size)] = new[part, :size]
    for index, count in enumerate((length, length, length)):
        span = slice(index * groups, (index + 1) * groups)
        lines = sums_ref[at_group + index * groups : at_group + (index + 1) * groups, :]
        new = decay_rate * cols_new_ref[span, :] + (1.0 - decay_rate) * (lines / count)
        cols_new_ref[span, :] = new
        for part in range(groups):
            if index == 0:
                for which in range(3):
                    in_cols_out[which : which + 1, part * share : (part + 1) * share] = new[
                        part : part + 1, which * share : (which + 1) * share
                    ]
                out_rows_out[pl.ds(part * share, share)] = new[part, 3 * share :]
            else:
                out = (expand_cols_out, contract_rows_out)[index - 1]
                out[pl.ds(part * width, width)] = new[part]
        if index == 0:
            means[1] = jnp.sum(jnp.where(first, 0.0, new), keepdims=True) / length
        if index == 2:
            means[3] = jnp.sum(new, keepdims=True) / hidden
    scalars = jnp.zeros((1, 128), f32)
    place_lane = lax.broadcasted_iota(jnp.int32, (1, 128), 1)
    for index, ref in enumerate((attend_ref, expand_ref, contract_ref)):
        across_row = pick(cols_new_ref[index * groups : (index + 1) * groups, :], group)

        def row(which):
            span = slice(which * 128, (which + 1) * 128)
            return down(pick(rows_new_ref[:, span], block), size)

        if index == 0:
            denominator = jnp.where(
                first, row(0) * across_row / means[0], row(1) * across_row / means[1]
            )
        else:
            denominator = row(index + 1) * across_row / means[index + 1]
        update = ref[...] * lax.rsqrt(denominator)
        update_ref[index] = update
        squared = update * update
        if index == 0:
            totals = (jnp.where(first, squared, 0.0), jnp.where(first, 0.0, squared))
        else:
            totals = (squared,)
        for part, total in enumerate(totals):
            spot = index + (index > 0) + part
            scalars = jnp.where(place_lane == spot, jnp.sum(total, keepdims=True), scalars)
    scalar_ref[...] = jnp.broadcast_to(scalars, scalar_ref.shape)
    squares = jnp.sum(sums_ref[:data, 512:640], 0, keepdims=True)
    square_ref[...] = jnp.broadcast_to(squares, square_ref.shape)


def step_kernel(
    place_ref,
    update_ref,
    scalar_ref,
    square_ref,
    attend_ref,
    expand_ref,
    contract_ref,
    in_ref,
    in_low_ref,
    out_ref,
    out_low_ref,
    expand_new_ref,
    expand_low_ref,
    contract_new_ref,
    contract_low_ref,
    *,
    sizes,
):
    share = in_ref.shape[2]
    scales = []
    for index, size in enumerate(sizes):
        total = scalar_ref[0:1, index : index + 1]
        square = square_ref[0:1, index : index + 1]
        clip = jnp.maximum(1.0, jnp.sqrt(total / size) / clip_level)
        scales.append(step_rate * jnp.maximum(eps_two, jnp.sqrt(square / size)) / clip)
    lane = lax.broadcasted_iota(jnp.int32, (1, attend_ref.shape[1]), 1)
    scale = jnp.where(lane < 3 * share, scales[0], scales[1])
    attend = attend_ref[...] - scale * update_ref[0]
    for part in range(3):
        lines = attend[:, part * share : (part + 1) * share]
        in_ref[part] = lines
        in_low_ref[part] = lines.astype(bf16)
    out = attend[:, 3 * share :].T
    out_ref[...] = out
    out_low_ref[...] = out.astype(bf16)
    expand = expand_ref[...] - scales[2] * update_ref[1]
    expand_new_ref[...] = expand
    expand_low_ref[...] = expand.astype(bf16)
    contract = contract_ref[...] - scales[3] * update_ref[2]
    contract_new_ref[...] = contract
    contract_low_ref[...] = contract.astype(bf16)


def call(
    body, order, place, operands, results, scratch=(), flops=0, weights=None, limit=48
):
    steps = len(order)
    pieces = weights is not None and len(weights) == 4

    def distance(step):
        at = order[0]
        for index, value in enumerate(order[1:], 1):
            at = jnp.where(step == index, value, at)
        return at

    def spec(shape, mark):
        zeros = (0,) * (len(shape) - 1)
        if mark == "any":
            return pl.BlockSpec(memory_space=pl.ANY)
        if mark == "smem":
            return pl.BlockSpec(memory_space=pltpu.SMEM)
        if mark is False:
            return pl.BlockSpec(shape, lambda g, p: (0,) + zeros)
        if mark is True:
            return pl.BlockSpec(
                (1,) + shape[1:], lambda g, p: ((p[2] * 2 + p[3]) ^ distance(g),) + zeros
            )
        if mark == "far":
            return pl.BlockSpec((1,) + shape[1:], lambda g, p: (distance(g),) + zeros)
        return pl.BlockSpec((1,) + shape[1:], lambda g, p: (mark(g),) + zeros)

    operands, scratch = tuple(operands), tuple(scratch)
    kernel = body
    if weights is not None:
        operands = tuple((weight, "any" if pieces else True) for weight in weights) + operands
    if pieces:
        some = weights[0]
        height, width = some.shape[0] * some.shape[1] * some.shape[2], some.shape[3]
        full = (steps, some.shape[1], some.shape[0]) + some.shape[2:]
        scratch += ((full, some.dtype), ((steps, 2), None))

        def kernel(place_ref, *refs):
            full_ref, sems = refs[-2:]
            step = pl.program_id(0)
            copies = [
                (r, group_copies(place_ref, refs[:4], full_ref.at[i], sems.at[i], r))
                for i, r in enumerate(order)
            ]

            @pl.when(step == 0)
            def _():
                for distance, choices in copies:
                    each_copy(place_ref, distance, choices, start_copy)

            for index in range(steps):

                @pl.when(step == index)
                def _(index=index):
                    each_copy(place_ref, *copies[index], wait_copy)

            def weight(start=0, stop=width):
                return full_ref[step, :, :, :, start:stop].reshape(height, stop - start)

            body(place_ref, weight, *refs[4:-2])

    elif weights is not None:

        def kernel(place_ref, weight_ref, *refs):
            def weight(start=0, stop=weight_ref.shape[2]):
                return weight_ref[0, :, start:stop]

            body(place_ref, weight, *refs)

    return pl.pallas_call(
        kernel,
        grid_spec=pltpu.PrefetchScalarGridSpec(
            num_scalar_prefetch=1,
            grid=(steps,),
            in_specs=[spec(value.shape, mark) for value, mark in operands],
            out_specs=[spec(shape, mark) for shape, _, mark in results],
            scratch_shapes=[
                pltpu.SemaphoreType.DMA(shape) if kind is None else pltpu.VMEM(shape, kind)
                for shape, kind in scratch
            ],
        ),
        out_shape=[jax.ShapeDtypeStruct(shape, kind) for shape, kind, _ in results],
        compiler_params=pltpu.CompilerParams(vmem_limit_bytes=limit * 1024 * 1024),
        cost_estimate=pl.CostEstimate(flops=flops, bytes_accessed=16_000_000, transcendentals=0),
    )(place, *[value for value, _ in operands])


def local(
    patches,
    keep_mask,
    labels,
    stem_weight,
    position_table,
    attend_in,
    attend_out,
    expand,
    contract,
    head_weight,
    vectors,
    stem_rows,
    stem_cols,
    table_rows,
    table_cols,
    attend_in_rows,
    attend_in_cols,
    attend_out_rows,
    attend_out_cols,
    expand_rows,
    expand_cols,
    contract_rows,
    contract_cols,
    head_rows,
    head_cols,
    vector_second,
):
    data_size, model_size = lax.axis_size("dp"), lax.axis_size("mp")
    links = Grid() if (data_size, model_size) == (8, 4) else Plain(data_size, model_size)
    here = links.place
    count, patch_count, _ = patches.shape
    groups = model_size
    pair = groups // 2
    image_count = count * data_size * model_size
    inverse_count = 1.0 / image_count
    row_share, _, head_share = attend_in.shape
    hidden_share = expand.shape[1]
    in_share = 3 * head_share
    slots = patch_count + 1
    padded = -(-slots // 16) * 16
    rows = count * padded
    contract_own = contract.T
    attend_own, attend_piece, expand_piece, contract_piece, squares, vector_lines = call(
        pieces_kernel,
        (0,),
        here,
        (
            (attend_in.swapaxes(0, 1), False),
            (attend_out, False),
            (expand, False),
            (contract_own, False),
            (vectors, False),
        ),
        (((row_share, D), f32, False),)
        + (((row_share, D), bf16, False),) * 3
        + (((1, 128), f32, False), ((24, D), f32, False)),
        limit=60,
    )
    attend_chain = Chain(links.gather(attend_piece))
    pixels = jnp.pad(patches, ((0, 0), (0, padded - patch_count), (0, 0))).reshape(rows, -1)
    pixels, vector_lines, expand_piece, contract_piece, head_weight = sync(
        [attend_chain], pixels, vector_lines, expand_piece, contract_piece, head_weight
    )
    expand_chain = Chain(links.gather(expand_piece))
    stream_zero, rows_one, present, facts = call(
        stem_kernel,
        (0,),
        here,
        (
            (labels, "smem"),
            (after(pixels, attend_chain.sent), False),
            (stem_weight, False),
            (position_table, False),
            (vector_lines, False),
            (keep_mask, False),
        ),
        (
            ((rows, D), f32, False),
            ((rows, D), bf16, False),
            ((count, padded), f32, False),
            ((2 * count, 128), f32, False),
        ),
        flops=2 * rows * D * D,
    )
    stream_zero, rows_one, contract_piece, head_weight = sync(
        [attend_chain, expand_chain],
        stream_zero,
        rows_one,
        contract_piece,
        head_weight,
    )
    contract_chain = Chain(links.gather(contract_piece))
    head_turned = head_weight.T
    head_low = head_turned.astype(bf16)

    head_low = sync([attend_chain, expand_chain, contract_chain], head_low)
    sync([attend_chain], contract_chain.sent, expand_chain.sent)
    attend_all = attend_chain.result
    every = tuple(range(groups))

    qkv, attended, stream_one, rows_two, stream_sum = call(
        functools.partial(attend_kernel, order=every),
        every,
        here,
        (
            (rows_one, False),
            (vector_lines, False),
            (present, False),
            (stream_zero, False),
        ),
        (
            ((groups, 3, rows, head_share), bf16, "far"),
            ((groups, rows, head_share), bf16, "far"),
            ((rows, D), f32, False),
            ((rows, D), bf16, False),
            ((2 * count, D), f32, False),
        ),
        flops=2 * rows * D * 4 * D,
        weights=attend_all,
    )
    rows_two, stream_sum = sync([expand_chain, contract_chain], rows_two, stream_sum)
    rows_two = sync([expand_chain], rows_two)
    expand_all = expand_chain.result
    active_sum, slope = call(
        functools.partial(hidden_kernel, order=every),
        every,
        here,
        (
            (rows_two, False),
            (vector_lines, False),
            (present, False),
        ),
        (
            ((groups, 2 * count, hidden_share), f32, "far"),
            ((groups, rows, hidden_share), bf16, "far"),
        ),
        (((rows, 1), f32),),
        flops=2 * rows * D * FF,
        weights=expand_all,
    )
    active_sum, slope = sync([contract_chain], active_sum, slope)
    active_sum, slope = sync([contract_chain], active_sum, slope)

    contract_all = contract_chain.result
    scratch = ()
    if len(contract_all) == 4:
        scratch = (
            ((groups, data_size // 2, 2, row_share, hidden_share), bf16),
            ((groups, 2), None),
        )
    piece, d_row, d_active_row = call(
        functools.partial(own_head_kernel, inverse_count=inverse_count),
        (0,),
        here,
        tuple((value, False) for value in (active_sum, stream_sum, facts, vector_lines, head_low))
        + tuple((value, "any" if scratch else False) for value in contract_all),
        (
            ((8 * count, D + 128), bf16, False),
            ((2 * count, D), f32, False),
            ((groups, 2 * count, hidden_share), f32, False),
        ),
        scratch,
    )

    pieces_chain = Chain(links.gather(piece))
    far_grad, near_grad, expand_bias_grad, d_rows_two = call(
        expand_back_kernel,
        (3, 1, 2, 0),
        here,
        (
            (rows_two, False),
            (slope, "far"),
            (d_active_row, "far"),
        ),
        (
            ((pair, D, hidden_share), bf16, lambda g: jnp.minimum(g, pair - 1)),
            ((pair, D, hidden_share), bf16, lambda g: jnp.maximum(g - pair, 0)),
            ((groups, 1, hidden_share), f32, "far"),
            ((rows, D), f32, False),
        ),
        (((rows, hidden_share), bf16),),
        flops=4 * rows * D * FF,
        weights=expand_all,
    )
    far_grad, near_grad, d_rows_two = sync([pieces_chain], far_grad, near_grad, d_rows_two)
    expand_sum = Chain(links.reduce(far_grad))
    d_stream, d_attend_low, vector_two = call(
        between_kernel,
        (0,),
        here,
        (
            (d_rows_two, False),
            (d_row, False),
            (present, False),
            (stream_one, False),
            (vector_lines, False),
        ),
        (
            ((rows, D), f32, False),
            ((rows, D), bf16, False),
            ((8, D), f32, False),
        ),
    )

    d_stream, d_attend_low = sync(
        [pieces_chain, (expand_sum, near_grad)], d_stream, d_attend_low
    )

    def attend_back(order, *before):
        return call(
            attend_back_kernel,
            order,
            here,
            (
                (rows_one, False),
                (qkv, "far"),
                (attended, "far"),
                (present, False),
                (d_attend_low, False),
            )
            + tuple((value, False) for value in before),
            (
                ((pair, D, D), bf16, lambda g: g),
                ((pair, 2 * count, head_share), f32, lambda g: g),
                ((rows, D), f32, False),
            ),
            (((rows, 3 * head_share), bf16), ((rows, 1), f32)),
            flops=2 * rows * D * 4 * D,
            weights=attend_all,
        )

    far_grad, heads_far, d_rows_one = attend_back((3, 1))
    far_grad, d_rows_one = sync([pieces_chain, expand_sum], far_grad, d_rows_one)
    attend_sum = Chain(links.reduce(far_grad))
    near_grad, heads_near, d_rows_one = attend_back((2, 0), d_rows_one)
    d_rows_one = sync([pieces_chain, expand_sum, (attend_sum, near_grad)], d_rows_one)
    both_far, both_near, vector_one = call(
        stem_back_kernel,
        (0,),
        here,
        (
            (after(d_rows_one, attend_sum.sent, expand_sum.sent), False),
            (d_stream, False),
            (stream_zero, False),
            (vector_lines, False),
            (pixels, False),
        ),
        (
            ((4, 128, D), bf16, False),
            ((4, 128, D), bf16, False),
            ((8 + padded, D), f32, False),
        ),
        flops=2 * rows * D * D,
    )
    pieces, both_far, both_near = sync(
        [attend_sum, expand_sum], pieces_chain.result, both_far, both_near
    )
    grad_expand = expand_sum.result
    both_sum = Chain(links.add_large(both_far, both_near))
    pieces, grad_expand, _ = sync([both_sum], pieces, grad_expand, attend_sum.sent)
    pieces = links.whole(*pieces).reshape((-1,) + piece.shape)
    pieces, grad_expand = sync([attend_sum, both_sum], pieces, grad_expand)
    steps = max(1, pieces.shape[0] // 32)
    grad_head, grad_contract, vector_last, vector_head = call(
        functools.partial(all_head_kernel, inverse_count=inverse_count),
        (0,) * steps,
        here,
        (
            (pieces.reshape((steps, -1) + piece.shape), lambda g: g),
            (vector_lines, False),
            (head_low, False),
        ),
        (
            ((CLASSES, D), f32, False),
            ((row_share, hidden_share), f32, False),
            ((8, D), f32, False),
            ((8, CLASSES), f32, False),
        ),
    )
    loss_sum = vector_head[1, 0]
    grad_expand, grad_contract = sync([attend_sum, both_sum], grad_expand, grad_contract)
    grad_attend = attend_sum.result

    names = dict(data=data_size, groups=groups, share=head_share)
    lines = layout(data_size, groups)[3]
    (sums,) = call(
        functools.partial(sums_kernel, patch_count=patch_count, **names),
        (0,),
        here,
        tuple(
            (value, False)
            for value in (
                grad_attend,
                grad_expand,
                grad_contract,
                squares,
                vector_one,
                vector_two,
                expand_bias_grad,
                heads_far,
                heads_near,
            )
        ),
        (((lines, D), f32, False),),
    )
    sums_chain = Chain(links.add(sums))
    sync([sums_chain])
    sync([sums_chain, both_sum])
    head_new, head_rows_new, head_cols_new = call(
        head_step_kernel,
        (0,),
        here,
        tuple((value, False) for value in (head_turned, grad_head, head_rows, head_cols)),
        (((CLASSES, D), f32, False), ((D,), f32, False), ((CLASSES,), f32, False)),
    )
    sync([sums_chain])
    head_new = sync([sums_chain, both_sum], head_new)
    sync([sums_chain, both_sum])
    sums = sums_chain.result
    statistics = (
        attend_in_rows,
        attend_out_cols,
        expand_rows,
        contract_cols,
        attend_in_cols,
        attend_out_rows,
        expand_cols,
        contract_rows,
    )
    *statistics, update, scalars, square_totals = call(
        functools.partial(renew_kernel, **names),
        (0,),
        here,
        tuple(
            (value, False)
            for value in (sums,) + statistics + (grad_attend, grad_expand, grad_contract)
        ),
        tuple((value.shape, f32, False) for value in statistics)
        + (
            ((3, row_share, D), f32, False),
            ((8, 128), f32, False),
            ((8, 128), f32, False),
        ),
        (((data_size, 512), f32), ((3 * groups, D), f32)),
    )
    (
        in_rows_new,
        out_cols_new,
        expand_rows_new,
        contract_cols_new,
        in_cols_new,
        out_rows_new,
        expand_cols_new,
        contract_rows_new,
    ) = statistics
    scalars_chain = Chain(links.add(scalars))
    sums = sync([scalars_chain], sums)
    sums = sync([scalars_chain, both_sum], sums)
    sums = sync([scalars_chain, both_sum], sums)
    stem_new, stem_rows_new, stem_cols_new, table_new, table_rows_new, table_cols_new = call(
        functools.partial(stem_step_kernel, padded=padded),
        (0,),
        here,
        tuple(
            (value, False)
            for value in both_sum.result
            + (stem_weight, stem_rows, stem_cols, position_table, table_rows, table_cols)
        ),
        tuple(
            (value.shape, f32, False)
            for value in (stem_weight, stem_rows, stem_cols, position_table, table_rows, table_cols)
        ),
        (((1024, D), bf16),),
    )
    stem_new, sums = sync([scalars_chain], stem_new, sums)
    grad_vector, vectors_new, second_new = call(
        functools.partial(vector_kernel, **names),
        (0,),
        here,
        tuple(
            (value, False) for value in (sums, vector_last, vector_head, vector_lines, vector_second)
        ),
        ((vectors.shape, f32, False),) * 3,
        (((24, D), f32), ((24, D), f32)),
    )
    vectors_new = sync([scalars_chain], vectors_new)
    block = call(
        functools.partial(step_kernel, sizes=(3 * D * D, D * D, D * FF, FF * D)),
        (0,),
        here,
        tuple(
            (value, False)
            for value in (
                update,
                scalars_chain.result,
                square_totals,
                attend_own,
                expand,
                contract_own,
            )
        ),
        tuple(
            (shape, kind, False)
            for shape in (
                (3, row_share, head_share),
                (head_share, row_share),
                (row_share, hidden_share),
                (row_share, hidden_share),
            )
            for kind in (f32, bf16)
        ),
    )
    in_new, in_copy, out_new, out_copy, expand_new, expand_copy, contract_new, contract_copy = block

    return (
        loss_sum,
        stem_new,
        stem_rows_new,
        stem_cols_new,
        table_new,
        table_rows_new,
        table_cols_new,
        in_new.swapaxes(0, 1),
        in_copy.swapaxes(0, 1),
        in_rows_new,
        in_cols_new,
        out_new,
        out_copy,
        out_rows_new,
        out_cols_new,
        expand_new,
        expand_copy,
        expand_rows_new,
        expand_cols_new,
        contract_new.T,
        contract_copy.T,
        contract_rows_new,
        contract_cols_new,
        head_new.T,
        head_rows_new,
        head_cols_new,
        vectors_new,
        grad_vector,
        second_new,
    )


def solution(mesh):
    placed = (
        P(ALL, None, None),
        P(ALL, None),
        P(ALL),
        P(),
        P(),
        P("dp", None, "mp"),
        P("mp", "dp"),
        P("dp", "mp"),
        P("mp", "dp"),
    ) + (P(),) * 17
    block = (P("dp", None, "mp"), P("mp", "dp"), P("dp", "mp"), P("mp", "dp"))
    given = [P()] * 7
    for spec in block:
        given += [spec, spec, P(), P()]
    given += [P()] * 6
    return jax.shard_map(
        local, mesh=mesh, in_specs=placed, out_specs=tuple(given), check_vma=False
    )
```

```python
import functools

import jax
import jax.numpy as jnp
from jax import lax
from jax.experimental import pallas as pl
from jax.experimental.pallas import tpu as pltpu
from jax.sharding import PartitionSpec as P

D = 768
HEAD_DIM = 64
FF = 3072
CLASSES = 1000

eps_norm = 1e-06
eps_one = 1e-30
eps_two = 0.001
decay_rate = 0.5
clip_level = 0.3
step_rate = 1.0
smoothing = 0.1

ALL = ("dp", "mp")
f32 = jnp.float32
bf16 = jnp.bfloat16


def after(value, *others):
    return lax.optimization_barrier((value,) + others)[0]


class Chain:
    def __init__(self, stages):
        self.stages = stages
        self.result = None
        self.sent, self.flight = next(stages)

    def advance(self, arrived):
        try:
            self.sent, self.flight = self.stages.send(arrived)
        except StopIteration as end:
            self.sent, self.flight, self.result = (), (), end.value


def sync(chains, *values):
    chains = [chain if isinstance(chain, tuple) else (chain,) for chain in chains]
    flights = [(chain[0].flight,) + chain[1:] for chain in chains]
    flights, values = lax.optimization_barrier((flights, values))
    for chain, flight in zip(chains, flights):
        chain[0].advance(flight if len(flight) > 1 else flight[0])
    return values[0] if len(values) == 1 else values


class Plain:
    blocks = None

    def __init__(self, rows, cols):
        self.rows, self.cols = rows, cols
        self.place = jnp.stack(
            [jnp.zeros((), jnp.int32)] * 4
            + [lax.axis_index("dp"), lax.axis_index("mp"), jnp.zeros((), jnp.int32)]
            + [jnp.full((), 4, jnp.int32)]
        ).astype(jnp.int32)

    def gather(self, piece):
        full = lax.all_gather(piece, ALL, axis=0)
        full = full.reshape((self.rows, self.cols) + piece.shape).swapaxes(0, 1)
        for _ in range(4):
            yield (), ()
        return (full.reshape(self.cols, self.rows * piece.shape[0], piece.shape[1]),)

    def whole(self, full):
        return full

    def reduce(self, far):
        _, near = yield (), ()
        grads = jnp.stack([near[1], far[1], near[0], far[0]])
        grads = grads.reshape(self.cols, self.rows, -1, grads.shape[2])
        grads = grads.swapaxes(0, 1).reshape((-1,) + grads.shape[2:])
        total = lax.psum_scatter(grads, ALL, scatter_dimension=0).astype(f32)
        for _ in range(3):
            total = yield (), total
        return total

    def add(self, values):
        values = lax.psum(values, ALL)
        for _ in range(5):
            values = yield (), values
        return values

    def add_large(self, far, near):
        values = lax.psum((near, far), ALL)
        for _ in range(8):
            values = yield (), values
        return values


def group_copies(place_ref, piece_refs, full_ref, sems, distance):
    near_ref, far_ref = piece_refs[2:] if distance % 2 else piece_refs[:2]
    flip = distance // 2
    x = place_ref[1]
    source = far_ref if flip else near_ref
    along_y = [
        pltpu.make_async_copy(source.at[0], full_ref.at[:, x], sems.at[0]),
        pltpu.make_async_copy(source.at[1], full_ref.at[:, 1 - x], sems.at[1]),
    ]
    along_x = [
        pltpu.make_async_copy(near_ref.at[flip], full_ref.at[:, x], sems.at[0]),
        pltpu.make_async_copy(far_ref.at[flip], full_ref.at[:, 1 - x], sems.at[1]),
    ]
    return along_y, along_x


def each_copy(place_ref, distance, choices, act):
    owner = place_ref[3] ^ (distance % 2)
    for core in range(2):

        @pl.when(owner == core)
        def _(copies=choices[core]):
            for copy in copies:
                act(copy)


def start_copy(copy):
    copy.start()


def wait_copy(copy):
    copy.wait()


def column_kernel(place_ref, *refs):
    *piece_refs, column_ref = refs
    for step, ref in enumerate(piece_refs):
        column_ref[0, lax.rem(place_ref[0] + step, len(piece_refs))] = ref[...]


class Grid:
    deep, devices, blocks = 4, 32, 8

    def __init__(self):
        dp, mp = lax.axis_index("dp"), lax.axis_index("mp")
        self.z, self.x, self.y, self.core = dp // 2, dp % 2, mp // 2, mp % 2
        self.at_first = jnp.where(self.core == 0, self.y, self.x)
        self.at_second = jnp.where(self.core == 0, self.x, self.y)
        chunk = self.core * 4 + self.at_first * 2 + self.at_second
        other_chunk = (1 - self.core) * 4 + self.at_second * 2 + self.at_first
        self.place = jnp.stack([self.z, self.x, self.y, self.core, dp, mp, chunk, other_chunk])
        self.place = self.place.astype(jnp.int32)
        self.other = self.pairs(lambda z, x, y, c: (z, x, y, 1 - c))
        self.first = self.pairs(lambda z, x, y, c: (z, x ^ c, y ^ (1 - c), c))
        self.second = self.pairs(lambda z, x, y, c: (z, x ^ (1 - c), y ^ c, c))
        self.along_x = self.pairs(lambda z, x, y, c: (z, 1 - x, y, c))
        self.along_y = self.pairs(lambda z, x, y, c: (z, x, 1 - y, c))
        self.up = [self.pairs(lambda z, x, y, c, s=s: ((z + s) % 4, x, y, c)) for s in range(4)]
        self.flip_z = [self.pairs(lambda z, x, y, c, s=s: (z ^ s, x, y, c)) for s in range(4)]

    def pairs(self, move):
        table = []
        for index in range(self.devices):
            z, x, y, c = move(index // 8, index // 4 % 2, index // 2 % 2, index % 2)
            table.append((index, ((z * 2 + x) * 2 + y) * 2 + c))
        return table

    @staticmethod
    def send(values, table):
        return lax.ppermute(values, ALL, table)

    def gather(self, piece):
        got = yield piece, [self.send(piece, self.up[-s]) for s in (1, 2, 3)]
        column = pl.pallas_call(
            column_kernel,
            in_specs=[pl.BlockSpec(memory_space=pltpu.SMEM)]
            + [pl.BlockSpec(memory_space=pltpu.VMEM)] * self.deep,
            out_specs=pl.BlockSpec(memory_space=pltpu.VMEM),
            out_shape=jax.ShapeDtypeStruct((1, self.deep) + piece.shape, piece.dtype),
        )(self.place, piece, *got)
        got = yield column, self.send(column, self.second)
        pair = jnp.concatenate([column, got])
        rest, theirs = yield pair, (self.send(pair, self.first), self.send(pair, self.other))
        rest_theirs = yield rest, self.send(rest, self.other)
        return pair, rest, theirs, rest_theirs

    def whole(self, *pieces):
        blocks, (r, c) = self.blocks, pieces[0].shape[2:]

        def body(place_ref, *refs):
            full_ref, sems = refs[-2:]
            own = place_ref[2] * 2 + place_ref[3]
            groups = [
                (i, group_copies(place_ref, refs[:4], full_ref.at[own ^ i], sems.at[i], i))
                for i in range(4)
            ]
            for act in (start_copy, wait_copy):
                for distance, choices in groups:
                    each_copy(place_ref, distance, choices, act)

        full = pl.pallas_call(
            body,
            in_specs=[pl.BlockSpec(memory_space=pltpu.SMEM)]
            + [pl.BlockSpec(memory_space=pl.ANY)] * 4,
            out_specs=pl.BlockSpec(memory_space=pltpu.VMEM),
            out_shape=jax.ShapeDtypeStruct((4, self.deep, 2, r, c), pieces[0].dtype),
            scratch_shapes=[pltpu.SemaphoreType.DMA((4, 2))],
            compiler_params=pltpu.CompilerParams(vmem_limit_bytes=60 * 1024 * 1024),
        )(self.place, *pieces)
        return full.reshape(4, blocks * r, c)

    def reduce(self, far):
        theirs, near = yield far, self.send(far, self.other)
        size, width = near.shape[1] // self.blocks, near.shape[2]
        near = near.reshape(2, self.deep, 2, size, width)
        theirs = theirs.reshape(near.shape)

        def chip(y, x):
            spot, part = (y, 0, x, 0, 0), (1, self.deep, 1, size, width)
            total = lax.dynamic_slice(near, spot, part).astype(f32)
            total = total + lax.dynamic_slice(theirs, spot, part).astype(f32)
            return total.reshape(self.deep, size, width)

        sent = jnp.stack(
            [chip(0, 1 - self.x), chip(self.core, jnp.where(self.core == 0, self.x, 1 - self.x))]
        ).astype(bf16)
        got = yield sent, self.send(sent, self.first)
        kept = chip(1 - self.core, jnp.where(self.core == 0, 1 - self.x, self.x))
        away = (kept + got[0].astype(f32)).astype(bf16)
        came = yield away, self.send(away, self.second)
        column = chip(1, self.x) + got[1].astype(f32) + came.astype(f32)
        low = column.astype(bf16)

        def level(values, step):
            return lax.dynamic_index_in_dim(values, (self.z + step) % 4, 0, keepdims=False)

        total = level(column, 0)
        for part in (yield low, [self.send(level(low, s), self.up[s]) for s in (1, 2, 3)]):
            total = total + part.astype(f32)
        return total

    def add(self, values):
        for table in (self.other, self.along_y, self.along_x, self.flip_z[1], self.flip_z[2]):
            values = values + (yield values, self.send(values, table))
        return values

    def add_large(self, far, near):
        parts = [near, (yield far, self.send(far, self.other))]

        def total(start, stop):
            return sum(part[start:stop].astype(f32) for part in parts)

        for table, half in ((self.first, 2), (self.second, 1)):
            sent = total(half, 2 * half).astype(bf16)
            parts = [part[:half] for part in parts] + [(yield sent, self.send(sent, table))]
        pile = total(0, 1).astype(bf16)
        for table in (self.flip_z[1], self.flip_z[2]):
            got = yield pile, self.send(pile, table)
            pile = (pile.astype(f32) + got.astype(f32)).astype(bf16)
        for table in (self.second, self.first):
            pile = jnp.concatenate([pile, (yield pile, self.send(pile, table))])
        return pile, (yield pile, self.send(pile, self.other))


def normal_parts(values):
    centred = values - jnp.mean(values, -1, keepdims=True)
    inverse = lax.rsqrt(jnp.mean(centred * centred, -1, keepdims=True) + eps_norm)
    return centred * inverse, inverse


def pull_normal(values, gain, grads):
    hat, inverse = normal_parts(values)
    scaled = grads * gain
    mean_one = jnp.mean(scaled, -1, keepdims=True)
    mean_two = jnp.mean(scaled * hat, -1, keepdims=True)
    below = (scaled - mean_one - hat * mean_two) * inverse
    return below, jnp.sum(grads * hat, 0, keepdims=True), jnp.sum(grads, 0, keepdims=True)


STEM_BIAS, GAIN_ONE, SHIFT_ONE, QUERY_BIAS, VALUE_BIAS, ATTEND_BIAS, GAIN_TWO, SHIFT_TWO = range(8)
EXPAND_BIAS, CONTRACT_BIAS, GAIN_LAST, SHIFT_LAST, HEAD_BIAS = 8, 12, 13, 14, 15


def line(vectors_ref, index):
    return vectors_ref[index : index + 1, :]


def to_column(present_ref, column_ref):
    padded = present_ref.shape[1]
    for image in range(present_ref.shape[0]):
        span = slice(image * padded, (image + 1) * padded)
        column_ref[span, :] = upright(present_ref[image : image + 1, :])


def to_lines(flat_ref, lines_ref):
    width = lines_ref.shape[1]
    lines_ref[...] = jnp.zeros(lines_ref.shape, f32)
    for row, start in enumerate(range(0, flat_ref.shape[0], width)):
        extent = min(width, flat_ref.shape[0] - start)
        values = flat_ref[pl.ds(start, extent)]
        lines_ref[row : row + 1, :extent] = values.reshape(1, extent)


def from_lines(lines, flat_ref):
    width = lines.shape[1]
    for row, start in enumerate(range(0, flat_ref.shape[0], width)):
        extent = min(width, flat_ref.shape[0] - start)
        flat_ref[pl.ds(start, extent)] = lines[row, :extent]


def share_of(vectors_ref, index, group, share):
    result = vectors_ref[index : index + 1, :share]
    for other in range(1, vectors_ref.shape[1] // share):
        part = vectors_ref[index : index + 1, other * share : (other + 1) * share]
        result = jnp.where(group == other, part, result)
    return result


def own_group(place_ref, order):
    step = pl.program_id(0)
    distance = order[0]
    for index, value in enumerate(order[1:], 1):
        distance = jnp.where(step == index, value, distance)
    return (place_ref[2] * 2 + place_ref[3]) ^ distance


def dot(left, right, left_dim=1, right_dim=0):
    return lax.dot_general(
        left, right, (((left_dim,), (right_dim,)), ((), ())), preferred_element_type=f32
    )


def put(count, index, line):
    spot = lax.broadcasted_iota(jnp.int32, (count, 1), 0)
    return jnp.where(spot == index, line, 0.0)


def pick(lines, index):
    spot = lax.broadcasted_iota(jnp.int32, (lines.shape[0], 1), 0)
    return jnp.sum(jnp.where(spot == index, lines, 0.0), 0, keepdims=True)


def upright(row):
    n = row.shape[1]
    more = -n % 128
    if more:
        row = jnp.concatenate([row, jnp.zeros((1, more), f32)], 1)
    return jnp.broadcast_to(row, (128, n + more)).T[:n, 0:1]


def lying(column):
    n = column.shape[0]
    wide = jnp.broadcast_to(column, (n, 128))
    more = -n % 128
    if more:
        wide = jnp.concatenate([wide, jnp.zeros((more, 128), f32)])
    return wide.T[0:1, :n]


def probabilities(query, key, visible):
    scores = dot(query, key, 1, 1) * HEAD_DIM ** (-0.5)
    scores = jnp.where(visible, scores, -1e30)
    raised = jnp.exp(scores - jnp.max(scores, -1, keepdims=True))
    return raised * (1.0 / jnp.sum(raised, -1, keepdims=True))


def head_masks(share):
    lane = lax.broadcasted_iota(jnp.int32, (1, share), 1) // HEAD_DIM
    return [lane == head for head in range(share // HEAD_DIM)]


def stacked(rows, masks):
    return jnp.concatenate([jnp.where(mask, rows, jnp.zeros((), rows.dtype)) for mask in masks])


def unstacked(every, masks):
    size = every.shape[0] // len(masks)
    result = every[:size]
    for head, mask in enumerate(masks[1:], 1):
        result = jnp.where(mask, every[head * size : (head + 1) * size], result)
    return result


def pieces_kernel(
    place_ref,
    in_ref,
    out_ref,
    expand_ref,
    contract_ref,
    vectors_ref,
    own_ref,
    attend_low_ref,
    expand_low_ref,
    contract_low_ref,
    square_ref,
    lines_ref,
):
    to_lines(vectors_ref, lines_ref)
    share = out_ref.shape[0]
    lane = lax.broadcasted_iota(jnp.int32, (1, 128), 1)
    for part in range(3):
        own_ref[:, part * share : (part + 1) * share] = in_ref[part]
    own_ref[:, 3 * share :] = out_ref[...].T
    attend_low_ref[...] = own_ref[...].astype(bf16)
    expand_low_ref[...] = expand_ref[...].astype(bf16)
    contract_low_ref[...] = contract_ref[...].astype(bf16)
    totals = jnp.zeros((1, 128), f32)
    for index, ref in enumerate((in_ref, out_ref, expand_ref, contract_ref)):
        values = ref[...]
        total = jnp.sum(values * values, keepdims=True).reshape(1, 1)
        totals = jnp.where(lane == index, total, totals)
    square_ref[...] = totals


def in_slots(table_ref, padded):
    empty = jnp.zeros((padded - table_ref.shape[0], table_ref.shape[1]), f32)
    return jnp.concatenate([table_ref[1:], table_ref[0:1], empty])


def stem_kernel(
    place_ref,
    labels_ref,
    pixels_ref,
    stem_ref,
    table_ref,
    vectors_ref,
    mask_ref,
    stream_ref,
    rows_ref,
    present_ref,
    facts_ref,
):
    count, patch_count = mask_ref.shape
    padded = present_ref.shape[1]
    low = stem_ref[...].astype(bf16)
    slot = lax.broadcasted_iota(jnp.int32, (padded, 1), 0)
    table = in_slots(table_ref, padded)
    table = table + jnp.where(slot < patch_count, line(vectors_ref, STEM_BIAS), 0.0)
    for image in range(count):
        span = slice(image * padded, (image + 1) * padded)
        stream = dot(pixels_ref[span, :], low) + table
        stream_ref[span, :] = stream
        hat, _ = normal_parts(stream)
        normed = hat * line(vectors_ref, GAIN_ONE) + line(vectors_ref, SHIFT_ONE)
        rows_ref[span, :] = normed.astype(bf16)
    lane = lax.broadcasted_iota(jnp.int32, (count, padded), 1)
    present_ref[...] = jnp.where(lane == patch_count, 1.0, 0.0)
    present_ref[:, :patch_count] = mask_ref[...].astype(f32)
    lane = lax.broadcasted_iota(jnp.int32, (1, 128), 1)
    for image in range(count):
        present = present_ref[image : image + 1, :]
        kept = jnp.sum(present, 1, keepdims=True)
        label = labels_ref[image].astype(f32)
        fact = jnp.where(lane == 0, kept, jnp.where(lane == 1, label, 0.0))
        facts_ref[image : image + 1, :] = fact
        facts_ref[count + image : count + image + 1, :] = fact


def attend_kernel(
    place_ref,
    weight,
    rows_ref,
    vectors_ref,
    present_ref,
    stream_ref,
    qkv_ref,
    attended_ref,
    stream_out_ref,
    rows_out_ref,
    sum_ref,
    *,
    order,
):
    step = pl.program_id(0)
    count, padded = present_ref.shape
    share = attended_ref.shape[2]

    group = own_group(place_ref, order)
    projected = dot(rows_ref[...], weight(0, 3 * share))
    query = projected[:, :share] + share_of(vectors_ref, QUERY_BIAS, group, share)
    query = query.astype(bf16)
    key = projected[:, share : 2 * share].astype(bf16)
    value = projected[:, 2 * share :] + share_of(vectors_ref, VALUE_BIAS, group, share)
    value = value.astype(bf16)
    qkv_ref[0, 0] = query
    qkv_ref[0, 1] = key
    qkv_ref[0, 2] = value
    masks = head_masks(share)
    for image in range(count):
        span = slice(image * padded, (image + 1) * padded)
        visible = present_ref[image : image + 1, :] > 0.5
        low = probabilities(stacked(query[span], masks), key[span], visible).astype(bf16)
        every = dot(low, value[span])
        attended_ref[0, span, :] = unstacked(every, masks).astype(bf16)
    part = dot(attended_ref[0], weight(3 * share, 4 * share), 1, 1)

    @pl.when(step == 0)
    def _():
        stream_out_ref[...] = stream_ref[...] + line(vectors_ref, ATTEND_BIAS) + part

    @pl.when(step > 0)
    def _():
        stream_out_ref[...] += part

    @pl.when(step == pl.num_programs(0) - 1)
    def _():
        hat, _ = normal_parts(stream_out_ref[...])
        rows_two = hat * line(vectors_ref, GAIN_TWO) + line(vectors_ref, SHIFT_TWO)
        rows_out_ref[...] = rows_two.astype(bf16)
        for image in range(count):
            span = slice(image * padded, (image + 1) * padded)
            here = upright(present_ref[image : image + 1, :])
            total = jnp.sum(stream_out_ref[span, :] * here, 0, keepdims=True)
            sum_ref[image : image + 1, :] = total
            sum_ref[image + count : image + count + 1, :] = total


def hidden_kernel(
    place_ref,
    weight,
    rows_ref,
    vectors_ref,
    present_ref,
    sum_ref,
    slope_ref,
    column_ref,
    *,
    order,
):
    bias = pick(vectors_ref[EXPAND_BIAS : EXPAND_BIAS + len(order), :], own_group(place_ref, order))
    hidden = dot(rows_ref[...], weight()) + bias
    first, second = 0.7978845608028654, 0.044715
    square = hidden * hidden
    half = 0.5 + 0.5 * jnp.tanh(hidden * (first + first * second * square))
    active = (hidden * half).astype(bf16)
    count, padded = present_ref.shape

    @pl.when(pl.program_id(0) == 0)
    def _():
        to_column(present_ref, column_ref)

    row = lax.broadcasted_iota(jnp.int32, (2 * count, 1), 0)
    sums = jnp.zeros(sum_ref.shape[1:], f32)
    for image in range(count):
        chooser = jnp.broadcast_to(present_ref[image : image + 1, :], (2 * count, padded))
        total = dot(chooser.astype(bf16), active[image * padded : (image + 1) * padded])
        sums = jnp.where(row % count == image, total, sums)
    sum_ref[0] = sums
    steep = hidden * (2.0 * first + 6.0 * first * second * square)
    slope = half * (1.0 + steep * (1.0 - half))
    slope_ref[0] = (slope * column_ref[...]).astype(bf16)


def expand_back_kernel(
    place_ref,
    weight,
    rows_ref,
    slope_ref,
    d_active_ref,
    far_ref,
    near_ref,
    bias_ref,
    d_rows_ref,
    d_hidden_low,
):
    step = pl.program_id(0)
    count = d_active_ref.shape[1] // 2
    padded = slope_ref.shape[1] // count
    bias = jnp.zeros((1, d_hidden_low.shape[1]), f32)
    for image in range(count):
        span = slice(image * padded, (image + 1) * padded)
        d_hidden = slope_ref[0, span, :].astype(f32) * d_active_ref[0, image : image + 1, :]
        bias = bias + jnp.sum(d_hidden, 0, keepdims=True)
        d_hidden_low[span, :] = d_hidden.astype(bf16)
    bias_ref[0] = bias
    half = pl.num_programs(0) // 2

    @pl.when(step < half)
    def _():
        far_ref[0] = dot(rows_ref[...], d_hidden_low[...], 0, 0).astype(bf16)

    @pl.when(step >= half)
    def _():
        near_ref[0] = dot(rows_ref[...], d_hidden_low[...], 0, 0).astype(bf16)

    part = dot(d_hidden_low[...], weight(), 1, 1)

    @pl.when(step == 0)
    def _():
        d_rows_ref[...] = part

    @pl.when(step > 0)
    def _():
        d_rows_ref[...] += part


def between_kernel(
    place_ref,
    d_rows_ref,
    d_row_ref,
    present_ref,
    stream_ref,
    vectors_ref,
    d_stream_ref,
    d_low_ref,
    vector_ref,
):
    count = d_row_ref.shape[0] // 2
    padded = stream_ref.shape[0] // count
    gain = line(vectors_ref, GAIN_TWO)
    below, gain, shift = pull_normal(stream_ref[...], gain, d_rows_ref[...])
    vector_ref[1:2, :] = gain
    vector_ref[2:3, :] = shift
    bias = jnp.zeros((1, below.shape[1]), f32)
    for image in range(count):
        span = slice(image * padded, (image + 1) * padded)
        here = upright(present_ref[image : image + 1, :])
        d_stream = below[span] + d_row_ref[image : image + 1, :] * here
        bias = bias + jnp.sum(d_stream, 0, keepdims=True)
        d_stream_ref[span, :] = d_stream
        d_low_ref[span, :] = d_stream.astype(bf16)
    vector_ref[0:1, :] = bias


def attend_back_kernel(
    place_ref,
    weight,
    rows_ref,
    qkv_ref,
    attended_ref,
    present_ref,
    d_low_ref,
    *refs,
):
    grad_ref, bias_ref, d_rows_ref, d_projected, column_ref = refs[-5:]
    step = pl.program_id(0)
    share = attended_ref.shape[2]
    count = bias_ref.shape[1] // 2
    padded = attended_ref.shape[1] // count
    scale = HEAD_DIM ** (-0.5)
    d_attended = dot(d_low_ref[...], weight(3 * share, 4 * share)).astype(bf16)

    @pl.when(step == 0)
    def _():
        to_column(present_ref, column_ref)

    masks = head_masks(share)
    for image in range(count):
        span = slice(image * padded, (image + 1) * padded)
        hidden = column_ref[span, :] < 0.5
        query, key, value = (qkv_ref[0, part, span, :] for part in range(3))
        query = query * jnp.asarray(scale, bf16)
        queries = stacked(query, masks)
        d_images = stacked(d_attended[span], masks)
        scores = jnp.where(hidden, -1e30, dot(key, queries, 1, 1))
        raised = jnp.exp(scores - jnp.max(scores, 0, keepdims=True))
        probs = raised * (1.0 / jnp.sum(raised, 0, keepdims=True))
        d_probs = dot(value, d_images, 1, 1)
        inner = jnp.sum(probs * d_probs, 0, keepdims=True)
        d_scores = (probs * (d_probs - inner)).astype(bf16)
        d_value = dot(probs.astype(bf16), d_images)
        d_key = dot(d_scores, queries)
        d_query = unstacked(dot(d_scores, key, 0, 0), masks) * scale
        bias_ref[0, image : image + 1, :] = jnp.sum(d_query, 0, keepdims=True)
        bias_ref[0, count + image : count + image + 1, :] = jnp.sum(d_value, 0, keepdims=True)
        d_projected[span, :share] = d_query.astype(bf16)
        d_projected[span, share : 2 * share] = d_key.astype(bf16)
        d_projected[span, 2 * share :] = d_value.astype(bf16)
    grad_ref[0, :, : 3 * share] = dot(rows_ref[...], d_projected[...], 0, 0).astype(bf16)
    grad_ref[0, :, 3 * share :] = dot(d_low_ref[...], attended_ref[0], 0, 0).astype(bf16)
    part = dot(d_projected[...], weight(0, 3 * share), 1, 1)

    @pl.when(step == 0)
    def _():
        d_rows_ref[...] = part + refs[0][...] if len(refs) > 5 else part

    @pl.when(step > 0)
    def _():
        d_rows_ref[...] += part


def stem_back_kernel(
    place_ref,
    d_rows_ref,
    d_stream_ref,
    stream_ref,
    vectors_ref,
    pixels_ref,
    far_ref,
    near_ref,
    vector_ref,
):
    rows, width = pixels_ref.shape
    gain = line(vectors_ref, GAIN_ONE)
    below, gain, shift = pull_normal(stream_ref[...], gain, d_rows_ref[...])
    vector_ref[0:1, :] = gain
    vector_ref[1:2, :] = shift
    below = below + d_stream_ref[...]
    slots = vector_ref.shape[0] - 8
    table = below[:slots]
    for image in range(1, rows // slots):
        table = table + below[image * slots : (image + 1) * slots]
    vector_ref[8:, :] = table
    stem = dot(pixels_ref[...], below.astype(bf16), 0, 0).astype(bf16)
    half, size, columns = near_ref.shape
    empty = jnp.zeros((2 * half * size - width - slots, columns), bf16)
    whole = jnp.concatenate([stem, table.astype(bf16), empty])
    for chunk in range(2 * half):
        near, far = place_ref[6] ^ chunk, place_ref[7] ^ chunk

        @pl.when(near < half)
        def _(chunk=chunk, near=near):
            near_ref[near] = whole[chunk * size : (chunk + 1) * size]

        @pl.when(far < half)
        def _(chunk=chunk, far=far):
            far_ref[far] = whole[chunk * size : (chunk + 1) * size]


def head_vectors(vectors_ref):
    rest = CLASSES - vectors_ref.shape[1]
    bias = jnp.concatenate(
        [line(vectors_ref, HEAD_BIAS), vectors_ref[HEAD_BIAS + 1 : HEAD_BIAS + 2, :rest]], 1
    )
    return line(vectors_ref, GAIN_LAST), line(vectors_ref, SHIFT_LAST), bias


def classify(pooled, labels, head, gain, shift, bias, inverse_count):
    hat, inverse = normal_parts(pooled)
    low = (hat * gain + shift).astype(bf16)
    logits = dot(low, head, 1, 1) + bias
    logits = logits - jnp.max(logits, -1, keepdims=True)
    raised = jnp.exp(logits)
    total = jnp.sum(raised, -1, keepdims=True)
    lane = lax.broadcasted_iota(jnp.int32, logits.shape, 1)
    target = jnp.where(lane == labels.astype(jnp.int32), 1.0 - smoothing, 0.0) + smoothing / CLASSES
    score = jnp.sum(target * (logits - jnp.log(total)), -1, keepdims=True)
    d_logits = (raised * (1.0 / total) - target) * inverse_count
    d_final = dot(d_logits.astype(bf16), head)
    scaled = d_final * gain
    mean_one = jnp.mean(scaled, -1, keepdims=True)
    mean_two = jnp.mean(scaled * hat, -1, keepdims=True)
    return score, low, d_logits, d_final, hat, (scaled - mean_one - hat * mean_two) * inverse


def split(values):
    high = values.astype(bf16)
    return high, (values - high.astype(f32)).astype(bf16)


def own_head_kernel(
    place_ref,
    active_ref,
    sum_ref,
    facts_ref,
    vectors_ref,
    head_ref,
    *refs,
    inverse_count,
):
    groups, twice, width = active_ref.shape
    rows = sum_ref.shape[1]
    if len(refs) == 4:
        full_ref, piece_ref, d_row_ref, d_active_ref = refs
        chosen = []
    else:
        piece_ref, d_row_ref, d_active_ref, full_ref, sems = refs[4:]
        chosen = [
            (r, group_copies(place_ref, refs[:4], full_ref.at[r], sems.at[r], r))
            for r in range(groups)
        ]
    for distance, choices in chosen:
        each_copy(place_ref, distance, choices, start_copy)
    mixed = jnp.zeros((2 * twice, rows), f32)
    for group in range(groups):
        for distance, choices in chosen[group : group + 1]:
            each_copy(place_ref, distance, choices, wait_copy)
        weight = full_ref[group].reshape(rows, width)
        mixed = mixed + dot(jnp.concatenate(split(active_ref[group])), weight, 1, 1)
    mixed = mixed[:twice] + mixed[twice:]
    kept, labels = facts_ref[:, 0:1], facts_ref[:, 1:2]
    pooled = (sum_ref[...] + mixed) / kept + line(vectors_ref, CONTRACT_BIAS)
    d_pooled = classify(
        pooled, labels, head_ref[...], *head_vectors(vectors_ref), inverse_count
    )[-1]
    d_row = d_pooled / kept
    d_row_ref[...] = d_row
    d_row_low = d_row.astype(bf16)
    first = lax.broadcasted_iota(jnp.int32, (twice, 1), 0) < twice // 2
    for group in range(groups):
        d_active_ref[group] = dot(d_row_low, full_ref[group].reshape(rows, width))
    for part, (pool, fact) in enumerate(zip(split(pooled), split(facts_ref[...]))):
        piece_ref[part * twice : (part + 1) * twice, :rows] = pool
        piece_ref[part * twice : (part + 1) * twice, rows:] = fact
    own = place_ref[2] * 2 + place_ref[3]
    for half in range(groups // 2):
        sums = jnp.where(first, active_ref[own ^ (2 * half)], active_ref[own ^ (2 * half + 1)])
        span = slice((2 + half) * twice, (3 + half) * twice)
        piece_ref[span, :rows] = sums.astype(bf16)
        piece_ref[span, rows:] = jnp.zeros((twice, piece_ref.shape[1] - rows), bf16)


def all_head_kernel(
    place_ref,
    pieces_ref,
    vectors_ref,
    head_ref,
    grad_ref,
    contract_ref,
    vector_ref,
    bias_ref,
    *,
    inverse_count,
):
    pieces = pieces_ref[0].astype(f32)
    count, rows = pieces.shape[0], vectors_ref.shape[1]
    twice = pieces.shape[1] // 4

    def part(index):
        return pieces[:, index * twice : (index + 1) * twice].reshape(count * twice, -1)

    lines = part(0) + part(1)
    pooled, kept, labels = lines[:, :rows], lines[:, rows : rows + 1], lines[:, rows + 1 : rows + 2]
    score, low, d_logits, d_final, hat, d_pooled = classify(
        pooled, labels, head_ref[...], *head_vectors(vectors_ref), inverse_count
    )
    half = lax.broadcasted_iota(jnp.int32, (count * twice, 1), 0) % twice // (twice // 2)
    once = half == 0
    d_logits = jnp.where(once, d_logits, 0.0)
    own = place_ref[5]
    active = jnp.where(own // 2 == 0, part(2)[:, :rows], part(3)[:, :rows]).astype(bf16)
    d_row = jnp.where(half == own % 2, d_pooled / kept, 0.0).astype(bf16)
    share = contract_ref.shape[0]
    place = lax.broadcasted_iota(jnp.int32, (rows, share), 0)
    lane = lax.broadcasted_iota(jnp.int32, (rows, share), 1)
    chooser = (place == lane + place_ref[4] * share).astype(f32).astype(bf16)
    d_row = dot(d_row, chooser).astype(bf16)

    def total(values):
        return jnp.sum(jnp.where(once, values, 0.0), 0, keepdims=True)

    results = (
        (grad_ref, slice(None), dot(d_logits.astype(bf16), low, 0, 0)),
        (contract_ref, slice(None), dot(d_row, active, 0, 0)),
        (vector_ref, slice(0, 1), total(d_pooled)),
        (vector_ref, slice(1, 2), total(d_final * hat)),
        (vector_ref, slice(2, 3), total(d_final)),
        (bias_ref, slice(0, 1), jnp.sum(d_logits, 0, keepdims=True)),
        (bias_ref, slice(1, 2), -total(score) + jnp.zeros((1, bias_ref.shape[1]), f32)),
    )
    for ref, span, value in results:

        @pl.when(pl.program_id(0) == 0)
        def _(ref=ref, span=span, value=value):
            ref[span, :] = value

        @pl.when(pl.program_id(0) > 0)
        def _(ref=ref, span=span, value=value):
            ref[span, :] += value


def head_step_kernel(
    place_ref,
    weight_ref,
    grad_ref,
    old_rows_ref,
    old_cols_ref,
    new_ref,
    new_rows_ref,
    new_cols_ref,
):
    new_ref[...], cols, rows = factored(
        weight_ref[...],
        grad_ref[...],
        old_cols_ref[...].reshape(1, -1),
        old_rows_ref[...].reshape(1, -1),
        True,
    )
    new_cols_ref[...] = cols[0]
    new_rows_ref[...] = rows[0]


def factored(weight, grad, down_old, across_old, turned, valid=None, count=None):
    down_old = upright(down_old)
    squared = grad * grad + eps_one
    n, m = grad.shape
    if valid is not None:
        squared = jnp.where(valid, squared, 0.0)
        n = count
    down_new = decay_rate * down_old + (1.0 - decay_rate) * (
        jnp.sum(squared, 1, keepdims=True) / m
    )
    across_new = decay_rate * across_old + (1.0 - decay_rate) * (
        jnp.sum(squared, 0, keepdims=True) / n
    )
    if turned:
        mean = jnp.sum(across_new, keepdims=True) / m
    else:
        mean = jnp.sum(down_new, keepdims=True) / n
    divisor = down_new if valid is None else jnp.where(valid, down_new, 1.0)
    update = grad * lax.rsqrt(divisor * across_new / mean)
    size = n * m
    clip = jnp.sqrt(jnp.sum(update * update, keepdims=True) / size) / clip_level
    magnitude = jnp.sqrt(jnp.sum(weight * weight, keepdims=True) / size)
    scale = step_rate * jnp.maximum(eps_two, magnitude) / jnp.maximum(1.0, clip)
    return weight - scale * update, lying(down_new), across_new


def stem_step_kernel(
    place_ref,
    near_ref,
    far_ref,
    stem_ref,
    stem_rows_ref,
    stem_cols_ref,
    table_ref,
    table_rows_ref,
    table_cols_ref,
    stem_new_ref,
    stem_rows_new_ref,
    stem_cols_new_ref,
    table_new_ref,
    table_rows_new_ref,
    table_cols_new_ref,
    both_ref,
    *,
    padded,
):
    n, slots = stem_ref.shape[0], table_ref.shape[0]
    half, size = near_ref.shape[:2]
    for chunk in range(2 * half):
        near, far = place_ref[6] ^ chunk, place_ref[7] ^ chunk
        span = slice(chunk * size, (chunk + 1) * size)

        @pl.when(near < half)
        def _(span=span, near=near):
            both_ref[span, :] = near_ref[near]

        @pl.when(far < half)
        def _(span=span, far=far):
            both_ref[span, :] = far_ref[far]

    stem_new_ref[...], rows, cols = factored(
        stem_ref[...],
        both_ref[:n, :].astype(f32),
        stem_rows_ref[...].reshape(1, -1),
        stem_cols_ref[...].reshape(1, -1),
        False,
    )
    stem_rows_new_ref[...] = rows[0]
    stem_cols_new_ref[...] = cols[0]
    old = table_rows_ref[...].reshape(1, slots)
    empty = jnp.zeros((1, padded - slots), f32)
    table, rows, cols = factored(
        in_slots(table_ref, padded),
        both_ref[n : n + padded, :].astype(f32),
        jnp.concatenate([old[:, 1:], old[:, 0:1], empty], 1),
        table_cols_ref[...].reshape(1, -1),
        False,
        lax.broadcasted_iota(jnp.int32, (padded, 1), 0) < slots,
        slots,
    )
    table_new_ref[1:] = table[: slots - 1]
    table_new_ref[0:1] = table[slots - 1 : slots]
    table_rows_new_ref[...] = jnp.concatenate(
        [rows[:, slots - 1 : slots], rows[:, : slots - 1]], 1
    )[0]
    table_cols_new_ref[...] = cols[0]


def layout(data, groups):
    return 0, data, data + 4 * groups, -(-(data + 4 * groups + 6) // 8) * 8


def across(column):
    n = column.shape[0]
    wide = jnp.broadcast_to(column, (n, 128))
    if n < 128:
        wide = jnp.concatenate([wide, jnp.zeros((128 - n, 128), f32)])
    return wide.T[0:1]


def down(row, n):
    return jnp.broadcast_to(row, (128, 128)).T[:n, 0:1]


def sums_kernel(
    place_ref,
    attend_ref,
    expand_ref,
    contract_ref,
    squares_ref,
    vector_one_ref,
    vector_two_ref,
    expand_bias_ref,
    heads_far_ref,
    heads_near_ref,
    sums_ref,
    *,
    data,
    groups,
    share,
    patch_count,
):
    block, group = place_ref[4], place_ref[5]
    own = place_ref[2] * 2 + place_ref[3]
    _, at_group, at_single, _ = layout(data, groups)
    sums_ref[...] = jnp.zeros(sums_ref.shape, f32)
    lane = lax.broadcasted_iota(jnp.int32, (1, attend_ref.shape[1]), 1)
    for index, ref in enumerate((attend_ref, expand_ref, contract_ref)):
        grad = ref[...]
        squared = grad * grad + eps_one
        span = slice(at_group + index * groups, at_group + (index + 1) * groups)
        sums_ref[span, :] = put(groups, group, jnp.sum(squared, 0, keepdims=True))
        if index == 0:
            lines = (
                jnp.sum(jnp.where(lane < 3 * share, squared, 0.0), 1, keepdims=True),
                jnp.sum(jnp.where(lane < 3 * share, 0.0, squared), 1, keepdims=True),
            )
        else:
            lines = (jnp.sum(squared, 1, keepdims=True),)
        for part, line in enumerate(lines):
            spot = (index + (index > 0) + part) * 128
            sums_ref[:data, spot : spot + 128] = put(data, block, across(line))
    sums_ref[:data, 512:640] = put(data, block, squares_ref[...])
    at_group += 3 * groups
    lines = jnp.zeros((groups, expand_bias_ref.shape[2]), f32)
    for distance in range(groups):
        lines = lines + put(groups, own ^ distance, expand_bias_ref[distance])
    sums_ref[at_group : at_group + groups, :] = lines
    count = heads_far_ref.shape[1] // 2
    for part in range(2):
        span = slice(part * count, (part + 1) * count)
        lines = jnp.zeros((groups, share), f32)
        for ref, order in ((heads_far_ref, (3, 1)), (heads_near_ref, (2, 0))):
            for step, distance in enumerate(order):
                total = jnp.sum(ref[step][span], 0, keepdims=True)
                lines = lines + put(groups, own ^ distance, total)
        sums_ref[part * groups : (part + 1) * groups, 3 * share :] = lines
    stem_bias = jnp.sum(vector_one_ref[8 : 8 + patch_count, :], 0, keepdims=True)
    singles = (stem_bias, vector_one_ref[0:2, :], vector_two_ref[0:3, :])
    for line in singles:
        sums_ref[at_single : at_single + line.shape[0], :] = line
        at_single += line.shape[0]


def vector_kernel(
    place_ref,
    sums_ref,
    last_ref,
    head_ref,
    vectors_ref,
    second_ref,
    grad_out,
    new_out,
    second_out,
    grad_ref,
    lines_ref,
    *,
    data,
    groups,
    share,
):
    to_lines(second_ref, lines_ref)
    length = second_ref.shape[0]
    _, at_group, at_single, _ = layout(data, groups)
    width = vectors_ref.shape[1]

    def single(index):
        return sums_ref[at_single + index : at_single + index + 1, :]

    def joined(part):
        lines = sums_ref[part * groups : (part + 1) * groups, 3 * share :]
        return jnp.concatenate([lines[g : g + 1] for g in range(groups)], 1)

    grad_ref[...] = jnp.zeros(grad_ref.shape, f32)
    spot = at_group + 3 * groups
    rest = CLASSES - width
    for index, value in (
        (STEM_BIAS, single(0)),
        (GAIN_ONE, single(1)),
        (SHIFT_ONE, single(2)),
        (QUERY_BIAS, joined(0)),
        (VALUE_BIAS, joined(1)),
        (ATTEND_BIAS, single(3)),
        (GAIN_TWO, single(4)),
        (SHIFT_TWO, single(5)),
        (EXPAND_BIAS, sums_ref[spot : spot + groups, :]),
        (CONTRACT_BIAS, last_ref[0:3, :]),
        (HEAD_BIAS, head_ref[0:1, :width]),
    ):
        grad_ref[index : index + value.shape[0], :] = value
    grad_ref[HEAD_BIAS + 1 : HEAD_BIAS + 2, :rest] = head_ref[0:1, width:]
    grad = grad_ref[...]
    row = lax.broadcasted_iota(jnp.int32, grad.shape, 0)
    lane = lax.broadcasted_iota(jnp.int32, grad.shape, 1)
    valid = row * width + lane < length
    second = decay_rate * lines_ref[...] + (1.0 - decay_rate) * (grad * grad + eps_one)
    update = grad * lax.rsqrt(jnp.where(valid, second, 1.0))
    total = jnp.sum(update * update, keepdims=True) / length
    square = jnp.sum(vectors_ref[...] * vectors_ref[...], keepdims=True) / length
    scale = step_rate * jnp.maximum(eps_two, jnp.sqrt(square))
    scale = scale / jnp.maximum(1.0, jnp.sqrt(total) / clip_level)
    from_lines(grad, grad_out)
    from_lines(vectors_ref[...] - scale * update, new_out)
    from_lines(second, second_out)


def renew_kernel(
    place_ref,
    sums_ref,
    in_rows_ref,
    out_cols_ref,
    expand_rows_ref,
    contract_cols_ref,
    in_cols_ref,
    out_rows_ref,
    expand_cols_ref,
    contract_rows_ref,
    attend_ref,
    expand_ref,
    contract_ref,
    in_rows_out,
    out_cols_out,
    expand_rows_out,
    contract_cols_out,
    in_cols_out,
    out_rows_out,
    expand_cols_out,
    contract_rows_out,
    update_ref,
    scalar_ref,
    square_ref,
    rows_new_ref,
    cols_new_ref,
    *,
    data,
    groups,
    share,
):
    block, group = place_ref[4], place_ref[5]
    size = attend_ref.shape[0]
    width = attend_ref.shape[1]
    _, at_group, _, _ = layout(data, groups)
    length, hidden = data * size, groups * width
    lane = lax.broadcasted_iota(jnp.int32, (1, width), 1)
    first = lane < 3 * share
    spare = lax.broadcasted_iota(jnp.int32, (1, 128), 1) < size
    for index, ref in enumerate((in_rows_ref, out_cols_ref, expand_rows_ref, contract_cols_ref)):
        for part in range(data):
            values = ref[pl.ds(part * size, size)].reshape(1, size)
            rows_new_ref[part : part + 1, index * 128 : index * 128 + size] = values
    for part in range(groups):
        span = slice(part * share, (part + 1) * share)
        for which in range(3):
            cols_new_ref[part : part + 1, which * share : (which + 1) * share] = in_cols_ref[
                which : which + 1, span
            ]
        values = out_rows_ref[pl.ds(part * share, share)].reshape(1, share)
        cols_new_ref[part : part + 1, 3 * share :] = values
        for index, ref in enumerate((expand_cols_ref, contract_rows_ref), 1):
            values = ref[pl.ds(part * width, width)].reshape(1, width)
            cols_new_ref[index * groups + part : index * groups + part + 1, :] = values
    counts = (3 * length, length, hidden, hidden)
    means = []
    for index, count in enumerate(counts):
        span = slice(index * 128, (index + 1) * 128)
        new = decay_rate * rows_new_ref[:, span]
        new = new + (1.0 - decay_rate) * (sums_ref[:data, span] / count)
        rows_new_ref[:, span] = new
        means.append(jnp.sum(jnp.where(spare, new, 0.0), keepdims=True) / length)
        out = (in_rows_out, out_cols_out, expand_rows_out, contract_cols_out)[index]
        for part in range(data):
            out[pl.ds(part * size, size)] = new[part, :size]
    for index, count in enumerate((length, length, length)):
        span = slice(index * groups, (index + 1) * groups)
        lines = sums_ref[at_group + index * groups : at_group + (index + 1) * groups, :]
        new = decay_rate * cols_new_ref[span, :] + (1.0 - decay_rate) * (lines / count)
        cols_new_ref[span, :] = new
        for part in range(groups):
            if index == 0:
                for which in range(3):
                    in_cols_out[which : which + 1, part * share : (part + 1) * share] = new[
                        part : part + 1, which * share : (which + 1) * share
                    ]
                out_rows_out[pl.ds(part * share, share)] = new[part, 3 * share :]
            else:
                out = (expand_cols_out, contract_rows_out)[index - 1]
                out[pl.ds(part * width, width)] = new[part]
        if index == 0:
            means[1] = jnp.sum(jnp.where(first, 0.0, new), keepdims=True) / length
        if index == 2:
            means[3] = jnp.sum(new, keepdims=True) / hidden
    scalars = jnp.zeros((1, 128), f32)
    place_lane = lax.broadcasted_iota(jnp.int32, (1, 128), 1)
    for index, ref in enumerate((attend_ref, expand_ref, contract_ref)):
        across_row = pick(cols_new_ref[index * groups : (index + 1) * groups, :], group)

        def row(which):
            span = slice(which * 128, (which + 1) * 128)
            return down(pick(rows_new_ref[:, span], block), size)

        if index == 0:
            denominator = jnp.where(
                first, row(0) * across_row / means[0], row(1) * across_row / means[1]
            )
        else:
            denominator = row(index + 1) * across_row / means[index + 1]
        update = ref[...] * lax.rsqrt(denominator)
        update_ref[index] = update
        squared = update * update
        if index == 0:
            totals = (jnp.where(first, squared, 0.0), jnp.where(first, 0.0, squared))
        else:
            totals = (squared,)
        for part, total in enumerate(totals):
            spot = index + (index > 0) + part
            scalars = jnp.where(place_lane == spot, jnp.sum(total, keepdims=True), scalars)
    scalar_ref[...] = jnp.broadcast_to(scalars, scalar_ref.shape)
    squares = jnp.sum(sums_ref[:data, 512:640], 0, keepdims=True)
    square_ref[...] = jnp.broadcast_to(squares, square_ref.shape)


def step_kernel(
    place_ref,
    update_ref,
    scalar_ref,
    square_ref,
    attend_ref,
    expand_ref,
    contract_ref,
    in_ref,
    in_low_ref,
    out_ref,
    out_low_ref,
    expand_new_ref,
    expand_low_ref,
    contract_new_ref,
    contract_low_ref,
    *,
    sizes,
):
    share = in_ref.shape[2]
    scales = []
    for index, size in enumerate(sizes):
        total = scalar_ref[0:1, index : index + 1]
        square = square_ref[0:1, index : index + 1]
        clip = jnp.maximum(1.0, jnp.sqrt(total / size) / clip_level)
        scales.append(step_rate * jnp.maximum(eps_two, jnp.sqrt(square / size)) / clip)
    lane = lax.broadcasted_iota(jnp.int32, (1, attend_ref.shape[1]), 1)
    scale = jnp.where(lane < 3 * share, scales[0], scales[1])
    attend = attend_ref[...] - scale * update_ref[0]
    for part in range(3):
        lines = attend[:, part * share : (part + 1) * share]
        in_ref[part] = lines
        in_low_ref[part] = lines.astype(bf16)
    out = attend[:, 3 * share :].T
    out_ref[...] = out
    out_low_ref[...] = out.astype(bf16)
    expand = expand_ref[...] - scales[2] * update_ref[1]
    expand_new_ref[...] = expand
    expand_low_ref[...] = expand.astype(bf16)
    contract = contract_ref[...] - scales[3] * update_ref[2]
    contract_new_ref[...] = contract
    contract_low_ref[...] = contract.astype(bf16)


def call(
    body, order, place, operands, results, scratch=(), flops=0, weights=None, limit=48
):
    steps = len(order)
    pieces = weights is not None and len(weights) == 4

    def distance(step):
        at = order[0]
        for index, value in enumerate(order[1:], 1):
            at = jnp.where(step == index, value, at)
        return at

    def spec(shape, mark):
        zeros = (0,) * (len(shape) - 1)
        if mark == "any":
            return pl.BlockSpec(memory_space=pl.ANY)
        if mark == "smem":
            return pl.BlockSpec(memory_space=pltpu.SMEM)
        if mark is False:
            return pl.BlockSpec(shape, lambda g, p: (0,) + zeros)
        if mark is True:
            return pl.BlockSpec(
                (1,) + shape[1:], lambda g, p: ((p[2] * 2 + p[3]) ^ distance(g),) + zeros
            )
        if mark == "far":
            return pl.BlockSpec((1,) + shape[1:], lambda g, p: (distance(g),) + zeros)
        return pl.BlockSpec((1,) + shape[1:], lambda g, p: (mark(g),) + zeros)

    operands, scratch = tuple(operands), tuple(scratch)
    kernel = body
    if weights is not None:
        operands = tuple((weight, "any" if pieces else True) for weight in weights) + operands
    if pieces:
        some = weights[0]
        height, width = some.shape[0] * some.shape[1] * some.shape[2], some.shape[3]
        full = (steps, some.shape[1], some.shape[0]) + some.shape[2:]
        scratch += ((full, some.dtype), ((steps, 2), None))

        def kernel(place_ref, *refs):
            full_ref, sems = refs[-2:]
            step = pl.program_id(0)
            copies = [
                (r, group_copies(place_ref, refs[:4], full_ref.at[i], sems.at[i], r))
                for i, r in enumerate(order)
            ]

            @pl.when(step == 0)
            def _():
                for distance, choices in copies:
                    each_copy(place_ref, distance, choices, start_copy)

            for index in range(steps):

                @pl.when(step == index)
                def _(index=index):
                    each_copy(place_ref, *copies[index], wait_copy)

            def weight(start=0, stop=width):
                return full_ref[step, :, :, :, start:stop].reshape(height, stop - start)

            body(place_ref, weight, *refs[4:-2])

    elif weights is not None:

        def kernel(place_ref, weight_ref, *refs):
            def weight(start=0, stop=weight_ref.shape[2]):
                return weight_ref[0, :, start:stop]

            body(place_ref, weight, *refs)

    return pl.pallas_call(
        kernel,
        grid_spec=pltpu.PrefetchScalarGridSpec(
            num_scalar_prefetch=1,
            grid=(steps,),
            in_specs=[spec(value.shape, mark) for value, mark in operands],
            out_specs=[spec(shape, mark) for shape, _, mark in results],
            scratch_shapes=[
                pltpu.SemaphoreType.DMA(shape) if kind is None else pltpu.VMEM(shape, kind)
                for shape, kind in scratch
            ],
        ),
        out_shape=[jax.ShapeDtypeStruct(shape, kind) for shape, kind, _ in results],
        compiler_params=pltpu.CompilerParams(vmem_limit_bytes=limit * 1024 * 1024),
        cost_estimate=pl.CostEstimate(flops=flops, bytes_accessed=16_000_000, transcendentals=0),
    )(place, *[value for value, _ in operands])


def local(
    patches,
    keep_mask,
    labels,
    stem_weight,
    position_table,
    attend_in,
    attend_out,
    expand,
    contract,
    head_weight,
    vectors,
    stem_rows,
    stem_cols,
    table_rows,
    table_cols,
    attend_in_rows,
    attend_in_cols,
    attend_out_rows,
    attend_out_cols,
    expand_rows,
    expand_cols,
    contract_rows,
    contract_cols,
    head_rows,
    head_cols,
    vector_second,
):
    data_size, model_size = lax.axis_size("dp"), lax.axis_size("mp")
    links = Grid() if (data_size, model_size) == (8, 4) else Plain(data_size, model_size)
    here = links.place
    count, patch_count, _ = patches.shape
    groups = model_size
    pair = groups // 2
    image_count = count * data_size * model_size
    inverse_count = 1.0 / image_count
    row_share, _, head_share = attend_in.shape
    hidden_share = expand.shape[1]
    in_share = 3 * head_share
    slots = patch_count + 1
    padded = -(-slots // 16) * 16
    rows = count * padded
    contract_own = contract.T
    attend_own, attend_piece, expand_piece, contract_piece, squares, vector_lines = call(
        pieces_kernel,
        (0,),
        here,
        (
            (attend_in.swapaxes(0, 1), False),
            (attend_out, False),
            (expand, False),
            (contract_own, False),
            (vectors, False),
        ),
        (((row_share, D), f32, False),)
        + (((row_share, D), bf16, False),) * 3
        + (((1, 128), f32, False), ((24, D), f32, False)),
        limit=60,
    )
    attend_chain = Chain(links.gather(attend_piece))
    pixels = jnp.pad(patches, ((0, 0), (0, padded - patch_count), (0, 0))).reshape(rows, -1)
    pixels, vector_lines, expand_piece, contract_piece, head_weight = sync(
        [attend_chain], pixels, vector_lines, expand_piece, contract_piece, head_weight
    )
    expand_chain = Chain(links.gather(expand_piece))
    stream_zero, rows_one, present, facts = call(
        stem_kernel,
        (0,),
        here,
        (
            (labels, "smem"),
            (after(pixels, attend_chain.sent), False),
            (stem_weight, False),
            (position_table, False),
            (vector_lines, False),
            (keep_mask, False),
        ),
        (
            ((rows, D), f32, False),
            ((rows, D), bf16, False),
            ((count, padded), f32, False),
            ((2 * count, 128), f32, False),
        ),
        flops=2 * rows * D * D,
    )
    stream_zero, rows_one, contract_piece, head_weight = sync(
        [attend_chain, expand_chain],
        stream_zero,
        rows_one,
        contract_piece,
        head_weight,
    )
    contract_chain = Chain(links.gather(contract_piece))
    head_turned = head_weight.T
    head_low = head_turned.astype(bf16)

    head_low = sync([attend_chain, expand_chain, contract_chain], head_low)
    sync([attend_chain], contract_chain.sent, expand_chain.sent)
    attend_all = attend_chain.result
    every = tuple(range(groups))

    qkv, attended, stream_one, rows_two, stream_sum = call(
        functools.partial(attend_kernel, order=every),
        every,
        here,
        (
            (rows_one, False),
            (vector_lines, False),
            (present, False),
            (stream_zero, False),
        ),
        (
            ((groups, 3, rows, head_share), bf16, "far"),
            ((groups, rows, head_share), bf16, "far"),
            ((rows, D), f32, False),
            ((rows, D), bf16, False),
            ((2 * count, D), f32, False),
        ),
        flops=2 * rows * D * 4 * D,
        weights=attend_all,
    )
    rows_two, stream_sum = sync([expand_chain, contract_chain], rows_two, stream_sum)
    rows_two = sync([expand_chain], rows_two)
    expand_all = expand_chain.result
    active_sum, slope = call(
        functools.partial(hidden_kernel, order=every),
        every,
        here,
        (
            (rows_two, False),
            (vector_lines, False),
            (present, False),
        ),
        (
            ((groups, 2 * count, hidden_share), f32, "far"),
            ((groups, rows, hidden_share), bf16, "far"),
        ),
        (((rows, 1), f32),),
        flops=2 * rows * D * FF,
        weights=expand_all,
    )
    active_sum, slope = sync([contract_chain], active_sum, slope)
    active_sum, slope = sync([contract_chain], active_sum, slope)

    contract_all = contract_chain.result
    scratch = ()
    if len(contract_all) == 4:
        scratch = (
            ((groups, data_size // 2, 2, row_share, hidden_share), bf16),
            ((groups, 2), None),
        )
    piece, d_row, d_active_row = call(
        functools.partial(own_head_kernel, inverse_count=inverse_count),
        (0,),
        here,
        tuple((value, False) for value in (active_sum, stream_sum, facts, vector_lines, head_low))
        + tuple((value, "any" if scratch else False) for value in contract_all),
        (
            ((8 * count, D + 128), bf16, False),
            ((2 * count, D), f32, False),
            ((groups, 2 * count, hidden_share), f32, False),
        ),
        scratch,
    )

    pieces_chain = Chain(links.gather(piece))
    far_grad, near_grad, expand_bias_grad, d_rows_two = call(
        expand_back_kernel,
        (3, 1, 2, 0),
        here,
        (
            (rows_two, False),
            (slope, "far"),
            (d_active_row, "far"),
        ),
        (
            ((pair, D, hidden_share), bf16, lambda g: jnp.minimum(g, pair - 1)),
            ((pair, D, hidden_share), bf16, lambda g: jnp.maximum(g - pair, 0)),
            ((groups, 1, hidden_share), f32, "far"),
            ((rows, D), f32, False),
        ),
        (((rows, hidden_share), bf16),),
        flops=4 * rows * D * FF,
        weights=expand_all,
    )
    far_grad, near_grad, d_rows_two = sync([pieces_chain], far_grad, near_grad, d_rows_two)
    expand_sum = Chain(links.reduce(far_grad))
    d_stream, d_attend_low, vector_two = call(
        between_kernel,
        (0,),
        here,
        (
            (d_rows_two, False),
            (d_row, False),
            (present, False),
            (stream_one, False),
            (vector_lines, False),
        ),
        (
            ((rows, D), f32, False),
            ((rows, D), bf16, False),
            ((8, D), f32, False),
        ),
    )

    d_stream, d_attend_low = sync(
        [pieces_chain, (expand_sum, near_grad)], d_stream, d_attend_low
    )

    def attend_back(order, *before):
        return call(
            attend_back_kernel,
            order,
            here,
            (
                (rows_one, False),
                (qkv, "far"),
                (attended, "far"),
                (present, False),
                (d_attend_low, False),
            )
            + tuple((value, False) for value in before),
            (
                ((pair, D, D), bf16, lambda g: g),
                ((pair, 2 * count, head_share), f32, lambda g: g),
                ((rows, D), f32, False),
            ),
            (((rows, 3 * head_share), bf16), ((rows, 1), f32)),
            flops=2 * rows * D * 4 * D,
            weights=attend_all,
        )

    far_grad, heads_far, d_rows_one = attend_back((3, 1))
    far_grad, d_rows_one = sync([pieces_chain, expand_sum], far_grad, d_rows_one)
    attend_sum = Chain(links.reduce(far_grad))
    near_grad, heads_near, d_rows_one = attend_back((2, 0), d_rows_one)
    d_rows_one = sync([pieces_chain, expand_sum, (attend_sum, near_grad)], d_rows_one)
    both_far, both_near, vector_one = call(
        stem_back_kernel,
        (0,),
        here,
        (
            (after(d_rows_one, attend_sum.sent, expand_sum.sent), False),
            (d_stream, False),
            (stream_zero, False),
            (vector_lines, False),
            (pixels, False),
        ),
        (
            ((4, 128, D), bf16, False),
            ((4, 128, D), bf16, False),
            ((8 + padded, D), f32, False),
        ),
        flops=2 * rows * D * D,
    )
    pieces, both_far, both_near = sync(
        [attend_sum, expand_sum], pieces_chain.result, both_far, both_near
    )
    grad_expand = expand_sum.result
    both_sum = Chain(links.add_large(both_far, both_near))
    pieces, grad_expand, _ = sync([both_sum], pieces, grad_expand, attend_sum.sent)
    pieces = links.whole(*pieces).reshape((-1,) + piece.shape)
    pieces, grad_expand = sync([attend_sum], pieces, grad_expand)
    pieces, grad_expand, _ = sync([both_sum], pieces, grad_expand, attend_sum.sent)
    steps = max(1, pieces.shape[0] // 32)
    grad_head, grad_contract, vector_last, vector_head = call(
        functools.partial(all_head_kernel, inverse_count=inverse_count),
        (0,) * steps,
        here,
        (
            (pieces.reshape((steps, -1) + piece.shape), lambda g: g),
            (vector_lines, False),
            (head_low, False),
        ),
        (
            ((CLASSES, D), f32, False),
            ((row_share, hidden_share), f32, False),
            ((8, D), f32, False),
            ((8, CLASSES), f32, False),
        ),
    )
    loss_sum = vector_head[1, 0]
    grad_expand, grad_contract = sync([attend_sum], grad_expand, grad_contract)
    grad_attend = attend_sum.result

    names = dict(data=data_size, groups=groups, share=head_share)
    lines = layout(data_size, groups)[3]
    (sums,) = call(
        functools.partial(sums_kernel, patch_count=patch_count, **names),
        (0,),
        here,
        tuple(
            (value, False)
            for value in (
                grad_attend,
                grad_expand,
                grad_contract,
                squares,
                vector_one,
                vector_two,
                expand_bias_grad,
                heads_far,
                heads_near,
            )
        ),
        (((lines, D), f32, False),),
    )
    sums_chain = Chain(links.add(sums))
    sync([sums_chain, both_sum])
    sync([sums_chain, both_sum])
    head_new, head_rows_new, head_cols_new = call(
        head_step_kernel,
        (0,),
        here,
        tuple((value, False) for value in (head_turned, grad_head, head_rows, head_cols)),
        (((CLASSES, D), f32, False), ((D,), f32, False), ((CLASSES,), f32, False)),
    )
    sync([sums_chain])
    head_new = sync([sums_chain, both_sum], head_new)
    sync([sums_chain, both_sum])
    sums = sums_chain.result
    statistics = (
        attend_in_rows,
        attend_out_cols,
        expand_rows,
        contract_cols,
        attend_in_cols,
        attend_out_rows,
        expand_cols,
        contract_rows,
    )
    *statistics, update, scalars, square_totals = call(
        functools.partial(renew_kernel, **names),
        (0,),
        here,
        tuple(
            (value, False)
            for value in (sums,) + statistics + (grad_attend, grad_expand, grad_contract)
        ),
        tuple((value.shape, f32, False) for value in statistics)
        + (
            ((3, row_share, D), f32, False),
            ((8, 128), f32, False),
            ((8, 128), f32, False),
        ),
        (((data_size, 512), f32), ((3 * groups, D), f32)),
    )
    (
        in_rows_new,
        out_cols_new,
        expand_rows_new,
        contract_cols_new,
        in_cols_new,
        out_rows_new,
        expand_cols_new,
        contract_rows_new,
    ) = statistics
    scalars_chain = Chain(links.add(scalars))
    sums = sync([scalars_chain], sums)
    sums = sync([scalars_chain, both_sum], sums)
    sums = sync([scalars_chain, both_sum], sums)
    stem_new, stem_rows_new, stem_cols_new, table_new, table_rows_new, table_cols_new = call(
        functools.partial(stem_step_kernel, padded=padded),
        (0,),
        here,
        tuple(
            (value, False)
            for value in both_sum.result
            + (stem_weight, stem_rows, stem_cols, position_table, table_rows, table_cols)
        ),
        tuple(
            (value.shape, f32, False)
            for value in (stem_weight, stem_rows, stem_cols, position_table, table_rows, table_cols)
        ),
        (((1024, D), bf16),),
    )
    stem_new, sums = sync([scalars_chain], stem_new, sums)
    grad_vector, vectors_new, second_new = call(
        functools.partial(vector_kernel, **names),
        (0,),
        here,
        tuple(
            (value, False) for value in (sums, vector_last, vector_head, vector_lines, vector_second)
        ),
        ((vectors.shape, f32, False),) * 3,
        (((24, D), f32), ((24, D), f32)),
    )
    vectors_new = sync([scalars_chain], vectors_new)
    block = call(
        functools.partial(step_kernel, sizes=(3 * D * D, D * D, D * FF, FF * D)),
        (0,),
        here,
        tuple(
            (value, False)
            for value in (
                update,
                scalars_chain.result,
                square_totals,
                attend_own,
                expand,
                contract_own,
            )
        ),
        tuple(
            (shape, kind, False)
            for shape in (
                (3, row_share, head_share),
                (head_share, row_share),
                (row_share, hidden_share),
                (row_share, hidden_share),
            )
            for kind in (f32, bf16)
        ),
    )
    in_new, in_copy, out_new, out_copy, expand_new, expand_copy, contract_new, contract_copy = block

    return (
        loss_sum,
        stem_new,
        stem_rows_new,
        stem_cols_new,
        table_new,
        table_rows_new,
        table_cols_new,
        in_new.swapaxes(0, 1),
        in_copy.swapaxes(0, 1),
        in_rows_new,
        in_cols_new,
        out_new,
        out_copy,
        out_rows_new,
        out_cols_new,
        expand_new,
        expand_copy,
        expand_rows_new,
        expand_cols_new,
        contract_new.T,
        contract_copy.T,
        contract_rows_new,
        contract_cols_new,
        head_new.T,
        head_rows_new,
        head_cols_new,
        vectors_new,
        grad_vector,
        second_new,
    )


def solution(mesh):
    placed = (
        P(ALL, None, None),
        P(ALL, None),
        P(ALL),
        P(),
        P(),
        P("dp", None, "mp"),
        P("mp", "dp"),
        P("dp", "mp"),
        P("mp", "dp"),
    ) + (P(),) * 17
    block = (P("dp", None, "mp"), P("mp", "dp"), P("dp", "mp"), P("mp", "dp"))
    given = [P()] * 7
    for spec in block:
        given += [spec, spec, P(), P()]
    given += [P()] * 6
    return jax.shard_map(
        local, mesh=mesh, in_specs=placed, out_specs=tuple(given), check_vma=False
    )
```

```python
import functools

import jax
import jax.numpy as jnp
from jax import lax
from jax.experimental import pallas as pl
from jax.experimental.pallas import tpu as pltpu
from jax.sharding import PartitionSpec as P

D = 768
HEAD_DIM = 64
FF = 3072
CLASSES = 1000

eps_norm = 1e-06
eps_one = 1e-30
eps_two = 0.001
decay_rate = 0.5
clip_level = 0.3
step_rate = 1.0
smoothing = 0.1

ALL = ("dp", "mp")
f32 = jnp.float32
bf16 = jnp.bfloat16


def after(value, *others):
    return lax.optimization_barrier((value,) + others)[0]


class Chain:
    def __init__(self, stages):
        self.stages = stages
        self.result = None
        self.sent, self.flight = next(stages)

    def advance(self, arrived):
        try:
            self.sent, self.flight = self.stages.send(arrived)
        except StopIteration as end:
            self.sent, self.flight, self.result = (), (), end.value


def sync(chains, *values):
    chains = [chain if isinstance(chain, tuple) else (chain,) for chain in chains]
    flights = [(chain[0].flight,) + chain[1:] for chain in chains]
    flights, values = lax.optimization_barrier((flights, values))
    for chain, flight in zip(chains, flights):
        chain[0].advance(flight if len(flight) > 1 else flight[0])
    return values[0] if len(values) == 1 else values


class Plain:
    blocks = None

    def __init__(self, rows, cols):
        self.rows, self.cols = rows, cols
        self.place = jnp.stack(
            [jnp.zeros((), jnp.int32)] * 4
            + [lax.axis_index("dp"), lax.axis_index("mp"), jnp.zeros((), jnp.int32)]
            + [jnp.full((), 4, jnp.int32)]
        ).astype(jnp.int32)

    def gather(self, piece):
        full = lax.all_gather(piece, ALL, axis=0)
        full = full.reshape((self.rows, self.cols) + piece.shape).swapaxes(0, 1)
        for _ in range(4):
            yield (), ()
        return (full.reshape(self.cols, self.rows * piece.shape[0], piece.shape[1]),)

    def whole(self, full):
        return full

    def reduce(self, far):
        _, near = yield (), ()
        grads = jnp.stack([near[1], far[1], near[0], far[0]])
        grads = grads.reshape(self.cols, self.rows, -1, grads.shape[2])
        grads = grads.swapaxes(0, 1).reshape((-1,) + grads.shape[2:])
        total = lax.psum_scatter(grads, ALL, scatter_dimension=0).astype(f32)
        for _ in range(3):
            total = yield (), total
        return total

    def add(self, values):
        values = lax.psum(values, ALL)
        for _ in range(5):
            values = yield (), values
        return values

    def add_large(self, far, near):
        values = lax.psum((near, far), ALL)
        for _ in range(8):
            values = yield (), values
        return values


def group_copies(place_ref, piece_refs, full_ref, sems, distance):
    near_ref, far_ref = piece_refs[2:] if distance % 2 else piece_refs[:2]
    flip = distance // 2
    x = place_ref[1]
    source = far_ref if flip else near_ref
    along_y = [
        pltpu.make_async_copy(source.at[0], full_ref.at[:, x], sems.at[0]),
        pltpu.make_async_copy(source.at[1], full_ref.at[:, 1 - x], sems.at[1]),
    ]
    along_x = [
        pltpu.make_async_copy(near_ref.at[flip], full_ref.at[:, x], sems.at[0]),
        pltpu.make_async_copy(far_ref.at[flip], full_ref.at[:, 1 - x], sems.at[1]),
    ]
    return along_y, along_x


def each_copy(place_ref, distance, choices, act):
    owner = place_ref[3] ^ (distance % 2)
    for core in range(2):

        @pl.when(owner == core)
        def _(copies=choices[core]):
            for copy in copies:
                act(copy)


def start_copy(copy):
    copy.start()


def wait_copy(copy):
    copy.wait()


def column_kernel(place_ref, *refs):
    *piece_refs, column_ref = refs
    for step, ref in enumerate(piece_refs):
        column_ref[0, lax.rem(place_ref[0] + step, len(piece_refs))] = ref[...]


class Grid:
    deep, devices, blocks = 4, 32, 8

    def __init__(self):
        dp, mp = lax.axis_index("dp"), lax.axis_index("mp")
        self.z, self.x, self.y, self.core = dp // 2, dp % 2, mp // 2, mp % 2
        self.at_first = jnp.where(self.core == 0, self.y, self.x)
        self.at_second = jnp.where(self.core == 0, self.x, self.y)
        chunk = self.core * 4 + self.at_first * 2 + self.at_second
        other_chunk = (1 - self.core) * 4 + self.at_second * 2 + self.at_first
        self.place = jnp.stack([self.z, self.x, self.y, self.core, dp, mp, chunk, other_chunk])
        self.place = self.place.astype(jnp.int32)
        self.other = self.pairs(lambda z, x, y, c: (z, x, y, 1 - c))
        self.first = self.pairs(lambda z, x, y, c: (z, x ^ c, y ^ (1 - c), c))
        self.second = self.pairs(lambda z, x, y, c: (z, x ^ (1 - c), y ^ c, c))
        self.along_x = self.pairs(lambda z, x, y, c: (z, 1 - x, y, c))
        self.along_y = self.pairs(lambda z, x, y, c: (z, x, 1 - y, c))
        self.up = [self.pairs(lambda z, x, y, c, s=s: ((z + s) % 4, x, y, c)) for s in range(4)]
        self.flip_z = [self.pairs(lambda z, x, y, c, s=s: (z ^ s, x, y, c)) for s in range(4)]

    def pairs(self, move):
        table = []
        for index in range(self.devices):
            z, x, y, c = move(index // 8, index // 4 % 2, index // 2 % 2, index % 2)
            table.append((index, ((z * 2 + x) * 2 + y) * 2 + c))
        return table

    @staticmethod
    def send(values, table):
        return lax.ppermute(values, ALL, table)

    def gather(self, piece):
        got = yield piece, [self.send(piece, self.up[-s]) for s in (1, 2, 3)]
        column = pl.pallas_call(
            column_kernel,
            in_specs=[pl.BlockSpec(memory_space=pltpu.SMEM)]
            + [pl.BlockSpec(memory_space=pltpu.VMEM)] * self.deep,
            out_specs=pl.BlockSpec(memory_space=pltpu.VMEM),
            out_shape=jax.ShapeDtypeStruct((1, self.deep) + piece.shape, piece.dtype),
        )(self.place, piece, *got)
        got = yield column, self.send(column, self.second)
        pair = jnp.concatenate([column, got])
        rest, theirs = yield pair, (self.send(pair, self.first), self.send(pair, self.other))
        rest_theirs = yield rest, self.send(rest, self.other)
        return pair, rest, theirs, rest_theirs

    def whole(self, *pieces):
        blocks, (r, c) = self.blocks, pieces[0].shape[2:]

        def body(place_ref, *refs):
            full_ref, sems = refs[-2:]
            own = place_ref[2] * 2 + place_ref[3]
            groups = [
                (i, group_copies(place_ref, refs[:4], full_ref.at[own ^ i], sems.at[i], i))
                for i in range(4)
            ]
            for act in (start_copy, wait_copy):
                for distance, choices in groups:
                    each_copy(place_ref, distance, choices, act)

        full = pl.pallas_call(
            body,
            in_specs=[pl.BlockSpec(memory_space=pltpu.SMEM)]
            + [pl.BlockSpec(memory_space=pl.ANY)] * 4,
            out_specs=pl.BlockSpec(memory_space=pltpu.VMEM),
            out_shape=jax.ShapeDtypeStruct((4, self.deep, 2, r, c), pieces[0].dtype),
            scratch_shapes=[pltpu.SemaphoreType.DMA((4, 2))],
            compiler_params=pltpu.CompilerParams(vmem_limit_bytes=60 * 1024 * 1024),
        )(self.place, *pieces)
        return full.reshape(4, blocks * r, c)

    def reduce(self, far):
        theirs, near = yield far, self.send(far, self.other)
        size, width = near.shape[1] // self.blocks, near.shape[2]
        near = near.reshape(2, self.deep, 2, size, width)
        theirs = theirs.reshape(near.shape)

        def chip(y, x):
            spot, part = (y, 0, x, 0, 0), (1, self.deep, 1, size, width)
            total = lax.dynamic_slice(near, spot, part).astype(f32)
            total = total + lax.dynamic_slice(theirs, spot, part).astype(f32)
            return total.reshape(self.deep, size, width)

        sent = jnp.stack(
            [chip(0, 1 - self.x), chip(self.core, jnp.where(self.core == 0, self.x, 1 - self.x))]
        ).astype(bf16)
        got = yield sent, self.send(sent, self.first)
        kept = chip(1 - self.core, jnp.where(self.core == 0, 1 - self.x, self.x))
        away = (kept + got[0].astype(f32)).astype(bf16)
        came = yield away, self.send(away, self.second)
        column = chip(1, self.x) + got[1].astype(f32) + came.astype(f32)
        low = column.astype(bf16)

        def level(values, step):
            return lax.dynamic_index_in_dim(values, (self.z + step) % 4, 0, keepdims=False)

        total = level(column, 0)
        for part in (yield low, [self.send(level(low, s), self.up[s]) for s in (1, 2, 3)]):
            total = total + part.astype(f32)
        return total

    def add(self, values):
        for table in (self.other, self.along_y, self.along_x, self.flip_z[1], self.flip_z[2]):
            values = values + (yield values, self.send(values, table))
        return values

    def add_large(self, far, near):
        parts = [near, (yield far, self.send(far, self.other))]

        def total(start, stop):
            return sum(part[start:stop].astype(f32) for part in parts)

        for table, half in ((self.first, 2), (self.second, 1)):
            sent = total(half, 2 * half).astype(bf16)
            parts = [part[:half] for part in parts] + [(yield sent, self.send(sent, table))]
        pile = total(0, 1).astype(bf16)
        for table in (self.flip_z[1], self.flip_z[2]):
            got = yield pile, self.send(pile, table)
            pile = (pile.astype(f32) + got.astype(f32)).astype(bf16)
        for table in (self.second, self.first):
            pile = jnp.concatenate([pile, (yield pile, self.send(pile, table))])
        return pile, (yield pile, self.send(pile, self.other))


def normal_parts(values):
    centred = values - jnp.mean(values, -1, keepdims=True)
    inverse = lax.rsqrt(jnp.mean(centred * centred, -1, keepdims=True) + eps_norm)
    return centred * inverse, inverse


def pull_normal(values, gain, grads):
    hat, inverse = normal_parts(values)
    scaled = grads * gain
    mean_one = jnp.mean(scaled, -1, keepdims=True)
    mean_two = jnp.mean(scaled * hat, -1, keepdims=True)
    below = (scaled - mean_one - hat * mean_two) * inverse
    return below, jnp.sum(grads * hat, 0, keepdims=True), jnp.sum(grads, 0, keepdims=True)


STEM_BIAS, GAIN_ONE, SHIFT_ONE, QUERY_BIAS, VALUE_BIAS, ATTEND_BIAS, GAIN_TWO, SHIFT_TWO = range(8)
EXPAND_BIAS, CONTRACT_BIAS, GAIN_LAST, SHIFT_LAST, HEAD_BIAS = 8, 12, 13, 14, 15


def line(vectors_ref, index):
    return vectors_ref[index : index + 1, :]


def to_column(present_ref, column_ref):
    padded = present_ref.shape[1]
    for image in range(present_ref.shape[0]):
        span = slice(image * padded, (image + 1) * padded)
        column_ref[span, :] = upright(present_ref[image : image + 1, :])


def to_lines(flat_ref, lines_ref):
    width = lines_ref.shape[1]
    lines_ref[...] = jnp.zeros(lines_ref.shape, f32)
    for row, start in enumerate(range(0, flat_ref.shape[0], width)):
        extent = min(width, flat_ref.shape[0] - start)
        values = flat_ref[pl.ds(start, extent)]
        lines_ref[row : row + 1, :extent] = values.reshape(1, extent)


def from_lines(lines, flat_ref):
    width = lines.shape[1]
    for row, start in enumerate(range(0, flat_ref.shape[0], width)):
        extent = min(width, flat_ref.shape[0] - start)
        flat_ref[pl.ds(start, extent)] = lines[row, :extent]


def share_of(vectors_ref, index, group, share):
    result = vectors_ref[index : index + 1, :share]
    for other in range(1, vectors_ref.shape[1] // share):
        part = vectors_ref[index : index + 1, other * share : (other + 1) * share]
        result = jnp.where(group == other, part, result)
    return result


def own_group(place_ref, order):
    step = pl.program_id(0)
    distance = order[0]
    for index, value in enumerate(order[1:], 1):
        distance = jnp.where(step == index, value, distance)
    return (place_ref[2] * 2 + place_ref[3]) ^ distance


def dot(left, right, left_dim=1, right_dim=0):
    return lax.dot_general(
        left, right, (((left_dim,), (right_dim,)), ((), ())), preferred_element_type=f32
    )


def put(count, index, line):
    spot = lax.broadcasted_iota(jnp.int32, (count, 1), 0)
    return jnp.where(spot == index, line, 0.0)


def pick(lines, index):
    spot = lax.broadcasted_iota(jnp.int32, (lines.shape[0], 1), 0)
    return jnp.sum(jnp.where(spot == index, lines, 0.0), 0, keepdims=True)


def upright(row):
    n = row.shape[1]
    more = -n % 128
    if more:
        row = jnp.concatenate([row, jnp.zeros((1, more), f32)], 1)
    return jnp.broadcast_to(row, (128, n + more)).T[:n, 0:1]


def lying(column):
    n = column.shape[0]
    wide = jnp.broadcast_to(column, (n, 128))
    more = -n % 128
    if more:
        wide = jnp.concatenate([wide, jnp.zeros((more, 128), f32)])
    return wide.T[0:1, :n]


def probabilities(query, key, visible):
    scores = dot(query, key, 1, 1) * HEAD_DIM ** (-0.5)
    scores = jnp.where(visible, scores, -1e30)
    raised = jnp.exp(scores - jnp.max(scores, -1, keepdims=True))
    return raised * (1.0 / jnp.sum(raised, -1, keepdims=True))


def head_masks(share):
    lane = lax.broadcasted_iota(jnp.int32, (1, share), 1) // HEAD_DIM
    return [lane == head for head in range(share // HEAD_DIM)]


def stacked(rows, masks):
    return jnp.concatenate([jnp.where(mask, rows, jnp.zeros((), rows.dtype)) for mask in masks])


def unstacked(every, masks):
    size = every.shape[0] // len(masks)
    result = every[:size]
    for head, mask in enumerate(masks[1:], 1):
        result = jnp.where(mask, every[head * size : (head + 1) * size], result)
    return result


def pieces_kernel(
    place_ref,
    in_ref,
    out_ref,
    expand_ref,
    contract_ref,
    vectors_ref,
    own_ref,
    attend_low_ref,
    expand_low_ref,
    contract_low_ref,
    square_ref,
    lines_ref,
):
    to_lines(vectors_ref, lines_ref)
    share = out_ref.shape[0]
    lane = lax.broadcasted_iota(jnp.int32, (1, 128), 1)
    for part in range(3):
        own_ref[:, part * share : (part + 1) * share] = in_ref[part]
    own_ref[:, 3 * share :] = out_ref[...].T
    attend_low_ref[...] = own_ref[...].astype(bf16)
    expand_low_ref[...] = expand_ref[...].astype(bf16)
    contract_low_ref[...] = contract_ref[...].astype(bf16)
    totals = jnp.zeros((1, 128), f32)
    for index, ref in enumerate((in_ref, out_ref, expand_ref, contract_ref)):
        values = ref[...]
        total = jnp.sum(values * values, keepdims=True).reshape(1, 1)
        totals = jnp.where(lane == index, total, totals)
    square_ref[...] = totals


def in_slots(table_ref, padded):
    empty = jnp.zeros((padded - table_ref.shape[0], table_ref.shape[1]), f32)
    return jnp.concatenate([table_ref[1:], table_ref[0:1], empty])


def stem_kernel(
    place_ref,
    labels_ref,
    pixels_ref,
    stem_ref,
    table_ref,
    vectors_ref,
    mask_ref,
    stream_ref,
    rows_ref,
    present_ref,
    facts_ref,
):
    count, patch_count = mask_ref.shape
    padded = present_ref.shape[1]
    low = stem_ref[...].astype(bf16)
    slot = lax.broadcasted_iota(jnp.int32, (padded, 1), 0)
    table = in_slots(table_ref, padded)
    table = table + jnp.where(slot < patch_count, line(vectors_ref, STEM_BIAS), 0.0)
    for image in range(count):
        span = slice(image * padded, (image + 1) * padded)
        stream = dot(pixels_ref[span, :], low) + table
        stream_ref[span, :] = stream
        hat, _ = normal_parts(stream)
        normed = hat * line(vectors_ref, GAIN_ONE) + line(vectors_ref, SHIFT_ONE)
        rows_ref[span, :] = normed.astype(bf16)
    lane = lax.broadcasted_iota(jnp.int32, (count, padded), 1)
    present_ref[...] = jnp.where(lane == patch_count, 1.0, 0.0)
    present_ref[:, :patch_count] = mask_ref[...].astype(f32)
    lane = lax.broadcasted_iota(jnp.int32, (1, 128), 1)
    for image in range(count):
        present = present_ref[image : image + 1, :]
        kept = jnp.sum(present, 1, keepdims=True)
        label = labels_ref[image].astype(f32)
        fact = jnp.where(lane == 0, kept, jnp.where(lane == 1, label, 0.0))
        facts_ref[image : image + 1, :] = fact
        facts_ref[count + image : count + image + 1, :] = fact


def attend_kernel(
    place_ref,
    weight,
    rows_ref,
    vectors_ref,
    present_ref,
    stream_ref,
    qkv_ref,
    attended_ref,
    stream_out_ref,
    rows_out_ref,
    sum_ref,
    stream_here,
    sem,
    *,
    order,
):
    step = pl.program_id(0)
    count, padded = present_ref.shape
    share = attended_ref.shape[2]

    late = pltpu.make_async_copy(stream_ref, stream_here, sem.at[0])

    @pl.when(step == 0)
    def _():
        late.start()

    group = own_group(place_ref, order)
    projected = dot(rows_ref[...], weight(0, 3 * share))
    query = projected[:, :share] + share_of(vectors_ref, QUERY_BIAS, group, share)
    query = query.astype(bf16)
    key = projected[:, share : 2 * share].astype(bf16)
    value = projected[:, 2 * share :] + share_of(vectors_ref, VALUE_BIAS, group, share)
    value = value.astype(bf16)
    qkv_ref[0, 0] = query
    qkv_ref[0, 1] = key
    qkv_ref[0, 2] = value
    masks = head_masks(share)
    for image in range(count):
        span = slice(image * padded, (image + 1) * padded)
        visible = present_ref[image : image + 1, :] > 0.5
        low = probabilities(stacked(query[span], masks), key[span], visible).astype(bf16)
        every = dot(low, value[span])
        attended_ref[0, span, :] = unstacked(every, masks).astype(bf16)
    part = dot(attended_ref[0], weight(3 * share, 4 * share), 1, 1)

    @pl.when(step == 0)
    def _():
        stream_out_ref[...] = part

    @pl.when(step > 0)
    def _():
        stream_out_ref[...] += part

    @pl.when(step == pl.num_programs(0) - 1)
    def _():
        late.wait()
        stream_out_ref[...] += stream_here[...] + line(vectors_ref, ATTEND_BIAS)
        hat, _ = normal_parts(stream_out_ref[...])
        rows_two = hat * line(vectors_ref, GAIN_TWO) + line(vectors_ref, SHIFT_TWO)
        rows_out_ref[...] = rows_two.astype(bf16)
        for image in range(count):
            span = slice(image * padded, (image + 1) * padded)
            here = upright(present_ref[image : image + 1, :])
            total = jnp.sum(stream_out_ref[span, :] * here, 0, keepdims=True)
            sum_ref[image : image + 1, :] = total
            sum_ref[image + count : image + count + 1, :] = total


def hidden_kernel(
    place_ref,
    weight,
    rows_ref,
    vectors_ref,
    present_ref,
    sum_ref,
    slope_ref,
    column_ref,
    *,
    order,
):
    bias = pick(vectors_ref[EXPAND_BIAS : EXPAND_BIAS + len(order), :], own_group(place_ref, order))
    hidden = dot(rows_ref[...], weight()) + bias
    first, second = 0.7978845608028654, 0.044715
    square = hidden * hidden
    half = 0.5 + 0.5 * jnp.tanh(hidden * (first + first * second * square))
    active = (hidden * half).astype(bf16)
    count, padded = present_ref.shape

    @pl.when(pl.program_id(0) == 0)
    def _():
        to_column(present_ref, column_ref)

    row = lax.broadcasted_iota(jnp.int32, (2 * count, 1), 0)
    sums = jnp.zeros(sum_ref.shape[1:], f32)
    for image in range(count):
        chooser = jnp.broadcast_to(present_ref[image : image + 1, :], (2 * count, padded))
        total = dot(chooser.astype(bf16), active[image * padded : (image + 1) * padded])
        sums = jnp.where(row % count == image, total, sums)
    sum_ref[0] = sums
    steep = hidden * (2.0 * first + 6.0 * first * second * square)
    slope = half * (1.0 + steep * (1.0 - half))
    slope_ref[0] = (slope * column_ref[...]).astype(bf16)


def expand_back_kernel(
    place_ref,
    weight,
    rows_ref,
    slope_ref,
    d_active_ref,
    far_ref,
    near_ref,
    bias_ref,
    d_rows_ref,
    d_hidden_low,
):
    step = pl.program_id(0)
    count = d_active_ref.shape[1] // 2
    padded = slope_ref.shape[1] // count
    bias = jnp.zeros((1, d_hidden_low.shape[1]), f32)
    for image in range(count):
        span = slice(image * padded, (image + 1) * padded)
        d_hidden = slope_ref[0, span, :].astype(f32) * d_active_ref[0, image : image + 1, :]
        bias = bias + jnp.sum(d_hidden, 0, keepdims=True)
        d_hidden_low[span, :] = d_hidden.astype(bf16)
    bias_ref[0] = bias
    half = pl.num_programs(0) // 2

    @pl.when(step < half)
    def _():
        far_ref[0] = dot(rows_ref[...], d_hidden_low[...], 0, 0).astype(bf16)

    @pl.when(step >= half)
    def _():
        near_ref[0] = dot(rows_ref[...], d_hidden_low[...], 0, 0).astype(bf16)

    part = dot(d_hidden_low[...], weight(), 1, 1)

    @pl.when(step == 0)
    def _():
        d_rows_ref[...] = part

    @pl.when(step > 0)
    def _():
        d_rows_ref[...] += part


def between_kernel(
    place_ref,
    d_rows_ref,
    d_row_ref,
    present_ref,
    stream_ref,
    vectors_ref,
    d_stream_ref,
    d_low_ref,
    vector_ref,
):
    count = d_row_ref.shape[0] // 2
    padded = stream_ref.shape[0] // count
    gain = line(vectors_ref, GAIN_TWO)
    below, gain, shift = pull_normal(stream_ref[...], gain, d_rows_ref[...])
    vector_ref[1:2, :] = gain
    vector_ref[2:3, :] = shift
    bias = jnp.zeros((1, below.shape[1]), f32)
    for image in range(count):
        span = slice(image * padded, (image + 1) * padded)
        here = upright(present_ref[image : image + 1, :])
        d_stream = below[span] + d_row_ref[image : image + 1, :] * here
        bias = bias + jnp.sum(d_stream, 0, keepdims=True)
        d_stream_ref[span, :] = d_stream
        d_low_ref[span, :] = d_stream.astype(bf16)
    vector_ref[0:1, :] = bias


def attend_back_kernel(
    place_ref,
    weight,
    rows_ref,
    qkv_ref,
    attended_ref,
    present_ref,
    d_low_ref,
    *refs,
):
    step = pl.program_id(0)
    late = None
    if len(refs) > 5:
        late = pltpu.make_async_copy(refs[0], refs[-2], refs[-1].at[0])
        given, refs = refs[-2], refs[1:-2]

        @pl.when(step == 0)
        def _():
            late.start()

    grad_ref, bias_ref, d_rows_ref, d_projected, column_ref = refs
    share = attended_ref.shape[2]
    count = bias_ref.shape[1] // 2
    padded = attended_ref.shape[1] // count
    scale = HEAD_DIM ** (-0.5)
    d_attended = dot(d_low_ref[...], weight(3 * share, 4 * share)).astype(bf16)

    @pl.when(step == 0)
    def _():
        to_column(present_ref, column_ref)

    masks = head_masks(share)
    for image in range(count):
        span = slice(image * padded, (image + 1) * padded)
        hidden = column_ref[span, :] < 0.5
        query, key, value = (qkv_ref[0, part, span, :] for part in range(3))
        query = query * jnp.asarray(scale, bf16)
        queries = stacked(query, masks)
        d_images = stacked(d_attended[span], masks)
        scores = jnp.where(hidden, -1e30, dot(key, queries, 1, 1))
        raised = jnp.exp(scores - jnp.max(scores, 0, keepdims=True))
        probs = raised * (1.0 / jnp.sum(raised, 0, keepdims=True))
        d_probs = dot(value, d_images, 1, 1)
        inner = jnp.sum(probs * d_probs, 0, keepdims=True)
        d_scores = (probs * (d_probs - inner)).astype(bf16)
        d_value = dot(probs.astype(bf16), d_images)
        d_key = dot(d_scores, queries)
        d_query = unstacked(dot(d_scores, key, 0, 0), masks) * scale
        bias_ref[0, image : image + 1, :] = jnp.sum(d_query, 0, keepdims=True)
        bias_ref[0, count + image : count + image + 1, :] = jnp.sum(d_value, 0, keepdims=True)
        d_projected[span, :share] = d_query.astype(bf16)
        d_projected[span, share : 2 * share] = d_key.astype(bf16)
        d_projected[span, 2 * share :] = d_value.astype(bf16)
    grad_ref[0, :, : 3 * share] = dot(rows_ref[...], d_projected[...], 0, 0).astype(bf16)
    grad_ref[0, :, 3 * share :] = dot(d_low_ref[...], attended_ref[0], 0, 0).astype(bf16)
    part = dot(d_projected[...], weight(0, 3 * share), 1, 1)

    @pl.when(step == 0)
    def _():
        d_rows_ref[...] = part

    @pl.when(step > 0)
    def _():
        d_rows_ref[...] += part

    if late is not None:

        @pl.when(step == pl.num_programs(0) - 1)
        def _():
            late.wait()
            d_rows_ref[...] += given[...]


def stem_back_kernel(
    place_ref,
    d_rows_ref,
    d_stream_ref,
    stream_ref,
    vectors_ref,
    pixels_ref,
    far_ref,
    near_ref,
    vector_ref,
):
    rows, width = pixels_ref.shape
    gain = line(vectors_ref, GAIN_ONE)
    below, gain, shift = pull_normal(stream_ref[...], gain, d_rows_ref[...])
    vector_ref[0:1, :] = gain
    vector_ref[1:2, :] = shift
    below = below + d_stream_ref[...]
    slots = vector_ref.shape[0] - 8
    table = below[:slots]
    for image in range(1, rows // slots):
        table = table + below[image * slots : (image + 1) * slots]
    vector_ref[8:, :] = table
    stem = dot(pixels_ref[...], below.astype(bf16), 0, 0).astype(bf16)
    half, size, columns = near_ref.shape
    empty = jnp.zeros((2 * half * size - width - slots, columns), bf16)
    whole = jnp.concatenate([stem, table.astype(bf16), empty])
    for chunk in range(2 * half):
        near, far = place_ref[6] ^ chunk, place_ref[7] ^ chunk

        @pl.when(near < half)
        def _(chunk=chunk, near=near):
            near_ref[near] = whole[chunk * size : (chunk + 1) * size]

        @pl.when(far < half)
        def _(chunk=chunk, far=far):
            far_ref[far] = whole[chunk * size : (chunk + 1) * size]


def head_vectors(vectors_ref):
    rest = CLASSES - vectors_ref.shape[1]
    bias = jnp.concatenate(
        [line(vectors_ref, HEAD_BIAS), vectors_ref[HEAD_BIAS + 1 : HEAD_BIAS + 2, :rest]], 1
    )
    return line(vectors_ref, GAIN_LAST), line(vectors_ref, SHIFT_LAST), bias


def classify(pooled, labels, head, gain, shift, bias, inverse_count):
    hat, inverse = normal_parts(pooled)
    low = (hat * gain + shift).astype(bf16)
    logits = dot(low, head, 1, 1) + bias
    logits = logits - jnp.max(logits, -1, keepdims=True)
    raised = jnp.exp(logits)
    total = jnp.sum(raised, -1, keepdims=True)
    lane = lax.broadcasted_iota(jnp.int32, logits.shape, 1)
    target = jnp.where(lane == labels.astype(jnp.int32), 1.0 - smoothing, 0.0) + smoothing / CLASSES
    score = jnp.sum(target * (logits - jnp.log(total)), -1, keepdims=True)
    d_logits = (raised * (1.0 / total) - target) * inverse_count
    d_final = dot(d_logits.astype(bf16), head)
    scaled = d_final * gain
    mean_one = jnp.mean(scaled, -1, keepdims=True)
    mean_two = jnp.mean(scaled * hat, -1, keepdims=True)
    return score, low, d_logits, d_final, hat, (scaled - mean_one - hat * mean_two) * inverse


def split(values):
    high = values.astype(bf16)
    return high, (values - high.astype(f32)).astype(bf16)


def own_head_kernel(
    place_ref,
    active_ref,
    sum_ref,
    facts_ref,
    vectors_ref,
    head_ref,
    *refs,
    inverse_count,
):
    groups, twice, width = active_ref.shape
    rows = sum_ref.shape[1]
    if len(refs) == 4:
        full_ref, piece_ref, d_row_ref, d_active_ref = refs
        chosen = []
    else:
        piece_ref, d_row_ref, d_active_ref, full_ref, sems = refs[4:]
        chosen = [
            (r, group_copies(place_ref, refs[:4], full_ref.at[r], sems.at[r], r))
            for r in range(groups)
        ]
    for distance, choices in chosen:
        each_copy(place_ref, distance, choices, start_copy)
    mixed = jnp.zeros((2 * twice, rows), f32)
    for group in range(groups):
        for distance, choices in chosen[group : group + 1]:
            each_copy(place_ref, distance, choices, wait_copy)
        weight = full_ref[group].reshape(rows, width)
        mixed = mixed + dot(jnp.concatenate(split(active_ref[group])), weight, 1, 1)
    mixed = mixed[:twice] + mixed[twice:]
    kept, labels = facts_ref[:, 0:1], facts_ref[:, 1:2]
    pooled = (sum_ref[...] + mixed) / kept + line(vectors_ref, CONTRACT_BIAS)
    d_pooled = classify(
        pooled, labels, head_ref[...], *head_vectors(vectors_ref), inverse_count
    )[-1]
    d_row = d_pooled / kept
    d_row_ref[...] = d_row
    d_row_low = d_row.astype(bf16)
    first = lax.broadcasted_iota(jnp.int32, (twice, 1), 0) < twice // 2
    for group in range(groups):
        d_active_ref[group] = dot(d_row_low, full_ref[group].reshape(rows, width))
    for part, (pool, fact) in enumerate(zip(split(pooled), split(facts_ref[...]))):
        piece_ref[part * twice : (part + 1) * twice, :rows] = pool
        piece_ref[part * twice : (part + 1) * twice, rows:] = fact
    own = place_ref[2] * 2 + place_ref[3]
    for half in range(groups // 2):
        sums = jnp.where(first, active_ref[own ^ (2 * half)], active_ref[own ^ (2 * half + 1)])
        span = slice((2 + half) * twice, (3 + half) * twice)
        piece_ref[span, :rows] = sums.astype(bf16)
        piece_ref[span, rows:] = jnp.zeros((twice, piece_ref.shape[1] - rows), bf16)


def all_head_kernel(
    place_ref,
    pieces_ref,
    vectors_ref,
    head_ref,
    grad_ref,
    contract_ref,
    vector_ref,
    bias_ref,
    *,
    inverse_count,
):
    pieces = pieces_ref[0].astype(f32)
    count, rows = pieces.shape[0], vectors_ref.shape[1]
    twice = pieces.shape[1] // 4

    def part(index):
        return pieces[:, index * twice : (index + 1) * twice].reshape(count * twice, -1)

    lines = part(0) + part(1)
    pooled, kept, labels = lines[:, :rows], lines[:, rows : rows + 1], lines[:, rows + 1 : rows + 2]
    score, low, d_logits, d_final, hat, d_pooled = classify(
        pooled, labels, head_ref[...], *head_vectors(vectors_ref), inverse_count
    )
    half = lax.broadcasted_iota(jnp.int32, (count * twice, 1), 0) % twice // (twice // 2)
    once = half == 0
    d_logits = jnp.where(once, d_logits, 0.0)
    own = place_ref[5]
    active = jnp.where(own // 2 == 0, part(2)[:, :rows], part(3)[:, :rows]).astype(bf16)
    d_row = jnp.where(half == own % 2, d_pooled / kept, 0.0).astype(bf16)
    share = contract_ref.shape[0]
    place = lax.broadcasted_iota(jnp.int32, (rows, share), 0)
    lane = lax.broadcasted_iota(jnp.int32, (rows, share), 1)
    chooser = (place == lane + place_ref[4] * share).astype(f32).astype(bf16)
    d_row = dot(d_row, chooser).astype(bf16)

    def total(values):
        return jnp.sum(jnp.where(once, values, 0.0), 0, keepdims=True)

    results = (
        (grad_ref, slice(None), dot(d_logits.astype(bf16), low, 0, 0)),
        (contract_ref, slice(None), dot(d_row, active, 0, 0)),
        (vector_ref, slice(0, 1), total(d_pooled)),
        (vector_ref, slice(1, 2), total(d_final * hat)),
        (vector_ref, slice(2, 3), total(d_final)),
        (bias_ref, slice(0, 1), jnp.sum(d_logits, 0, keepdims=True)),
        (bias_ref, slice(1, 2), -total(score) + jnp.zeros((1, bias_ref.shape[1]), f32)),
    )
    for ref, span, value in results:

        @pl.when(pl.program_id(0) == 0)
        def _(ref=ref, span=span, value=value):
            ref[span, :] = value

        @pl.when(pl.program_id(0) > 0)
        def _(ref=ref, span=span, value=value):
            ref[span, :] += value


def head_step_kernel(
    place_ref,
    weight_ref,
    grad_ref,
    old_rows_ref,
    old_cols_ref,
    new_ref,
    new_rows_ref,
    new_cols_ref,
):
    new_ref[...], cols, rows = factored(
        weight_ref[...],
        grad_ref[...],
        old_cols_ref[...].reshape(1, -1),
        old_rows_ref[...].reshape(1, -1),
        True,
    )
    new_cols_ref[...] = cols[0]
    new_rows_ref[...] = rows[0]


def factored(weight, grad, down_old, across_old, turned, valid=None, count=None):
    down_old = upright(down_old)
    squared = grad * grad + eps_one
    n, m = grad.shape
    if valid is not None:
        squared = jnp.where(valid, squared, 0.0)
        n = count
    down_new = decay_rate * down_old + (1.0 - decay_rate) * (
        jnp.sum(squared, 1, keepdims=True) / m
    )
    across_new = decay_rate * across_old + (1.0 - decay_rate) * (
        jnp.sum(squared, 0, keepdims=True) / n
    )
    if turned:
        mean = jnp.sum(across_new, keepdims=True) / m
    else:
        mean = jnp.sum(down_new, keepdims=True) / n
    divisor = down_new if valid is None else jnp.where(valid, down_new, 1.0)
    update = grad * lax.rsqrt(divisor * across_new / mean)
    size = n * m
    clip = jnp.sqrt(jnp.sum(update * update, keepdims=True) / size) / clip_level
    magnitude = jnp.sqrt(jnp.sum(weight * weight, keepdims=True) / size)
    scale = step_rate * jnp.maximum(eps_two, magnitude) / jnp.maximum(1.0, clip)
    return weight - scale * update, lying(down_new), across_new


def stem_step_kernel(
    place_ref,
    near_ref,
    far_ref,
    stem_ref,
    stem_rows_ref,
    stem_cols_ref,
    table_ref,
    table_rows_ref,
    table_cols_ref,
    stem_new_ref,
    stem_rows_new_ref,
    stem_cols_new_ref,
    table_new_ref,
    table_rows_new_ref,
    table_cols_new_ref,
    both_ref,
    *,
    padded,
):
    n, slots = stem_ref.shape[0], table_ref.shape[0]
    half, size = near_ref.shape[:2]
    for chunk in range(2 * half):
        near, far = place_ref[6] ^ chunk, place_ref[7] ^ chunk
        span = slice(chunk * size, (chunk + 1) * size)

        @pl.when(near < half)
        def _(span=span, near=near):
            both_ref[span, :] = near_ref[near]

        @pl.when(far < half)
        def _(span=span, far=far):
            both_ref[span, :] = far_ref[far]

    stem_new_ref[...], rows, cols = factored(
        stem_ref[...],
        both_ref[:n, :].astype(f32),
        stem_rows_ref[...].reshape(1, -1),
        stem_cols_ref[...].reshape(1, -1),
        False,
    )
    stem_rows_new_ref[...] = rows[0]
    stem_cols_new_ref[...] = cols[0]
    old = table_rows_ref[...].reshape(1, slots)
    empty = jnp.zeros((1, padded - slots), f32)
    table, rows, cols = factored(
        in_slots(table_ref, padded),
        both_ref[n : n + padded, :].astype(f32),
        jnp.concatenate([old[:, 1:], old[:, 0:1], empty], 1),
        table_cols_ref[...].reshape(1, -1),
        False,
        lax.broadcasted_iota(jnp.int32, (padded, 1), 0) < slots,
        slots,
    )
    table_new_ref[1:] = table[: slots - 1]
    table_new_ref[0:1] = table[slots - 1 : slots]
    table_rows_new_ref[...] = jnp.concatenate(
        [rows[:, slots - 1 : slots], rows[:, : slots - 1]], 1
    )[0]
    table_cols_new_ref[...] = cols[0]


def layout(data, groups):
    return 0, data, data + 4 * groups, -(-(data + 4 * groups + 6) // 8) * 8


def across(column):
    n = column.shape[0]
    wide = jnp.broadcast_to(column, (n, 128))
    if n < 128:
        wide = jnp.concatenate([wide, jnp.zeros((128 - n, 128), f32)])
    return wide.T[0:1]


def down(row, n):
    return jnp.broadcast_to(row, (128, 128)).T[:n, 0:1]


def sums_kernel(
    place_ref,
    attend_ref,
    expand_ref,
    contract_ref,
    squares_ref,
    vector_one_ref,
    vector_two_ref,
    expand_bias_ref,
    heads_far_ref,
    heads_near_ref,
    sums_ref,
    *,
    data,
    groups,
    share,
    patch_count,
):
    block, group = place_ref[4], place_ref[5]
    own = place_ref[2] * 2 + place_ref[3]
    _, at_group, at_single, _ = layout(data, groups)
    sums_ref[...] = jnp.zeros(sums_ref.shape, f32)
    lane = lax.broadcasted_iota(jnp.int32, (1, attend_ref.shape[1]), 1)
    for index, ref in enumerate((attend_ref, expand_ref, contract_ref)):
        grad = ref[...]
        squared = grad * grad + eps_one
        span = slice(at_group + index * groups, at_group + (index + 1) * groups)
        sums_ref[span, :] = put(groups, group, jnp.sum(squared, 0, keepdims=True))
        if index == 0:
            lines = (
                jnp.sum(jnp.where(lane < 3 * share, squared, 0.0), 1, keepdims=True),
                jnp.sum(jnp.where(lane < 3 * share, 0.0, squared), 1, keepdims=True),
            )
        else:
            lines = (jnp.sum(squared, 1, keepdims=True),)
        for part, line in enumerate(lines):
            spot = (index + (index > 0) + part) * 128
            sums_ref[:data, spot : spot + 128] = put(data, block, across(line))
    sums_ref[:data, 512:640] = put(data, block, squares_ref[...])
    at_group += 3 * groups
    lines = jnp.zeros((groups, expand_bias_ref.shape[2]), f32)
    for distance in range(groups):
        lines = lines + put(groups, own ^ distance, expand_bias_ref[distance])
    sums_ref[at_group : at_group + groups, :] = lines
    count = heads_far_ref.shape[1] // 2
    for part in range(2):
        span = slice(part * count, (part + 1) * count)
        lines = jnp.zeros((groups, share), f32)
        for ref, order in ((heads_far_ref, (3, 1)), (heads_near_ref, (2, 0))):
            for step, distance in enumerate(order):
                total = jnp.sum(ref[step][span], 0, keepdims=True)
                lines = lines + put(groups, own ^ distance, total)
        sums_ref[part * groups : (part + 1) * groups, 3 * share :] = lines
    stem_bias = jnp.sum(vector_one_ref[8 : 8 + patch_count, :], 0, keepdims=True)
    singles = (stem_bias, vector_one_ref[0:2, :], vector_two_ref[0:3, :])
    for line in singles:
        sums_ref[at_single : at_single + line.shape[0], :] = line
        at_single += line.shape[0]


def vector_kernel(
    place_ref,
    sums_ref,
    last_ref,
    head_ref,
    vectors_ref,
    second_ref,
    grad_out,
    new_out,
    second_out,
    grad_ref,
    lines_ref,
    *,
    data,
    groups,
    share,
):
    to_lines(second_ref, lines_ref)
    length = second_ref.shape[0]
    _, at_group, at_single, _ = layout(data, groups)
    width = vectors_ref.shape[1]

    def single(index):
        return sums_ref[at_single + index : at_single + index + 1, :]

    def joined(part):
        lines = sums_ref[part * groups : (part + 1) * groups, 3 * share :]
        return jnp.concatenate([lines[g : g + 1] for g in range(groups)], 1)

    grad_ref[...] = jnp.zeros(grad_ref.shape, f32)
    spot = at_group + 3 * groups
    rest = CLASSES - width
    for index, value in (
        (STEM_BIAS, single(0)),
        (GAIN_ONE, single(1)),
        (SHIFT_ONE, single(2)),
        (QUERY_BIAS, joined(0)),
        (VALUE_BIAS, joined(1)),
        (ATTEND_BIAS, single(3)),
        (GAIN_TWO, single(4)),
        (SHIFT_TWO, single(5)),
        (EXPAND_BIAS, sums_ref[spot : spot + groups, :]),
        (CONTRACT_BIAS, last_ref[0:3, :]),
        (HEAD_BIAS, head_ref[0:1, :width]),
    ):
        grad_ref[index : index + value.shape[0], :] = value
    grad_ref[HEAD_BIAS + 1 : HEAD_BIAS + 2, :rest] = head_ref[0:1, width:]
    grad = grad_ref[...]
    row = lax.broadcasted_iota(jnp.int32, grad.shape, 0)
    lane = lax.broadcasted_iota(jnp.int32, grad.shape, 1)
    valid = row * width + lane < length
    second = decay_rate * lines_ref[...] + (1.0 - decay_rate) * (grad * grad + eps_one)
    update = grad * lax.rsqrt(jnp.where(valid, second, 1.0))
    total = jnp.sum(update * update, keepdims=True) / length
    square = jnp.sum(vectors_ref[...] * vectors_ref[...], keepdims=True) / length
    scale = step_rate * jnp.maximum(eps_two, jnp.sqrt(square))
    scale = scale / jnp.maximum(1.0, jnp.sqrt(total) / clip_level)
    from_lines(grad, grad_out)
    from_lines(vectors_ref[...] - scale * update, new_out)
    from_lines(second, second_out)


def renew_kernel(
    place_ref,
    sums_ref,
    in_rows_ref,
    out_cols_ref,
    expand_rows_ref,
    contract_cols_ref,
    in_cols_ref,
    out_rows_ref,
    expand_cols_ref,
    contract_rows_ref,
    attend_ref,
    expand_ref,
    contract_ref,
    in_rows_out,
    out_cols_out,
    expand_rows_out,
    contract_cols_out,
    in_cols_out,
    out_rows_out,
    expand_cols_out,
    contract_rows_out,
    update_ref,
    scalar_ref,
    square_ref,
    rows_new_ref,
    cols_new_ref,
    *,
    data,
    groups,
    share,
):
    block, group = place_ref[4], place_ref[5]
    size = attend_ref.shape[0]
    width = attend_ref.shape[1]
    _, at_group, _, _ = layout(data, groups)
    length, hidden = data * size, groups * width
    lane = lax.broadcasted_iota(jnp.int32, (1, width), 1)
    first = lane < 3 * share
    spare = lax.broadcasted_iota(jnp.int32, (1, 128), 1) < size
    for index, ref in enumerate((in_rows_ref, out_cols_ref, expand_rows_ref, contract_cols_ref)):
        for part in range(data):
            values = ref[pl.ds(part * size, size)].reshape(1, size)
            rows_new_ref[part : part + 1, index * 128 : index * 128 + size] = values
    for part in range(groups):
        span = slice(part * share, (part + 1) * share)
        for which in range(3):
            cols_new_ref[part : part + 1, which * share : (which + 1) * share] = in_cols_ref[
                which : which + 1, span
            ]
        values = out_rows_ref[pl.ds(part * share, share)].reshape(1, share)
        cols_new_ref[part : part + 1, 3 * share :] = values
        for index, ref in enumerate((expand_cols_ref, contract_rows_ref), 1):
            values = ref[pl.ds(part * width, width)].reshape(1, width)
            cols_new_ref[index * groups + part : index * groups + part + 1, :] = values
    counts = (3 * length, length, hidden, hidden)
    means = []
    for index, count in enumerate(counts):
        span = slice(index * 128, (index + 1) * 128)
        new = decay_rate * rows_new_ref[:, span]
        new = new + (1.0 - decay_rate) * (sums_ref[:data, span] / count)
        rows_new_ref[:, span] = new
        means.append(jnp.sum(jnp.where(spare, new, 0.0), keepdims=True) / length)
        out = (in_rows_out, out_cols_out, expand_rows_out, contract_cols_out)[index]
        for part in range(data):
            out[pl.ds(part * size, size)] = new[part, :size]
    for index, count in enumerate((length, length, length)):
        span = slice(index * groups, (index + 1) * groups)
        lines = sums_ref[at_group + index * groups : at_group + (index + 1) * groups, :]
        new = decay_rate * cols_new_ref[span, :] + (1.0 - decay_rate) * (lines / count)
        cols_new_ref[span, :] = new
        for part in range(groups):
            if index == 0:
                for which in range(3):
                    in_cols_out[which : which + 1, part * share : (part + 1) * share] = new[
                        part : part + 1, which * share : (which + 1) * share
                    ]
                out_rows_out[pl.ds(part * share, share)] = new[part, 3 * share :]
            else:
                out = (expand_cols_out, contract_rows_out)[index - 1]
                out[pl.ds(part * width, width)] = new[part]
        if index == 0:
            means[1] = jnp.sum(jnp.where(first, 0.0, new), keepdims=True) / length
        if index == 2:
            means[3] = jnp.sum(new, keepdims=True) / hidden
    scalars = jnp.zeros((1, 128), f32)
    place_lane = lax.broadcasted_iota(jnp.int32, (1, 128), 1)
    for index, ref in enumerate((attend_ref, expand_ref, contract_ref)):
        across_row = pick(cols_new_ref[index * groups : (index + 1) * groups, :], group)

        def row(which):
            span = slice(which * 128, (which + 1) * 128)
            return down(pick(rows_new_ref[:, span], block), size)

        if index == 0:
            denominator = jnp.where(
                first, row(0) * across_row / means[0], row(1) * across_row / means[1]
            )
        else:
            denominator = row(index + 1) * across_row / means[index + 1]
        update = ref[...] * lax.rsqrt(denominator)
        update_ref[index] = update
        squared = update * update
        if index == 0:
            totals = (jnp.where(first, squared, 0.0), jnp.where(first, 0.0, squared))
        else:
            totals = (squared,)
        for part, total in enumerate(totals):
            spot = index + (index > 0) + part
            scalars = jnp.where(place_lane == spot, jnp.sum(total, keepdims=True), scalars)
    scalar_ref[...] = jnp.broadcast_to(scalars, scalar_ref.shape)
    squares = jnp.sum(sums_ref[:data, 512:640], 0, keepdims=True)
    square_ref[...] = jnp.broadcast_to(squares, square_ref.shape)


def step_kernel(
    place_ref,
    update_ref,
    scalar_ref,
    square_ref,
    attend_ref,
    expand_ref,
    contract_ref,
    in_ref,
    in_low_ref,
    out_ref,
    out_low_ref,
    expand_new_ref,
    expand_low_ref,
    contract_new_ref,
    contract_low_ref,
    *,
    sizes,
):
    share = in_ref.shape[2]
    scales = []
    for index, size in enumerate(sizes):
        total = scalar_ref[0:1, index : index + 1]
        square = square_ref[0:1, index : index + 1]
        clip = jnp.maximum(1.0, jnp.sqrt(total / size) / clip_level)
        scales.append(step_rate * jnp.maximum(eps_two, jnp.sqrt(square / size)) / clip)
    lane = lax.broadcasted_iota(jnp.int32, (1, attend_ref.shape[1]), 1)
    scale = jnp.where(lane < 3 * share, scales[0], scales[1])
    attend = attend_ref[...] - scale * update_ref[0]
    for part in range(3):
        lines = attend[:, part * share : (part + 1) * share]
        in_ref[part] = lines
        in_low_ref[part] = lines.astype(bf16)
    out = attend[:, 3 * share :].T
    out_ref[...] = out
    out_low_ref[...] = out.astype(bf16)
    expand = expand_ref[...] - scales[2] * update_ref[1]
    expand_new_ref[...] = expand
    expand_low_ref[...] = expand.astype(bf16)
    contract = contract_ref[...] - scales[3] * update_ref[2]
    contract_new_ref[...] = contract
    contract_low_ref[...] = contract.astype(bf16)


def call(
    body, order, place, operands, results, scratch=(), flops=0, weights=None, limit=48
):
    steps = len(order)
    pieces = weights is not None and len(weights) == 4

    def distance(step):
        at = order[0]
        for index, value in enumerate(order[1:], 1):
            at = jnp.where(step == index, value, at)
        return at

    def spec(shape, mark):
        zeros = (0,) * (len(shape) - 1)
        if mark == "any":
            return pl.BlockSpec(memory_space=pl.ANY)
        if mark == "smem":
            return pl.BlockSpec(memory_space=pltpu.SMEM)
        if mark is False:
            return pl.BlockSpec(shape, lambda g, p: (0,) + zeros)
        if mark is True:
            return pl.BlockSpec(
                (1,) + shape[1:], lambda g, p: ((p[2] * 2 + p[3]) ^ distance(g),) + zeros
            )
        if mark == "far":
            return pl.BlockSpec((1,) + shape[1:], lambda g, p: (distance(g),) + zeros)
        return pl.BlockSpec((1,) + shape[1:], lambda g, p: (mark(g),) + zeros)

    operands, scratch = tuple(operands), tuple(scratch)
    kernel = body
    if weights is not None:
        operands = tuple((weight, "any" if pieces else True) for weight in weights) + operands
    if pieces:
        some = weights[0]
        height, width = some.shape[0] * some.shape[1] * some.shape[2], some.shape[3]
        full = (steps, some.shape[1], some.shape[0]) + some.shape[2:]
        scratch += ((full, some.dtype), ((steps, 2), None))

        def kernel(place_ref, *refs):
            full_ref, sems = refs[-2:]
            step = pl.program_id(0)
            copies = [
                (r, group_copies(place_ref, refs[:4], full_ref.at[i], sems.at[i], r))
                for i, r in enumerate(order)
            ]

            @pl.when(step == 0)
            def _():
                for distance, choices in copies:
                    each_copy(place_ref, distance, choices, start_copy)

            for index in range(steps):

                @pl.when(step == index)
                def _(index=index):
                    each_copy(place_ref, *copies[index], wait_copy)

            def weight(start=0, stop=width):
                return full_ref[step, :, :, :, start:stop].reshape(height, stop - start)

            body(place_ref, weight, *refs[4:-2])

    elif weights is not None:

        def kernel(place_ref, weight_ref, *refs):
            def weight(start=0, stop=weight_ref.shape[2]):
                return weight_ref[0, :, start:stop]

            body(place_ref, weight, *refs)

    return pl.pallas_call(
        kernel,
        grid_spec=pltpu.PrefetchScalarGridSpec(
            num_scalar_prefetch=1,
            grid=(steps,),
            in_specs=[spec(value.shape, mark) for value, mark in operands],
            out_specs=[spec(shape, mark) for shape, _, mark in results],
            scratch_shapes=[
                pltpu.SemaphoreType.DMA(shape) if kind is None else pltpu.VMEM(shape, kind)
                for shape, kind in scratch
            ],
        ),
        out_shape=[jax.ShapeDtypeStruct(shape, kind) for shape, kind, _ in results],
        compiler_params=pltpu.CompilerParams(vmem_limit_bytes=limit * 1024 * 1024),
        cost_estimate=pl.CostEstimate(flops=flops, bytes_accessed=16_000_000, transcendentals=0),
    )(place, *[value for value, _ in operands])


def local(
    patches,
    keep_mask,
    labels,
    stem_weight,
    position_table,
    attend_in,
    attend_out,
    expand,
    contract,
    head_weight,
    vectors,
    stem_rows,
    stem_cols,
    table_rows,
    table_cols,
    attend_in_rows,
    attend_in_cols,
    attend_out_rows,
    attend_out_cols,
    expand_rows,
    expand_cols,
    contract_rows,
    contract_cols,
    head_rows,
    head_cols,
    vector_second,
):
    data_size, model_size = lax.axis_size("dp"), lax.axis_size("mp")
    links = Grid() if (data_size, model_size) == (8, 4) else Plain(data_size, model_size)
    here = links.place
    count, patch_count, _ = patches.shape
    groups = model_size
    pair = groups // 2
    image_count = count * data_size * model_size
    inverse_count = 1.0 / image_count
    row_share, _, head_share = attend_in.shape
    hidden_share = expand.shape[1]
    in_share = 3 * head_share
    slots = patch_count + 1
    padded = -(-slots // 16) * 16
    rows = count * padded
    contract_own = contract.T
    attend_own, attend_piece, expand_piece, contract_piece, squares, vector_lines = call(
        pieces_kernel,
        (0,),
        here,
        (
            (attend_in.swapaxes(0, 1), False),
            (attend_out, False),
            (expand, False),
            (contract_own, False),
            (vectors, False),
        ),
        (((row_share, D), f32, False),)
        + (((row_share, D), bf16, False),) * 3
        + (((1, 128), f32, False), ((24, D), f32, False)),
        limit=60,
    )
    attend_chain = Chain(links.gather(attend_piece))
    pixels = jnp.pad(patches, ((0, 0), (0, padded - patch_count), (0, 0))).reshape(rows, -1)
    pixels, vector_lines, expand_piece, contract_piece, head_weight = sync(
        [attend_chain], pixels, vector_lines, expand_piece, contract_piece, head_weight
    )
    expand_chain = Chain(links.gather(expand_piece))
    stream_zero, rows_one, present, facts = call(
        stem_kernel,
        (0,),
        here,
        (
            (labels, "smem"),
            (after(pixels, attend_chain.sent), False),
            (stem_weight, False),
            (position_table, False),
            (vector_lines, False),
            (keep_mask, False),
        ),
        (
            ((rows, D), f32, False),
            ((rows, D), bf16, False),
            ((count, padded), f32, False),
            ((2 * count, 128), f32, False),
        ),
        flops=2 * rows * D * D,
    )
    stream_zero, rows_one, contract_piece, head_weight = sync(
        [attend_chain, expand_chain],
        stream_zero,
        rows_one,
        contract_piece,
        head_weight,
    )
    contract_chain = Chain(links.gather(contract_piece))
    head_turned = head_weight.T
    head_low = head_turned.astype(bf16)

    head_low = sync([attend_chain, expand_chain, contract_chain], head_low)
    sync([attend_chain], contract_chain.sent, expand_chain.sent)
    attend_all = attend_chain.result
    every = tuple(range(groups))

    qkv, attended, stream_one, rows_two, stream_sum = call(
        functools.partial(attend_kernel, order=every),
        every,
        here,
        (
            (rows_one, False),
            (vector_lines, False),
            (present, False),
            (stream_zero, "any"),
        ),
        (
            ((groups, 3, rows, head_share), bf16, "far"),
            ((groups, rows, head_share), bf16, "far"),
            ((rows, D), f32, False),
            ((rows, D), bf16, False),
            ((2 * count, D), f32, False),
        ),
        scratch=(((rows, D), f32), ((1,), None)),
        flops=2 * rows * D * 4 * D,
        weights=attend_all,
    )
    rows_two, stream_sum = sync([expand_chain, contract_chain], rows_two, stream_sum)
    rows_two = sync([expand_chain], rows_two)
    expand_all = expand_chain.result
    active_sum, slope = call(
        functools.partial(hidden_kernel, order=every),
        every,
        here,
        (
            (rows_two, False),
            (vector_lines, False),
            (present, False),
        ),
        (
            ((groups, 2 * count, hidden_share), f32, "far"),
            ((groups, rows, hidden_share), bf16, "far"),
        ),
        (((rows, 1), f32),),
        flops=2 * rows * D * FF,
        weights=expand_all,
    )
    active_sum, slope = sync([contract_chain], active_sum, slope)
    active_sum, slope = sync([contract_chain], active_sum, slope)

    contract_all = contract_chain.result
    scratch = ()
    if len(contract_all) == 4:
        scratch = (
            ((groups, data_size // 2, 2, row_share, hidden_share), bf16),
            ((groups, 2), None),
        )
    piece, d_row, d_active_row = call(
        functools.partial(own_head_kernel, inverse_count=inverse_count),
        (0,),
        here,
        tuple((value, False) for value in (active_sum, stream_sum, facts, vector_lines, head_low))
        + tuple((value, "any" if scratch else False) for value in contract_all),
        (
            ((8 * count, D + 128), bf16, False),
            ((2 * count, D), f32, False),
            ((groups, 2 * count, hidden_share), f32, False),
        ),
        scratch,
    )

    pieces_chain = Chain(links.gather(piece))
    far_grad, near_grad, expand_bias_grad, d_rows_two = call(
        expand_back_kernel,
        (3, 1, 2, 0),
        here,
        (
            (rows_two, False),
            (slope, "far"),
            (d_active_row, "far"),
        ),
        (
            ((pair, D, hidden_share), bf16, lambda g: jnp.minimum(g, pair - 1)),
            ((pair, D, hidden_share), bf16, lambda g: jnp.maximum(g - pair, 0)),
            ((groups, 1, hidden_share), f32, "far"),
            ((rows, D), f32, False),
        ),
        (((rows, hidden_share), bf16),),
        flops=4 * rows * D * FF,
        weights=expand_all,
    )
    far_grad, near_grad, d_rows_two = sync([pieces_chain], far_grad, near_grad, d_rows_two)
    expand_sum = Chain(links.reduce(far_grad))
    d_stream, d_attend_low, vector_two = call(
        between_kernel,
        (0,),
        here,
        (
            (d_rows_two, False),
            (d_row, False),
            (present, False),
            (stream_one, False),
            (vector_lines, False),
        ),
        (
            ((rows, D), f32, False),
            ((rows, D), bf16, False),
            ((8, D), f32, False),
        ),
    )

    d_stream, d_attend_low = sync(
        [pieces_chain, (expand_sum, near_grad)], d_stream, d_attend_low
    )

    def attend_back(order, *before):
        return call(
            attend_back_kernel,
            order,
            here,
            (
                (rows_one, False),
                (qkv, "far"),
                (attended, "far"),
                (present, False),
                (d_attend_low, False),
            )
            + tuple((value, "any") for value in before),
            (
                ((pair, D, D), bf16, lambda g: g),
                ((pair, 2 * count, head_share), f32, lambda g: g),
                ((rows, D), f32, False),
            ),
            (((rows, 3 * head_share), bf16), ((rows, 1), f32))
            + ((((rows, D), f32), ((1,), None)) if before else ()),
            flops=2 * rows * D * 4 * D,
            weights=attend_all,
        )

    far_grad, heads_far, d_rows_one = attend_back((3, 1))
    far_grad, d_rows_one = sync([pieces_chain, expand_sum], far_grad, d_rows_one)
    attend_sum = Chain(links.reduce(far_grad))
    near_grad, heads_near, d_rows_one = attend_back((2, 0), d_rows_one)
    d_rows_one = sync([pieces_chain, expand_sum, (attend_sum, near_grad)], d_rows_one)
    both_far, both_near, vector_one = call(
        stem_back_kernel,
        (0,),
        here,
        (
            (after(d_rows_one, attend_sum.sent, expand_sum.sent), False),
            (d_stream, False),
            (stream_zero, False),
            (vector_lines, False),
            (pixels, False),
        ),
        (
            ((4, 128, D), bf16, False),
            ((4, 128, D), bf16, False),
            ((8 + padded, D), f32, False),
        ),
        flops=2 * rows * D * D,
    )
    pieces, both_far, both_near = sync(
        [attend_sum, expand_sum], pieces_chain.result, both_far, both_near
    )
    grad_expand = expand_sum.result
    both_sum = Chain(links.add_large(both_far, both_near))
    pieces, grad_expand, _ = sync([both_sum], pieces, grad_expand, attend_sum.sent)
    pieces = links.whole(*pieces).reshape((-1,) + piece.shape)
    pieces, grad_expand = sync([attend_sum], pieces, grad_expand)
    pieces, grad_expand, _ = sync([both_sum], pieces, grad_expand, attend_sum.sent)
    steps = max(1, pieces.shape[0] // 32)
    grad_head, grad_contract, vector_last, vector_head = call(
        functools.partial(all_head_kernel, inverse_count=inverse_count),
        (0,) * steps,
        here,
        (
            (pieces.reshape((steps, -1) + piece.shape), lambda g: g),
            (vector_lines, False),
            (head_low, False),
        ),
        (
            ((CLASSES, D), f32, False),
            ((row_share, hidden_share), f32, False),
            ((8, D), f32, False),
            ((8, CLASSES), f32, False),
        ),
    )
    loss_sum = vector_head[1, 0]
    grad_expand, grad_contract = sync([attend_sum], grad_expand, grad_contract)
    grad_attend = attend_sum.result

    names = dict(data=data_size, groups=groups, share=head_share)
    lines = layout(data_size, groups)[3]
    (sums,) = call(
        functools.partial(sums_kernel, patch_count=patch_count, **names),
        (0,),
        here,
        tuple(
            (value, False)
            for value in (
                grad_attend,
                grad_expand,
                grad_contract,
                squares,
                vector_one,
                vector_two,
                expand_bias_grad,
                heads_far,
                heads_near,
            )
        ),
        (((lines, D), f32, False),),
    )
    sums_chain = Chain(links.add(sums))
    sync([sums_chain, both_sum])
    sync([sums_chain, both_sum])
    head_new, head_rows_new, head_cols_new = call(
        head_step_kernel,
        (0,),
        here,
        tuple((value, False) for value in (head_turned, grad_head, head_rows, head_cols)),
        (((CLASSES, D), f32, False), ((D,), f32, False), ((CLASSES,), f32, False)),
    )
    sync([sums_chain])
    head_new = sync([sums_chain, both_sum], head_new)
    sync([sums_chain, both_sum])
    sums = sums_chain.result
    statistics = (
        attend_in_rows,
        attend_out_cols,
        expand_rows,
        contract_cols,
        attend_in_cols,
        attend_out_rows,
        expand_cols,
        contract_rows,
    )
    *statistics, update, scalars, square_totals = call(
        functools.partial(renew_kernel, **names),
        (0,),
        here,
        tuple(
            (value, False)
            for value in (sums,) + statistics + (grad_attend, grad_expand, grad_contract)
        ),
        tuple((value.shape, f32, False) for value in statistics)
        + (
            ((3, row_share, D), f32, False),
            ((8, 128), f32, False),
            ((8, 128), f32, False),
        ),
        (((data_size, 512), f32), ((3 * groups, D), f32)),
    )
    (
        in_rows_new,
        out_cols_new,
        expand_rows_new,
        contract_cols_new,
        in_cols_new,
        out_rows_new,
        expand_cols_new,
        contract_rows_new,
    ) = statistics
    scalars_chain = Chain(links.add(scalars))
    sums = sync([scalars_chain], sums)
    sums = sync([scalars_chain, both_sum], sums)
    sums = sync([scalars_chain, both_sum], sums)
    stem_new, stem_rows_new, stem_cols_new, table_new, table_rows_new, table_cols_new = call(
        functools.partial(stem_step_kernel, padded=padded),
        (0,),
        here,
        tuple(
            (value, False)
            for value in both_sum.result
            + (stem_weight, stem_rows, stem_cols, position_table, table_rows, table_cols)
        ),
        tuple(
            (value.shape, f32, False)
            for value in (stem_weight, stem_rows, stem_cols, position_table, table_rows, table_cols)
        ),
        (((1024, D), bf16),),
    )
    stem_new, sums = sync([scalars_chain], stem_new, sums)
    grad_vector, vectors_new, second_new = call(
        functools.partial(vector_kernel, **names),
        (0,),
        here,
        tuple(
            (value, False) for value in (sums, vector_last, vector_head, vector_lines, vector_second)
        ),
        ((vectors.shape, f32, False),) * 3,
        (((24, D), f32), ((24, D), f32)),
    )
    vectors_new = sync([scalars_chain], vectors_new)
    block = call(
        functools.partial(step_kernel, sizes=(3 * D * D, D * D, D * FF, FF * D)),
        (0,),
        here,
        tuple(
            (value, False)
            for value in (
                update,
                scalars_chain.result,
                square_totals,
                attend_own,
                expand,
                contract_own,
            )
        ),
        tuple(
            (shape, kind, False)
            for shape in (
                (3, row_share, head_share),
                (head_share, row_share),
                (row_share, hidden_share),
                (row_share, hidden_share),
            )
            for kind in (f32, bf16)
        ),
    )
    in_new, in_copy, out_new, out_copy, expand_new, expand_copy, contract_new, contract_copy = block

    return (
        loss_sum,
        stem_new,
        stem_rows_new,
        stem_cols_new,
        table_new,
        table_rows_new,
        table_cols_new,
        in_new.swapaxes(0, 1),
        in_copy.swapaxes(0, 1),
        in_rows_new,
        in_cols_new,
        out_new,
        out_copy,
        out_rows_new,
        out_cols_new,
        expand_new,
        expand_copy,
        expand_rows_new,
        expand_cols_new,
        contract_new.T,
        contract_copy.T,
        contract_rows_new,
        contract_cols_new,
        head_new.T,
        head_rows_new,
        head_cols_new,
        vectors_new,
        grad_vector,
        second_new,
    )


def solution(mesh):
    placed = (
        P(ALL, None, None),
        P(ALL, None),
        P(ALL),
        P(),
        P(),
        P("dp", None, "mp"),
        P("mp", "dp"),
        P("dp", "mp"),
        P("mp", "dp"),
    ) + (P(),) * 17
    block = (P("dp", None, "mp"), P("mp", "dp"), P("dp", "mp"), P("mp", "dp"))
    given = [P()] * 7
    for spec in block:
        given += [spec, spec, P(), P()]
    given += [P()] * 6
    return jax.shard_map(
        local, mesh=mesh, in_specs=placed, out_specs=tuple(given), check_vma=False
    )
```
